32 devices in a mesh: dp: 8 (over y, x, core), tensor: 4 (over z).
Axes of the slice: x: 2, y: 2, z: 4, core: 2. Of those that a mesh axis runs over, the one named last changes fastest.
Arguments:
- tokens_in: bfloat16 [16, 1024, 768], P('dp', 'tensor'), may hold values from -6 to 6
- token_mask: int32 [16, 1024], P('dp', 'tensor'), may hold values from 0 to 1, as said below
- grid_index: int32 [16], P('dp'), may hold values from 0 to 15, each once
- time_table: float32 [16, 128], replicated, may hold values from -5 to 5
- cotangent: bfloat16 [16, 1024, 768], P('dp', 'tensor'), may hold values from -6 to 6
- w_ada: bfloat16 [128, 6, 768], replicated, may hold values from -0.5 to 0.5
- b_ada: float32 [6, 768], replicated, may hold values from -3 to 3
- norm1: float32 [768], replicated, may hold values from 0.25 to 1.75
- norm2: float32 [768], replicated, may hold values from 0.25 to 1.75
- mask_vector: float32 [768], replicated, may hold values from -5 to 5
- w_qkv: bfloat16 [768, 3, 768], P(None, None, 'tensor'), may hold values from -0.21875 to 0.21875
- w_out: bfloat16 [768, 768], P('tensor'), may hold values from -0.875 to 0.875
- w_up: bfloat16 [768, 3072], P(None, 'tensor'), may hold values from -0.21875 to 0.21875
- b_up: float32 [3072], P('tensor'), may hold values from -3 to 3
- w_down: bfloat16 [3072, 768], P('tensor'), may hold values from -0.109375 to 0.109375
- b_down: float32 [768], replicated, may hold values from -3 to 3
Outputs:
- layer_out: bfloat16 [16, 1024, 768], P('dp', 'tensor')
- grad_in: bfloat16 [16, 1024, 768], P('dp', 'tensor')
- grad_time_table: float32 [16, 128], replicated
- grad_mask_vector: float32 [768], replicated
- grad_w_ada: float32 [128, 6, 768], replicated
- grad_b_ada: float32 [6, 768], replicated
- grad_norm1: float32 [768], replicated
- grad_norm2: float32 [768], replicated
- grad_w_qkv: float32 [768, 3, 768], P(None, None, 'tensor')
- grad_w_out: float32 [768, 768], P('tensor')
- grad_w_up: float32 [768, 3072], P(None, 'tensor')
- grad_b_up: float32 [3072], P('tensor')
- grad_w_down: float32 [3072, 768], P('tensor')
- grad_b_down: float32 [768], replicated
The draws below stay inside these ranges and needn't reach their ends.
Inputs may be any that keep to these rules, and one draw needn't show every extreme that they name: `token_mask`: each sequence masks its tokens at a rate of its own, from none of them to all. `grid_index`: each sequence has a grid point of its own.
All inputs are finite; a program needn't handle non-finite values.
Results may differ from the reference program's by a relative error of at most 0.019.
Values may be sent and summed in bfloat16 or wider, within the bound.
No kernel may reach another device: no remote copies, remote signals or barrier semaphores. Data moves between devices by JAX's collectives and lax.ppermute only.
A program may use at most 128 MiB of HBM per device.

```python
import jax
import jax.numpy as jnp
from jax import lax

D = 768
HEADS = 12
HEAD_DIM = 64
FF = 3072
COND = 128
SEQ_LEN = 1024
SEQS = 16
N_TENSOR = 4


def draw_token_mask(key, part):
    key = jax.random.fold_in(key, 7)
    level_key, noise_key = jax.random.split(key)
    levels = jax.random.randint(level_key, (SEQS, 1), 0, 17)
    noise = jax.random.randint(noise_key, (SEQS, SEQ_LEN), 0, 16)
    return (noise < levels).astype(jnp.int32)


def steps_of(rng, extent, cuts, low, high):
    level = 1.0
    for position, shards_of in cuts:
        steps = jax.random.uniform(jax.random.fold_in(jax.random.fold_in(rng, 6), position), (shards_of,), jnp.float32, low / len(cuts), high / len(cuts))
        level = level * jnp.repeat(jnp.exp(steps), extent[position] // shards_of).reshape((-1,) + (1,) * (len(extent) - 1 - position))
    return level


def scatter_about(key, dims, deviation, bound, shards=(), dtype=jnp.bfloat16):
    values = deviation * jax.random.normal(key, dims, jnp.float32)
    if shards:
        values = values * steps_of(key, dims, shards, -0.22, 0.18)
    return jnp.clip(values, -bound, bound).astype(dtype)


def setup_inputs(seed: int = 0) -> dict:
    streams_of = jax.random.split(jax.random.key(seed), 17)
    tokens_in = scatter_about(streams_of[0], (SEQS, SEQ_LEN, D), 1.0, 6.0, ((0, 8), (1, 4)))
    token_mask = draw_token_mask(jax.random.fold_in(streams_of[16], 71), 0)
    grid_index = jax.random.permutation(streams_of[2], SEQS).astype(jnp.int32)
    time_table = scatter_about(streams_of[3], (SEQS, COND), 1.0, 5.0, (), jnp.float32)
    cotangent = scatter_about(streams_of[4], (SEQS, SEQ_LEN, D), 1.0, 6.0, ((0, 8), (1, 4)))
    w_ada = scatter_about(streams_of[5], (COND, 6, D), COND ** -0.5, 0.5)
    b_ada = scatter_about(streams_of[6], (6, D), 0.5, 3.0, (), jnp.float32)
    norm1 = jnp.clip(1.0 + 0.15 * jax.random.normal(streams_of[7], (D,), jnp.float32), 0.25, 1.75)
    norm2 = jnp.clip(1.0 + 0.15 * jax.random.normal(streams_of[8], (D,), jnp.float32), 0.25, 1.75)
    mask_vector = scatter_about(streams_of[9], (D,), 1.0, 5.0, (), jnp.float32)
    w_qkv = scatter_about(streams_of[10], (D, 3, D), D ** -0.5, 0.21875, ((2, 4),))
    w_out = scatter_about(streams_of[11], (D, D), (D // 16) ** -0.5, 0.875, ((0, 4),))
    w_up = scatter_about(streams_of[12], (D, FF), D ** -0.5, 0.21875, ((1, 4),))
    b_up = scatter_about(streams_of[13], (FF,), 0.5, 3.0, ((0, 4),), jnp.float32)
    w_down = scatter_about(streams_of[14], (FF, D), FF ** -0.5, 0.109375, ((0, 4),))
    b_down = scatter_about(streams_of[15], (D,), 0.5, 3.0, (), jnp.float32)
    return dict(tokens_in=tokens_in, token_mask=token_mask, grid_index=grid_index, time_table=time_table, cotangent=cotangent, w_ada=w_ada, b_ada=b_ada, norm1=norm1, norm2=norm2, mask_vector=mask_vector, w_qkv=w_qkv, w_out=w_out, w_up=w_up, b_up=b_up, w_down=w_down, b_down=b_down)


highest = lax.Precision.HIGHEST

@jax.custom_vjp
def low(v):
    return lax.optimization_barrier(v.astype(jnp.bfloat16)).astype(jnp.float32)

@jax.custom_vjp
def low_back(v):
    return v

def low_keep(v):
    return (low(v), None)

def low_pass(kept, grad):
    return (grad,)

def back_keep(v):
    return (v, None)

def back_low(kept, grad):
    return (low(grad),)
low.defvjp(low_keep, low_pass)
low_back.defvjp(back_keep, back_low)

def normalize(values, gain):
    average = lax.optimization_barrier(jnp.mean(values, axis=-1, keepdims=True))
    centered = values - average
    variance = lax.optimization_barrier(jnp.mean(centered * centered, axis=-1, keepdims=True))
    return centered * lax.rsqrt(variance + 1e-05) * gain

def rotary_angles(length, head_dim):
    half_dim = head_dim // 2
    positions = jnp.arange(length).astype(jnp.float32)
    frequency = 10000.0 ** (-jnp.arange(half_dim).astype(jnp.float32) / half_dim)
    angles = positions[:, None] * frequency[None, :]
    return (jnp.cos(angles), jnp.sin(angles))

def rotate(values, cosine, sine):
    half_dim = values.shape[-1] // 2
    former = values[..., :half_dim]
    latter = values[..., half_dim:]
    cos_head = cosine[:, None, :]
    sin_head = sine[:, None, :]
    return jnp.concatenate([former * cos_head - latter * sin_head, latter * cos_head + former * sin_head], axis=-1)

def sequence_forward(weights, tokens, mask_row, onehot, cosine, sine):
    time_table, w_ada, b_ada, norm1, norm2, mask_vector, w_qkv, w_out, w_up, b_up, w_down, b_down = weights
    shard_width = D // N_TENSOR
    hidden_shard = FF // N_TENSOR
    cond_pre = jnp.dot(onehot, time_table, precision=highest)
    cond_low = low(jax.nn.silu(cond_pre))
    modulation = jnp.dot(cond_low, w_ada.reshape(COND, 6 * D), precision=highest).reshape(6, D) + b_ada
    residual = tokens + mask_row[:, None] * mask_vector
    first_in = low(normalize(residual, norm1) * (1.0 + modulation[1]) + modulation[0])
    qkv_all = low_back(jnp.dot(first_in, w_qkv.reshape(D, 3 * D), precision=highest))
    qkv_all = qkv_all.reshape(SEQ_LEN, 3, HEADS, HEAD_DIM)
    queries = low(rotate(qkv_all[:, 0], cosine, sine))
    key_rows = low(rotate(qkv_all[:, 1], cosine, sine))
    values = low(qkv_all[:, 2])
    scores = low_back(jnp.einsum('qhd,khd->hqk', queries, key_rows, precision=highest) * HEAD_DIM ** (-0.5))
    probs = jax.nn.softmax(scores, axis=-1)
    mixed = low(low_back(jnp.einsum('hqk,khd->qhd', low(probs), values, precision=highest)))
    mixed_groups = mixed.reshape(SEQ_LEN, N_TENSOR, shard_width)
    partial_attn = jnp.einsum('ltc,tcd->tld', mixed_groups, w_out.reshape(N_TENSOR, shard_width, D), precision=highest)
    attn_out = low_back(lax.optimization_barrier(jnp.sum(low(partial_attn), axis=0)))
    second_res = residual + modulation[2] * attn_out
    second_in = low(normalize(second_res, norm2) * (1.0 + modulation[4]) + modulation[3])
    upper_in = low_back(jnp.dot(second_in, w_up, precision=highest) + b_up)
    active = low(jax.nn.gelu(upper_in, approximate=True))
    active_groups = active.reshape(SEQ_LEN, N_TENSOR, hidden_shard)
    partial_mlp = jnp.einsum('ltc,tcd->tld', active_groups, w_down.reshape(N_TENSOR, hidden_shard, D), precision=highest)
    mlp_out = low_back(lax.optimization_barrier(jnp.sum(low(partial_mlp), axis=0)) + b_down)
    return second_res + modulation[5] * mlp_out

def reference(tokens_in, token_mask, grid_index, time_table, cotangent, w_ada, b_ada, norm1, norm2, mask_vector, w_qkv, w_out, w_up, b_up, w_down, b_down):
    initials = (time_table, w_ada, b_ada, norm1, norm2, mask_vector, w_qkv, w_out, w_up, b_up, w_down, b_down)
    weights = tuple((weight.astype(jnp.float32) for weight in initials))
    grid_points = jnp.arange(SEQS).astype(jnp.int32)
    onehots = (grid_index.astype(jnp.int32)[:, None] == grid_points[None, :]).astype(jnp.float32)
    cosine, sine = rotary_angles(SEQ_LEN, HEAD_DIM)

    def sequence_step(totals, inputs):
        tokens, mask_row, onehot, upstream = inputs

        def forward(params, activations):
            return sequence_forward(params, activations, mask_row, onehot, cosine, sine)
        output, pullback = jax.vjp(forward, weights, tokens)
        grad_weights, grad_tokens = pullback(upstream)
        totals = jax.tree.map(lambda left, right: left + right, totals, grad_weights)
        return (totals, (output.astype(jnp.bfloat16), grad_tokens.astype(jnp.bfloat16)))
    zeros = jax.tree.map(jnp.zeros_like, weights)
    inputs = (tokens_in.astype(jnp.float32), token_mask.astype(jnp.float32), onehots, cotangent.astype(jnp.float32))
    totals, (outputs, grads_in) = lax.scan(sequence_step, zeros, inputs)
    return (outputs, grads_in, totals[0], totals[5], totals[1], totals[2], totals[3], totals[4], totals[6], totals[7], totals[8], totals[9], totals[10], totals[11])
```

```python
import jax
import jax.numpy as jnp
from jax import lax
from jax.experimental import pallas as pl
from jax.experimental.pallas import tpu as pltpu
from jax.sharding import PartitionSpec as P

HEAD_DIM = 64
LANES = 128
f32 = jnp.float32
bf16 = jnp.bfloat16
highest = lax.Precision.HIGHEST
NN = (((1,), (0,)), ((), ()))
NT = (((1,), (1,)), ((), ()))
TN = (((0,), (0,)), ((), ()))
CORE, X, Y = 0, 1, 2
VMEM_BYTES = 48 * 2**20

SHIFT1, SCALE1, GATE1, SHIFT2, SCALE2, GATE2, NORM1, NORM2, MASKED, B_DOWN = range(10)


def dot(left, right, dims=NN):
    return lax.dot_general(left, right, dims, preferred_element_type=f32)


def row(table, index):
    return table[index : index + 1, :]


def full(shape):
    return pl.BlockSpec(shape, lambda i: (0,) * len(shape))


def rows_of(size, width, turn=0, steps=1):
    return pl.BlockSpec((size, width), lambda i: ((i + turn) % steps if turn else i, 0))


def call(body, grid, ins, specs, outs, out_specs, scratch=(), flops=0, moved=0, special=0):
    return pl.pallas_call(
        body,
        grid=(grid,),
        in_specs=specs,
        out_specs=out_specs,
        out_shape=outs,
        scratch_shapes=list(scratch),
        compiler_params=pltpu.CompilerParams(vmem_limit_bytes=VMEM_BYTES),
        cost_estimate=pl.CostEstimate(flops=flops, bytes_accessed=moved, transcendentals=special),
    )(*ins)


def centered(values):
    average = jnp.mean(values, axis=-1, keepdims=True)
    away = values - average
    inverse = lax.rsqrt(jnp.mean(away * away, axis=-1, keepdims=True) + 1e-05)
    return away * inverse, inverse


def norm_back(grads, hat, inverse, factor):
    slope = grads * factor
    lean = jnp.mean(slope, axis=-1, keepdims=True)
    tilt = jnp.mean(slope * hat, axis=-1, keepdims=True)
    return (slope - lean - hat * tilt) * inverse


def over_rows(values):
    return jnp.sum(values, axis=0, keepdims=True)


def enter_kernel(tokens, mask, table, residual, first):
    values = tokens[...].astype(f32) + mask[...] * row(table, MASKED)
    residual[...] = values
    hat, _ = centered(values)
    factor = row(table, NORM1) * (1.0 + row(table, SCALE1))
    first[...] = (hat * factor + row(table, SHIFT1)).astype(bf16)


def partner(values):
    lane = lax.broadcasted_iota(jnp.int32, values.shape, 1)
    ahead = pltpu.roll(values, LANES - HEAD_DIM // 2, 1)
    behind = pltpu.roll(values, HEAD_DIM // 2, 1)
    return jnp.where(lane % HEAD_DIM < HEAD_DIM // 2, ahead, behind)


def heads_of(values):
    lane = lax.broadcasted_iota(jnp.int32, values.shape, 1)
    return lane < HEAD_DIM


def attend_kernel(first, weights, w_out, cosine, sine, queries, keys, values, mixed, log_sum, part, total):
    step = pl.program_id(0)
    length = first.shape[0]
    chunk = 256
    tokens = first[...]
    query = dot(tokens, weights[0], NT)
    queries[...] = ((query * cosine[...] + partner(query) * sine[...]).astype(bf16) * HEAD_DIM**-0.5).astype(bf16)
    key = dot(tokens, weights[1], NT)
    keys[...] = (key * cosine[...] + partner(key) * sine[...]).astype(bf16)
    values[...] = dot(tokens, weights[2], NT).astype(bf16)

    @pl.when(step == 0)
    def _():
        total[...] = jnp.zeros_like(total)

    for start in range(0, length, chunk):
        here = pl.ds(start, chunk)
        block = queries[here, :]
        former = heads_of(block)
        halves = []
        for head in range(2):
            mine = former if head == 0 else ~former
            scores = dot(jnp.where(mine, block, 0), keys[...], NT)
            top = jnp.max(scores, axis=1, keepdims=True)
            powers = jnp.exp(scores - top)
            sums = jnp.sum(powers, axis=1, keepdims=True)
            out = dot(powers.astype(bf16), values[...]) / sums
            halves.append((out, top + jnp.log(sums)))
        out = jnp.where(former, halves[0][0], halves[1][0])
        mixed[here, :] = out
        log_sum[here, :] = jnp.where(former, halves[0][1], halves[1][1])
        total[here, :] += dot(out.astype(bf16), w_out[...])

    @pl.when(step == pl.num_programs(0) - 1)
    def _():
        part[...] = total[...].astype(bf16)


def attend(first, weights, w_out, cosine, sine):
    length, width = first.shape
    wide = w_out.shape[0]
    tall = pl.BlockSpec((length, LANES), lambda i: (0, i))
    narrow = jax.ShapeDtypeStruct((length, wide), bf16)
    wider = jax.ShapeDtypeStruct((length, wide), f32)
    return call(
        attend_kernel,
        wide // LANES,
        (first, weights, w_out, cosine, sine),
        [
            full(first.shape),
            pl.BlockSpec((3, LANES, width), lambda i: (0, i, 0)),
            pl.BlockSpec((LANES, width), lambda i: (i, 0)),
            full(cosine.shape),
            full(sine.shape),
        ],
        [narrow, narrow, narrow, wider, wider, jax.ShapeDtypeStruct((length, width), bf16)],
        [tall] * 5 + [full((length, width))],
        [pltpu.VMEM((length, width), f32)],
        flops=8 * length * width * wide + 16 * length * length * wide,
        moved=12 * length * width,
        special=length * length * wide // HEAD_DIM,
    )


def attend_back_kernel(
    grads, first, weights, w_out, cosine, sine, queries, keys, values, mixed, log_sum, d_weights, d_out, part, total, scores_t
):
    step = pl.program_id(0)
    length = first.shape[0]
    chunk = 256
    grad = dot(grads[...], w_out[...], NT).astype(bf16)
    outs = mixed[...]
    d_out[...] = dot(outs.astype(bf16), grads[...], TN).astype(bf16)
    lean_t = (grad.astype(f32) * outs).T
    log_t = log_sum[...].T
    query, key, value = queries[...], keys[...], values[...]
    former = heads_of(query)
    former_chunk = heads_of(query[:chunk])
    found_q, found_k, found_v = [], [], []
    for head in range(2):
        lean = over_rows(lean_t[head * HEAD_DIM : (head + 1) * HEAD_DIM])
        log_row = log_t[head * HEAD_DIM : head * HEAD_DIM + 1]
        mine = former_chunk if head == 0 else ~former_chunk
        part_k, part_v = [], []
        for start in range(0, length, chunk):
            key_rows = jnp.where(mine, key[start : start + chunk], 0)
            value_rows = jnp.where(mine, value[start : start + chunk], 0)
            probs = jnp.exp(dot(key_rows, query, NT) - log_row)
            part_v.append(dot(probs.astype(bf16), grad))
            slopes = (probs * (dot(value_rows, grad, NT) - lean)).astype(bf16)
            scores_t[start : start + chunk, :] = slopes
            part_k.append(dot(slopes, query))
        found_q.append(dot(scores_t[...], key, TN))
        found_k.append(jnp.concatenate(part_k, axis=0))
        found_v.append(jnp.concatenate(part_v, axis=0))
    d_query = jnp.where(former, found_q[0], found_q[1]) * HEAD_DIM**-0.5
    d_key = jnp.where(former, found_k[0], found_k[1])
    d_value = jnp.where(former, found_v[0], found_v[1]).astype(bf16)
    d_query = (d_query * cosine[...] + partner(d_query * sine[...])).astype(bf16)
    d_key = (d_key * cosine[...] + partner(d_key * sine[...])).astype(bf16)
    tokens = first[...]
    d_weights[0] = dot(d_query, tokens, TN).astype(bf16)
    d_weights[1] = dot(d_key, tokens, TN).astype(bf16)
    d_weights[2] = dot(d_value, tokens, TN).astype(bf16)
    more = dot(d_query, weights[0]) + dot(d_key, weights[1]) + dot(d_value, weights[2])

    @pl.when(step == 0)
    def _():
        total[...] = more

    @pl.when(step > 0)
    def _():
        total[...] += more

    @pl.when(step == pl.num_programs(0) - 1)
    def _():
        part[...] = total[...].astype(bf16)


def attend_back(grads, first, weights, w_out, cosine, sine, queries, keys, values, mixed, log_sum):
    length, width = first.shape
    wide = w_out.shape[0]
    tall = pl.BlockSpec((length, LANES), lambda i: (0, i))
    blocks = pl.BlockSpec((3, LANES, width), lambda i: (0, i, 0))
    flat = pl.BlockSpec((LANES, width), lambda i: (i, 0))
    return call(
        attend_back_kernel,
        wide // LANES,
        (grads, first, weights, w_out, cosine, sine, queries, keys, values, mixed, log_sum),
        [full(grads.shape), full(first.shape), blocks, flat, full(cosine.shape), full(sine.shape)] + [tall] * 5,
        [
            jax.ShapeDtypeStruct(weights.shape, bf16),
            jax.ShapeDtypeStruct(w_out.shape, bf16),
            jax.ShapeDtypeStruct((length, width), bf16),
        ],
        [blocks, flat, full((length, width))],
        [pltpu.VMEM((length, width), f32), pltpu.VMEM((length, length), bf16)],
        flops=16 * length * width * wide + 40 * length * length * wide,
        moved=16 * length * width,
        special=length * length * wide // HEAD_DIM,
    )


def upper_kernel(residual, own, other, table, w_up, second_res, second, active, bend):
    values = residual[...] + row(table, GATE1) * (own[...].astype(f32) + other[...].astype(f32))
    second_res[...] = values
    hat, _ = centered(values)
    factor = row(table, NORM2) * (1.0 + row(table, SCALE2))
    inner = (hat * factor + row(table, SHIFT2)).astype(bf16)
    second[...] = inner
    hidden = w_up.shape[2]
    root = 0.7978845608028654
    for block in range(2):
        span = slice(block * hidden, (block + 1) * hidden)
        u = dot(inner, w_up[block]) + table[10 + block : 11 + block, :hidden]
        square = u * u
        curve = jnp.tanh(root * (u + 0.044715 * (square * u)))
        rise = 0.5 + 0.5 * curve
        active[:, span] = (u * rise).astype(bf16)
        bend[:, span] = rise + (0.5 * root) * u * (1.0 - curve * curve) * (1.0 + 0.134145 * square)


def upper(residual, own, other, table, w_up, size=256):
    length, width = residual.shape
    hidden = 2 * w_up.shape[2]
    steps = length // size
    spec = rows_of(size, width)
    return call(
        upper_kernel,
        steps,
        (residual, own, other, table, w_up),
        [spec, spec, rows_of(size, width, steps // 2, steps), full(table.shape), full(w_up.shape)],
        [
            jax.ShapeDtypeStruct((length, width), f32),
            jax.ShapeDtypeStruct((length, width), bf16),
            jax.ShapeDtypeStruct((length, hidden), bf16),
            jax.ShapeDtypeStruct((length, hidden), f32),
        ],
        [spec, spec, rows_of(size, hidden), rows_of(size, hidden)],
        flops=2 * length * width * hidden,
        moved=14 * length * width + 6 * length * hidden,
        special=length * hidden,
    )


def ffn_back_kernel(upstream, table, w_down, w_up, bend, grad_mlp, grad_upper, part, sums, sum_down):
    step = pl.program_id(0)
    low = (row(table, GATE2) * upstream[...].astype(f32)).astype(bf16)
    grad_mlp[...] = low
    grad = (dot(low, w_down[...], NT) * bend[...]).astype(bf16)
    grad_upper[...] = grad
    hidden = w_up.shape[2]
    part[...] = (dot(grad[:, :hidden], w_up[0], NT) + dot(grad[:, hidden:], w_up[1], NT)).astype(bf16)

    @pl.when(step == 0)
    def _():
        sums[...] = jnp.zeros_like(sums)
        sum_down[...] = jnp.zeros_like(sum_down)

    sums[0:1, :] += over_rows(grad.astype(f32))

    @pl.when(step < pl.num_programs(0) // 2)
    def _():
        sum_down[0:1, :] += over_rows(low.astype(f32))


def ffn_back(upstream, table, w_down, w_up, bend, size=256):
    length, width = upstream.shape
    hidden = w_down.shape[0]
    spec = rows_of(size, width)
    broad = rows_of(size, hidden)
    return call(
        ffn_back_kernel,
        length // size,
        (upstream, table, w_down, w_up, bend),
        [spec, full(table.shape), full(w_down.shape), full(w_up.shape), broad],
        [
            jax.ShapeDtypeStruct((length, width), bf16),
            jax.ShapeDtypeStruct((length, hidden), bf16),
            jax.ShapeDtypeStruct((length, width), bf16),
            jax.ShapeDtypeStruct((8, hidden), f32),
            jax.ShapeDtypeStruct((8, width), f32),
        ],
        [spec, broad, spec, full((8, hidden)), full((8, width))],
        flops=4 * length * width * hidden,
        moved=6 * length * width + 6 * length * hidden + 4 * width * hidden,
    )


def middle_kernel(own, other, upstream, second_res, attn_own, attn_other, table, grad_res, grad_attn, sums):
    step = pl.program_id(0)
    grad = own[...].astype(f32) + other[...].astype(f32)
    hat, inverse = centered(second_res[...])
    factor = row(table, NORM2) * (1.0 + row(table, SCALE2))
    result = upstream[...].astype(f32) + norm_back(grad, hat, inverse, factor)
    grad_res[...] = result
    grad_attn[...] = (row(table, GATE1) * result).astype(bf16)

    @pl.when(step == 0)
    def _():
        sums[...] = jnp.zeros_like(sums)

    @pl.when(step < pl.num_programs(0) // 2)
    def _():
        attn = attn_own[...].astype(f32) + attn_other[...].astype(f32)
        sums[0:1, :] += over_rows(grad)
        sums[1:2, :] += over_rows(grad * hat)
        sums[2:3, :] += over_rows(result * attn)


def middle(own, other, upstream, second_res, attn_own, attn_other, table, size=256):
    length, width = upstream.shape
    steps = length // size
    spec = rows_of(size, width)
    turned = rows_of(size, width, steps // 2, steps)
    return call(
        middle_kernel,
        steps,
        (own, other, upstream, second_res, attn_own, attn_other, table),
        [spec, turned, spec, spec, spec, turned, full(table.shape)],
        [
            jax.ShapeDtypeStruct((length, width), f32),
            jax.ShapeDtypeStruct((length, width), bf16),
            jax.ShapeDtypeStruct((8, width), f32),
        ],
        [spec, spec, full((8, width))],
        flops=40 * length * width,
        moved=20 * length * width,
    )


def leave_kernel(second_res, own, other, upstream, table, layer, sums):
    step = pl.program_id(0)
    mlp = own[...].astype(f32) + other[...].astype(f32) + row(table, B_DOWN)
    layer[...] = (second_res[...] + row(table, GATE2) * mlp).astype(bf16)

    @pl.when(step == 0)
    def _():
        sums[...] = jnp.zeros_like(sums)

    sums[0:1, :] += over_rows(upstream[...].astype(f32) * mlp)


def leave(second_res, own, other, upstream, table, size=256):
    length, width = other.shape
    spec = rows_of(size, width)
    return call(
        leave_kernel,
        length // size,
        (second_res, own, other, upstream, table),
        [spec, spec, spec, spec, full(table.shape)],
        [jax.ShapeDtypeStruct((length, width), bf16), jax.ShapeDtypeStruct((8, width), f32)],
        [spec, full((8, width))],
        flops=6 * length * width,
        moved=12 * length * width,
    )


def end_kernel(own, other, residual, mask, grad_res, table, grad_in, sums):
    step = pl.program_id(0)
    grad = own[...].astype(f32) + other[...].astype(f32)
    hat, inverse = centered(residual[...])
    factor = row(table, NORM1) * (1.0 + row(table, SCALE1))
    result = grad_res[...] + norm_back(grad, hat, inverse, factor)
    grad_in[...] = result.astype(bf16)

    @pl.when(step == 0)
    def _():
        sums[...] = jnp.zeros_like(sums)

    sums[0:1, :] += over_rows(grad)
    sums[1:2, :] += over_rows(grad * hat)
    sums[2:3, :] += over_rows(result * mask[...])


def end(own, other, residual, mask, grad_res, table, size=256):
    length, width = other.shape
    spec = rows_of(size, width)
    return call(
        end_kernel,
        length // size,
        (own, other, residual, mask, grad_res, table),
        [spec, spec, spec, rows_of(size, 1), spec, full(table.shape)],
        [jax.ShapeDtypeStruct((length, width), bf16), jax.ShapeDtypeStruct((8, width), f32)],
        [spec, full((8, width))],
        flops=30 * length * width,
        moved=16 * length * width,
    )


class Moves:
    def __init__(self, dp_size, rank_size):
        self.dp_size, self.rank_size = dp_size, rank_size

    def by(self, values, target, back=False):
        pairs = []
        for dp in range(self.dp_size):
            for rank in range(self.rank_size):
                core, to_rank = target(dp & 1, rank)
                pair = (dp * self.rank_size + rank, (dp >> 1 << 1 | core) * self.rank_size + to_rank)
                pairs.append(pair[::-1] if back else pair)
        return lax.ppermute(values, ("dp", "tensor"), pairs)

    def flip(self, values, bit):
        pairs = [
            (dp * self.rank_size + rank, (dp ^ 1 << bit) * self.rank_size + rank)
            for dp in range(self.dp_size)
            for rank in range(self.rank_size)
        ]
        return lax.ppermute(values, ("dp", "tensor"), pairs)

    def flip_rank(self, values, bit):
        return self.by(values, lambda core, rank: (core, rank ^ 1 << bit))

    @staticmethod
    def even(core, rank):
        return (core, rank) if core == rank >> 1 else (rank >> 1, rank ^ 2)

    @staticmethod
    def odd(core, rank):
        return (core, rank ^ 1) if core == rank >> 1 else (rank >> 1, rank ^ 3)

    @staticmethod
    def gathering(turn):
        def target(core, rank):
            to_rank = rank ^ turn
            return (0, to_rank) if to_rank >> 1 == core else (1, to_rank ^ 2)

        return target


def shards(
    tokens_in,
    token_mask,
    grid_index,
    time_table,
    cotangent,
    w_ada,
    b_ada,
    norm1,
    norm2,
    mask_vector,
    w_qkv,
    w_out,
    w_up,
    b_up,
    w_down,
    b_down,
):
    dp_size, ranks = lax.axis_size("dp"), lax.axis_size("tensor")
    dp, rank = lax.axis_index("dp"), lax.axis_index("tensor")
    core, quarter = dp & 1, dp >> 1 & 3
    parity = rank & 1
    moves = Moves(dp_size, ranks)
    _, row_count, width = tokens_in.shape
    shard_width = w_out.shape[0]
    hidden = w_up.shape[1]
    length = row_count * ranks
    half_rows = row_count // 2
    own_rows = length // 2
    cond_width = time_table.shape[0 + 1]

    grid_all = grid_index
    pair_grid = None
    for bit in range(dp_size.bit_length() - 1):
        came = moves.flip(grid_all, bit)
        ahead = (dp >> bit & 1) == 1
        grid_all = jnp.where(ahead, jnp.concatenate([came, grid_all]), jnp.concatenate([grid_all, came]))
        if bit == 0:
            pair_grid = grid_all

    def sender_chunk(values, turn):
        to_rank = rank ^ turn
        half = jnp.where(to_rank >> 1 == core, 0, 1)
        return (to_rank & 1, half)

    def to_chip(values):
        blocks = []
        for turn in range(4):
            b, h = sender_chunk(values, turn)
            chunk = lax.dynamic_slice(values, (b, h, 0, 0), (1, 1) + values.shape[2:])[0, 0]
            blocks.append(moves.by(chunk, moves.gathering(turn)))
        return blocks

    def from_chip(values):
        result = jnp.zeros((2, 2) + values.shape[1:], values.dtype)
        for turn in range(4):
            chunk = moves.by(values[turn], moves.gathering(turn), back=True)
            b, h = sender_chunk(result, turn)
            result = lax.dynamic_update_slice(result, chunk[None, None], (b, h, 0, 0))
        return result.reshape(2, 2 * values.shape[1], values.shape[2])

    mask_rows = token_mask.reshape(2, 2, 1, half_rows).astype(bf16)
    mask_rows = jnp.pad(mask_rows, ((0, 0), (0, 0), (0, 15), (0, width - half_rows)))
    packed = jnp.concatenate([tokens_in.reshape(2, 2, half_rows, width), mask_rows], axis=2)
    own_blocks = jnp.stack(to_chip(packed))
    other_blocks = moves.flip(own_blocks, CORE)
    both_blocks = jnp.concatenate([own_blocks, other_blocks])
    tokens = both_blocks[:, :half_rows].reshape(length, width)
    mask = both_blocks[:, half_rows, :half_rows].astype(f32).reshape(length, 1)
    upstream_own = jnp.concatenate(to_chip(cotangent.reshape(2, 2, half_rows, width)))
    upstream = jnp.concatenate([upstream_own, moves.flip(upstream_own, CORE)])

    starts = []
    for side in (core, 1 - core):
        for turn in range(4):
            starts.append((rank ^ turn ^ 2 * side) * row_count + side * half_rows)
    positions = jnp.stack(starts)[:, None] + jnp.arange(half_rows, dtype=jnp.int32)[None, :]
    lane = jnp.arange(LANES, dtype=jnp.int32)
    half_dim = HEAD_DIM // 2
    frequency = 10000.0 ** (-(lane % half_dim).astype(f32) / half_dim)
    angles = positions.reshape(length, 1).astype(f32) * frequency[None, :]
    cosine = jnp.cos(angles)
    sine = jnp.sin(angles) * jnp.where(lane % HEAD_DIM < half_dim, -1.0, 1.0)[None, :]

    here = lax.dynamic_index_in_dim(pair_grid, rank, 0, keepdims=False)
    cond_pre = lax.dynamic_slice(time_table, (here, 0), (1, cond_width))
    cond_low = jax.nn.silu(cond_pre).astype(bf16)
    ada_flat = w_ada.reshape(cond_width, 6 * width)
    modulation = jnp.dot(cond_low, ada_flat, preferred_element_type=f32).reshape(6, width) + b_ada

    def quarter_of(values, rows):
        return lax.dynamic_slice_in_dim(values, quarter * rows, rows, 0)

    def collect(piece):
        first, second = moves.by(piece, moves.even), moves.by(piece, moves.odd)
        first_x, second_y = moves.flip(first, X), moves.flip(second, Y)
        first_more = moves.flip(jnp.stack([first, first_x]), Y)
        second_more = moves.flip(jnp.stack([second, second_y]), X)
        return (
            (first, first_x, first_more[0], first_more[1]),
            (second, second_more[0], second_y, second_more[1]),
        )

    def place(pieces, rows):
        pieces = tuple(tuple(p if rows is None else p[rows] for p in shard) for shard in pieces)
        shape = pieces[0][0].shape
        result = jnp.zeros((2, 4) + shape, bf16)
        for index, shard in enumerate(pieces):
            for turn, p in enumerate(shard):
                result = lax.dynamic_update_slice(result, p[None, None], (index, quarter ^ turn) + (0,) * len(shape))
        return result

    qkv_rows = shard_width // 4
    qkv_slice = lax.dynamic_slice_in_dim(w_qkv, quarter * qkv_rows, qkv_rows, 2)
    qkv_piece = qkv_slice.transpose(1, 2, 0).reshape(3 * qkv_rows, width)
    attn_pieces = collect(jnp.concatenate([qkv_piece, quarter_of(w_out, qkv_rows)]))
    up_pieces = collect(quarter_of(w_up, width // 4))
    down_pieces = collect(quarter_of(w_down, hidden // 4))
    attn_placed = place(attn_pieces, None)
    qkv_t = attn_placed[:, :, : 3 * qkv_rows].reshape(2, 4, 3, qkv_rows, width).transpose(2, 0, 1, 3, 4)
    qkv_t = qkv_t.reshape(3, 2 * shard_width, width)
    out_rows = attn_placed[:, :, 3 * qkv_rows :].reshape(2 * shard_width, width)
    up_full = place(up_pieces, None).reshape(2, width, hidden)
    down_full = place(down_pieces, None).reshape(2 * hidden, width)
    bias_up = jnp.stack([moves.by(b_up, moves.even), moves.by(b_up, moves.odd)])

    table = jnp.concatenate(
        [modulation, norm1[None], norm2[None], mask_vector[None], b_down[None], bias_up, jnp.zeros((4, width), f32)]
    )

    residual, first_in = call(
        enter_kernel,
        length // 256,
        (tokens, mask, table),
        [rows_of(256, width), rows_of(256, 1), full(table.shape)],
        [jax.ShapeDtypeStruct((length, width), f32), jax.ShapeDtypeStruct((length, width), bf16)],
        [rows_of(256, width), rows_of(256, width)],
        flops=10 * length * width,
        moved=8 * length * width,
    )
    queries, keys, values, mixed, log_sum, attn_own = attend(first_in, qkv_t, out_rows, cosine, sine)
    attn_other = moves.flip(attn_own, CORE)
    second_res, second_in, active, bend = upper(residual, attn_own, attn_other, table, up_full)
    grad_mlp, grad_upper, second_own, sum_upper, sum_down = ffn_back(upstream, table, down_full, up_full, bend)
    second_other = moves.flip(second_own, CORE)
    mlp_part = dot(active, down_full).astype(bf16)
    mlp_other = moves.flip(mlp_part[own_rows:], CORE)
    layer_own, sum_gate2 = leave(second_res, mlp_part, mlp_other, upstream, table)
    layer_out = from_chip(layer_own.reshape(4, half_rows, width))

    def reduce(shards_here):
        def piece(index, turn):
            return lax.dynamic_index_in_dim(shards_here[index], quarter ^ turn, 0, keepdims=False)

        first_came = moves.flip(jnp.stack([piece(0, 2), piece(0, 3)]), Y).astype(f32)
        second_came = moves.flip(jnp.stack([piece(1, 1), piece(1, 3)]), X).astype(f32)
        first_next = (piece(0, 1).astype(f32) + first_came[1]).astype(bf16)
        second_next = (piece(1, 2).astype(f32) + second_came[1]).astype(bf16)
        first_last = moves.flip(first_next, X).astype(f32)
        second_last = moves.flip(second_next, Y).astype(f32)
        first = (piece(0, 0).astype(f32) + first_came[0] + first_last).astype(bf16)
        second = (piece(1, 0).astype(f32) + second_came[0] + second_last).astype(bf16)
        mine = moves.by(first, moves.even, back=True).astype(f32) + moves.by(second, moves.odd, back=True).astype(f32)
        for bit in range(3, dp_size.bit_length() - 1):
            mine = mine + moves.flip(mine, bit)
        halves = mine.reshape(2, mine.shape[0] // 2, width)
        kept = lax.dynamic_index_in_dim(halves, core, 0, keepdims=False)
        given = lax.dynamic_index_in_dim(halves, 1 - core, 0, keepdims=False)
        half = (kept + moves.flip(given, CORE)).astype(bf16)
        upper_half, lower_half = jnp.split(half, 2)
        upper_x, lower_y = moves.flip(upper_half, X), moves.flip(lower_half, Y)
        upper_more = moves.flip(jnp.stack([upper_half, upper_x]), Y)
        lower_more = moves.flip(jnp.stack([lower_half, lower_y]), X)
        pieces = jnp.stack(
            [
                jnp.stack([upper_half, lower_half]),
                jnp.stack([upper_x, lower_more[0]]),
                jnp.stack([upper_more[0], lower_y]),
                jnp.stack([upper_more[1], lower_more[1]]),
            ]
        ).reshape(4, half.shape[0], width)
        sides = jnp.stack([pieces, moves.flip(pieces, CORE)])
        ordered = [
            lax.dynamic_slice(sides, (core ^ side, quarter ^ turn, 0, 0), (1, 1) + half.shape)[0, 0]
            for turn in range(4)
            for side in range(2)
        ]
        return jnp.concatenate(ordered).astype(f32).reshape(4, 2 * half.shape[0], width)

    d_down = dot(active, grad_mlp, TN).astype(bf16).reshape(2, 4, hidden // 4, width)
    grad_w_down = reduce((d_down[0], d_down[1])).reshape(hidden, width)
    d_up = [
        dot(second_in, grad_upper[:, block * hidden : (block + 1) * hidden], TN).astype(bf16).reshape(4, width // 4, hidden)
        for block in range(2)
    ]
    grad_w_up = reduce(d_up).reshape(width, hidden)

    grad_res, grad_attn, sum_middle = middle(second_own, second_other, upstream, second_res, attn_own, attn_other, table)
    d_qkv, d_out, first_own = attend_back(
        grad_attn, first_in, qkv_t, out_rows, cosine, sine, queries, keys, values, mixed, log_sum
    )
    first_other = moves.flip(first_own[own_rows:], CORE)
    grad_own, sum_end = end(first_own, first_other, residual, mask, grad_res, table)
    grad_in = from_chip(grad_own.reshape(4, half_rows, width))
    d_attn = jnp.concatenate(
        [
            d_qkv.reshape(3, 2, 4, qkv_rows, width).transpose(1, 2, 0, 3, 4).reshape(2, 4, 3 * qkv_rows, width),
            d_out.reshape(2, 4, qkv_rows, width),
        ],
        axis=2,
    )
    grad_attn_rows = reduce((d_attn[0], d_attn[1]))
    grad_w_out = grad_attn_rows[:, 3 * qkv_rows :].reshape(shard_width, width)
    grad_w_qkv = grad_attn_rows[:, : 3 * qkv_rows].reshape(4, 3, qkv_rows, width)
    grad_w_qkv = grad_w_qkv.transpose(3, 1, 0, 2).reshape(width, 3, shard_width)

    def of_all(rows):
        result = rows[None]
        for bit in range(ranks.bit_length() - 1):
            came = moves.flip_rank(result, bit)
            ahead = (rank >> bit & 1) == 1
            result = jnp.where(ahead, jnp.concatenate([came, result]), jnp.concatenate([result, came]))
        for bit in range(1, dp_size.bit_length() - 1):
            came = moves.flip(result, bit)
            ahead = (dp >> bit & 1) == 1
            result = jnp.where(ahead, jnp.concatenate([came, result]), jnp.concatenate([result, came]))
        return result

    scale_up = 1.0 + modulation
    upper_two = sum_upper[0].reshape(2, hidden)
    upper_two = jnp.where(parity == 1, upper_two[::-1], upper_two)
    early = jnp.stack(
        [
            sum_middle[2],
            sum_middle[0],
            sum_middle[1] * norm2,
            sum_gate2[0],
            sum_middle[1] * scale_up[4],
            sum_down[0],
        ]
    )
    came = moves.flip(jnp.concatenate([early, upper_two]), CORE)
    upper_came = came[6:]
    early = jnp.concatenate(
        [
            early + came[:6],
            jnp.where(core == 0, upper_two, upper_came),
            jnp.where(core == 0, upper_came, upper_two),
        ]
    )
    early = of_all(early)
    late = jnp.stack([sum_end[0], sum_end[1] * norm1, sum_end[1] * scale_up[1], sum_end[2]])
    late = of_all(late + moves.flip(late, CORE))
    early_sums, late_sums = jnp.sum(early, axis=0), jnp.sum(late, axis=0)
    grad_mods = jnp.concatenate([late[:, :2], early[:, :4]], axis=1)
    grad_b_up = lax.dynamic_index_in_dim(early_sums[6:], rank, 0, keepdims=False)

    points = time_table.shape[0]
    onehot = (grid_all[:, None] == jnp.arange(points, dtype=jnp.int32)[None, :]).astype(f32)
    cond_all = jnp.dot(onehot, time_table, precision=highest)
    cond_act, silu_back = jax.vjp(jax.nn.silu, cond_all)
    cond_act = cond_act.astype(bf16).astype(f32)
    grad_flat = grad_mods.reshape(-1, 6 * width)
    grad_w_ada = jnp.dot(cond_act.T, grad_flat, precision=highest).reshape(cond_width, 6, width)
    grad_b_ada = jnp.sum(grad_mods, axis=0)
    grad_cond = jnp.dot(grad_flat, ada_flat.astype(f32).T, precision=highest)
    grad_pre = silu_back(grad_cond)[0]
    grad_table = jnp.dot(onehot.T, grad_pre, precision=highest)
    return (
        layer_out,
        grad_in,
        grad_table,
        late_sums[3],
        grad_w_ada,
        grad_b_ada,
        late_sums[2],
        early_sums[4],
        grad_w_qkv,
        grad_w_out,
        grad_w_up,
        grad_b_up,
        grad_w_down,
        early_sums[5],
    )


def solution(mesh):
    whole = P()
    split = P("dp", "tensor", None)
    return jax.shard_map(
        shards,
        mesh=mesh,
        in_specs=(
            split,
            P("dp", "tensor"),
            P("dp"),
            whole,
            split,
            whole,
            whole,
            whole,
            whole,
            whole,
            P(None, None, "tensor"),
            P("tensor", None),
            P(None, "tensor"),
            P("tensor"),
            P("tensor", None),
            whole,
        ),
        out_specs=(
            split,
            split,
            whole,
            whole,
            whole,
            whole,
            whole,
            whole,
            P(None, None, "tensor"),
            P("tensor", None),
            P(None, "tensor"),
            P("tensor"),
            P("tensor", None),
            whole,
        ),
        check_vma=False,
    )
```

```python
import functools

import jax
import jax.numpy as jnp
from jax import lax
from jax.experimental import pallas as pl
from jax.experimental.pallas import tpu as pltpu
from jax.sharding import PartitionSpec as P

HEAD_DIM = 64
LANES = 128
EXTRA = 16
f32 = jnp.float32
bf16 = jnp.bfloat16
highest = lax.Precision.HIGHEST
NN = (((1,), (0,)), ((), ()))
NT = (((1,), (1,)), ((), ()))
TN = (((0,), (0,)), ((), ()))
DP = ("r", "y", "x", "c")
AXES = DP + ("tensor",)
MIB = 2**20
SHARE = 64

SHIFT1, SCALE1, GATE1, SHIFT2, SCALE2, GATE2, NORM1, NORM2, MASKED, B_DOWN, B_UP = range(11)


def dot(left, right, dims=NN):
    return lax.dot_general(left, right, dims, preferred_element_type=f32)


def row(table, index):
    return table[index : index + 1, :]


def full(shape):
    return pl.BlockSpec(shape, lambda *i: (0,) * len(shape))


def by_rows(size, width):
    return pl.BlockSpec((size, width), lambda i: (i, 0))


def like(shape, dtype):
    return jax.ShapeDtypeStruct(shape, dtype)


def call(body, grid, ins, specs, outs, out_specs, scratch=(), mib=24, flops=0, special=0, name=None):
    moved = sum(x.size * x.dtype.itemsize for x in ins) + sum(x.size * x.dtype.itemsize for x in outs)
    return pl.pallas_call(
        body,
        grid=(grid,),
        in_specs=specs,
        out_specs=out_specs,
        out_shape=outs,
        scratch_shapes=list(scratch),
        name=name,
        compiler_params=pltpu.CompilerParams(vmem_limit_bytes=mib * MIB),
        cost_estimate=pl.CostEstimate(flops=flops // SHARE, bytes_accessed=moved // SHARE, transcendentals=special // SHARE),
    )(*ins)


def centered(values):
    average = jnp.mean(values, axis=-1, keepdims=True)
    away = values - average
    inverse = lax.rsqrt(jnp.mean(away * away, axis=-1, keepdims=True) + 1e-05)
    return away * inverse, inverse


def norm_back(grads, hat, inverse, factor):
    slope = grads * factor
    lean = jnp.mean(slope, axis=-1, keepdims=True)
    tilt = jnp.mean(slope * hat, axis=-1, keepdims=True)
    return (slope - lean - hat * tilt) * inverse


def after(values, *others):
    return lax.optimization_barrier((values,) + others)[0]


def together(values, *others):
    return lax.optimization_barrier(values + others)[: len(values)]


def over_rows(values):
    return jnp.sum(values, axis=0, keepdims=True)


def mask_column(extra):
    count = extra.shape[1] // LANES * LANES
    line = extra[0:1, :].astype(f32)
    return jnp.broadcast_to(line, (LANES, count)).T[:, 0:1]


def place_kernel(plan, steps, place_of, *refs):
    (one, two, first_y, second_x), outs = refs[:4], refs[4:]
    if steps == 0:
        shards_of = (tuple((piece, None) for piece in refs[:4]),)
    elif steps == 1:
        shards_of = tuple(tuple((piece, shard) for piece in refs[:4]) for shard in range(2))
    else:
        shards_of = (((one, 0), (one, 1), (first_y, 0), (first_y, 1)), ((two, 0), (second_x, 0), (two, 1), (second_x, 1)))
    for turn in range(4):
        here = place_of[0] ^ turn
        for (shard, start, size), out, (lead, base, pitch) in plan:
            piece, index = shards_of[shard][turn]
            rows = pl.ds(pl.multiple_of(base + here * pitch, 16), size)
            where = (rows, slice(None)) if lead is None else (lead, rows, slice(None))
            rows_of = slice(start, start + size)
            outs[out][where] = piece[rows_of, :] if index is None else piece[index, rows_of, :]


def place(pieces, place_of, plan, outs, steps=2):
    moved = sum(2 * x.size * x.dtype.itemsize for x in outs)
    return pl.pallas_call(
        functools.partial(place_kernel, plan, steps),
        in_specs=[pl.BlockSpec(memory_space=pltpu.SMEM)] + [pl.BlockSpec(memory_space=pltpu.VMEM)] * 4,
        out_specs=[pl.BlockSpec(memory_space=pltpu.VMEM)] * len(outs),
        out_shape=outs,
        name="place",
        compiler_params=pltpu.CompilerParams(vmem_limit_bytes=12 * MIB),
        cost_estimate=pl.CostEstimate(flops=0, bytes_accessed=moved // SHARE, transcendentals=0),
    )(place_of, *pieces)


def finish_kernel(plan, place_of, *refs):
    pieces, outs = refs[:8], refs[8:]
    quarter, core = place_of[0], place_of[1]
    for turn in range(4):
        here = quarter ^ turn
        for side in range(2):
            which = core ^ side
            piece = pieces[2 * turn + side]
            for out, size, pitch in plan:
                rows = pl.ds(pl.multiple_of(here * pitch + which * size, 8), size)
                outs[out][rows, :] = piece[...].astype(f32)


def finish(pieces, place_of, shape):
    half = pieces[0].shape[0]
    return pl.pallas_call(
        functools.partial(finish_kernel, ((0, half, 2 * half),)),
        in_specs=[pl.BlockSpec(memory_space=pltpu.SMEM)] + [pl.BlockSpec(memory_space=pltpu.VMEM)] * 8,
        out_specs=[pl.BlockSpec(memory_space=pltpu.VMEM)],
        out_shape=[like(shape, f32)],
        name="finish",
        compiler_params=pltpu.CompilerParams(vmem_limit_bytes=16 * MIB),
        cost_estimate=pl.CostEstimate(flops=0, bytes_accessed=6 * shape[0] * shape[1] // SHARE, transcendentals=0),
    )(place_of, *pieces)[0]


def enter_kernel(even, odd, table, residual, first):
    rows = even.shape[0] - EXTRA
    for index, pack in enumerate((even, odd)):
        here = slice(index * rows, (index + 1) * rows)
        mask = mask_column(pack[rows:, :rows])
        values = pack[:rows, :].astype(f32) + mask * row(table, MASKED)
        residual[here, :] = values
        hat, _ = centered(values)
        factor = row(table, NORM1) * (1.0 + row(table, SCALE1))
        first[here, :] = (hat * factor + row(table, SHIFT1)).astype(bf16)


def enter(even, odd, table):
    rows, width = 2 * (even.shape[0] - EXTRA), even.shape[1]
    return call(
        enter_kernel,
        1,
        (even, odd, table),
        [full(even.shape), full(odd.shape), full(table.shape)],
        [like((rows, width), f32), like((rows, width), bf16)],
        [full((rows, width))] * 2,
        name="enter",
    )


def partner(values):
    lane = lax.broadcasted_iota(jnp.int32, values.shape, 1)
    ahead = pltpu.roll(values, LANES - HEAD_DIM // 2, 1)
    behind = pltpu.roll(values, HEAD_DIM // 2, 1)
    return jnp.where(lane % HEAD_DIM < HEAD_DIM // 2, ahead, behind)


def heads_of(values):
    lane = lax.broadcasted_iota(jnp.int32, values.shape, 1)
    return lane < HEAD_DIM


def attend_kernel(
    own, other, weights, w_out, cosine, sine, queries, keys, values, mixed, log_sum, part_own, part_other, total
):
    step = pl.program_id(0)
    half = own.shape[0]
    length = 2 * half
    chunk = 256
    for index, tokens in enumerate((own, other)):
        here = slice(index * half, (index + 1) * half)
        query = dot(tokens[...], weights[0], NT)
        turned = (query * cosine[here, :] + partner(query) * sine[here, :]).astype(bf16)
        queries[here, :] = (turned * HEAD_DIM**-0.5).astype(bf16)
        key = dot(tokens[...], weights[1], NT)
        keys[here, :] = (key * cosine[here, :] + partner(key) * sine[here, :]).astype(bf16)
        values[here, :] = dot(tokens[...], weights[2], NT).astype(bf16)

    @pl.when(step == 0)
    def _():
        total[...] = jnp.zeros_like(total)

    for start in range(0, length, chunk):
        here = pl.ds(start, chunk)
        block = queries[here, :]
        former = heads_of(block)
        halves = []
        for head in range(2):
            mine = former if head == 0 else ~former
            scores = dot(jnp.where(mine, block, 0), keys[...], NT)
            top = jnp.max(scores, axis=1, keepdims=True)
            powers = jnp.exp(scores - top)
            sums = jnp.sum(powers, axis=1, keepdims=True)
            out = dot(powers.astype(bf16), values[...]) / sums
            halves.append((out, top + jnp.log(sums)))
        out = jnp.where(former, halves[0][0], halves[1][0])
        mixed[here, :] = out
        log_sum[here, :] = jnp.where(former, halves[0][1], halves[1][1])
        total[here, :] += dot(out.astype(bf16), w_out[...])

    @pl.when(step == pl.num_programs(0) - 1)
    def _():
        part_own[...] = total[:half, :].astype(bf16)
        part_other[...] = total[half:, :].astype(bf16)


def attend(own, other, weights, w_out, cosine, sine):
    half, width = own.shape
    length = 2 * half
    wide = w_out.shape[0]
    tall = pl.BlockSpec((length, LANES), lambda i: (0, i))
    return call(
        attend_kernel,
        wide // LANES,
        (own, other, weights, w_out, cosine, sine),
        [
            full(own.shape),
            full(own.shape),
            pl.BlockSpec((3, LANES, width), lambda i: (0, i, 0)),
            pl.BlockSpec((LANES, width), lambda i: (i, 0)),
            full(cosine.shape),
            full(sine.shape),
        ],
        [like((length, wide), bf16)] * 3 + [like((length, wide), f32)] * 2 + [like((half, width), bf16)] * 2,
        [tall] * 5 + [full((half, width))] * 2,
        [pltpu.VMEM((length, width), f32)],
        mib=36,
        flops=8 * length * width * wide + 16 * length * length * wide,
        special=length * length * wide // HEAD_DIM,
        name="attend",
    )


def pair_back(grads_own, grads_other, own, other, w_out, cosine, sine, queries, keys, values, mixed, log_sum, scores_t):
    half = own.shape[0]
    length = 2 * half
    chunk = 256
    outs = mixed[...]
    low = outs.astype(bf16)
    grad = jnp.concatenate([dot(grads_own[...], w_out[...], NT), dot(grads_other[...], w_out[...], NT)]).astype(bf16)
    d_out = dot(low[:half], grads_own[...], TN) + dot(low[half:], grads_other[...], TN)
    lean_t = (grad.astype(f32) * outs).T
    log_t = log_sum[...].T
    query, key, value = queries[...], keys[...], values[...]
    former = heads_of(query)
    former_chunk = heads_of(query[:chunk])
    found_q, found_k, found_v = [], [], []
    for head in range(2):
        lean = over_rows(lean_t[head * HEAD_DIM : (head + 1) * HEAD_DIM])
        log_row = log_t[head * HEAD_DIM : head * HEAD_DIM + 1]
        mine = former_chunk if head == 0 else ~former_chunk
        part_k, part_v = [], []
        for start in range(0, length, chunk):
            key_rows = jnp.where(mine, key[start : start + chunk], 0)
            value_rows = jnp.where(mine, value[start : start + chunk], 0)
            probs = jnp.exp(dot(key_rows, query, NT) - log_row)
            part_v.append(dot(probs.astype(bf16), grad))
            slopes = (probs * (dot(value_rows, grad, NT) - lean)).astype(bf16)
            scores_t[start : start + chunk, :] = slopes
            part_k.append(dot(slopes, query))
        found_q.append(dot(scores_t[...], key, TN))
        found_k.append(jnp.concatenate(part_k, axis=0))
        found_v.append(jnp.concatenate(part_v, axis=0))
    d_query = jnp.where(former, found_q[0], found_q[1]) * HEAD_DIM**-0.5
    d_key = jnp.where(former, found_k[0], found_k[1])
    d_value = jnp.where(former, found_v[0], found_v[1]).astype(bf16)
    d_query = (d_query * cosine[...] + partner(d_query * sine[...])).astype(bf16)
    d_key = (d_key * cosine[...] + partner(d_key * sine[...])).astype(bf16)
    found = (d_query, d_key, d_value)
    return found, [dot(g[:half], own[...], TN) + dot(g[half:], other[...], TN) for g in found] + [d_out]


def put_pieces(pieces, rows_of_weight, quarter, size):
    for turn, piece in enumerate(pieces):
        rows = pl.ds(pl.multiple_of((quarter ^ turn) * size, 16), size)
        for index in range(4):
            piece[index * size : (index + 1) * size, :] = rows_of_weight[index, rows, :]


def attend_back_kernel(shard_rows, place_of, *refs):
    ins, (found_all, *pieces), rest, scores_t, d_weights = refs[:12], refs[12:17], refs[17], refs[18], refs[19]
    step = pl.program_id(0)
    found, rows = pair_back(*ins, scores_t)
    here = pl.ds(pl.multiple_of(step * LANES, LANES), LANES)
    for index in range(3):
        found_all[index] = found[index]
    for index in range(4):
        d_weights[index, here, :] = rows[index].astype(bf16)

    @pl.when(step == pl.num_programs(0) - 1)
    def _():
        put_pieces(pieces, d_weights, place_of[0], shard_rows // 4)
        rest[...] = d_weights[:, shard_rows:, :]


def attend_back_end_kernel(shard_rows, place_of, rows_before, *refs):
    ins, (found_all, *pieces), scores_t, d_weights = refs[:12], refs[12:17], refs[17], refs[18]
    found, rows = pair_back(*ins, scores_t)
    start = rows_before.shape[1]
    d_weights[:, :start, :] = rows_before[...]
    for index in range(3):
        found_all[index] = found[index]
    for index in range(4):
        d_weights[index, start:, :] = rows[index].astype(bf16)
    put_pieces(pieces, d_weights, place_of[0], shard_rows // 4)


def first_grads_kernel(before, last, weights, part_own, part_other):
    half, wide = part_own.shape[0], before.shape[2]
    for out, here in ((part_other, slice(half, None)), (part_own, slice(0, half))):
        total = dot(last[0, here, :], weights[0, wide:, :])
        total += dot(last[1, here, :], weights[1, wide:, :]) + dot(last[2, here, :], weights[2, wide:, :])
        for index in range(3):
            total += dot(before[index, here, :], weights[index, :wide, :])
        out[...] = total.astype(bf16)


def attend_back(place_of, grads_own, grads_other, own, other, weights, w_out, cosine, sine, *kept):
    half, width = own.shape
    length = 2 * half
    wide = w_out.shape[0]
    shard_rows = wide // 2
    first = -(-shard_rows // LANES)
    rows = full((half, width))
    quarter = like((shard_rows, width), bf16)
    smem = pl.BlockSpec(memory_space=pltpu.SMEM)

    def specs(base):
        tall = pl.BlockSpec((length, LANES), lambda i: (0, i + base))
        flat = pl.BlockSpec((LANES, width), lambda i: (i + base, 0))
        return [rows] * 4 + [flat, full(cosine.shape), full(sine.shape)] + [tall] * 5

    ins = (grads_own, grads_other, own, other, w_out, cosine, sine) + kept
    work = dict(flops=14 * length * width * LANES + 40 * length * length * LANES, special=2 * length * length)
    found, *pieces, rest = call(
        functools.partial(attend_back_kernel, shard_rows),
        first,
        (place_of,) + ins,
        [smem] + specs(0),
        [like((3, length, first * LANES), bf16)] + [quarter] * 4 + [like((4, first * LANES - shard_rows, width), bf16)],
        [pl.BlockSpec((3, length, LANES), lambda i: (0, 0, i))]
        + [full(quarter.shape)] * 4
        + [full((4, first * LANES - shard_rows, width))],
        [pltpu.VMEM((length, length), bf16), pltpu.VMEM((4, first * LANES, width), bf16)],
        mib=60,
        name="attend_back",
        **work,
    )

    def finish_back(found, rest):
        last, *more = call(
            functools.partial(attend_back_end_kernel, shard_rows),
            1,
            (place_of, rest) + ins,
            [smem, full(rest.shape)] + specs(first),
            [like((3, length, LANES), bf16)] + [quarter] * 4,
            [full((3, length, LANES))] + [full(quarter.shape)] * 4,
            [pltpu.VMEM((length, length), bf16), pltpu.VMEM((4, shard_rows, width), bf16)],
            mib=60,
            name="attend_back_end",
            **work,
        )

        def first_grads(last):
            return call(
                first_grads_kernel,
                1,
                (found, last, weights),
                [full(found.shape), full(last.shape), full(weights.shape)],
                [like((half, width), bf16)] * 2,
                [rows] * 2,
                name="first_grads",
            )

        return more, last, first_grads

    return pieces, found, rest, finish_back


def lift(inner, table, w_up, active, bend):
    hidden = w_up.shape[2]
    root = 0.7978845608028654
    for block in range(2):
        span = slice(block * hidden, (block + 1) * hidden)
        u = dot(inner, w_up[block]) + table[B_UP + block : B_UP + block + 1, :hidden]
        square = u * u
        curve = jnp.tanh(root * (u + 0.044715 * (square * u)))
        rise = 0.5 + 0.5 * curve
        active[:, span] = (u * rise).astype(bf16)
        slope = rise + (0.5 * root) * u * (1.0 - curve * curve) * (1.0 + 0.134145 * square)
        bend[:, span] = slope.astype(bf16)


def second_kernel(residual, mine, came, table, second_res, second):
    values = residual[...] + row(table, GATE1) * (mine[...].astype(f32) + came[...].astype(f32))
    second_res[...] = values
    hat, _ = centered(values)
    factor = row(table, NORM2) * (1.0 + row(table, SCALE2))
    second[...] = (hat * factor + row(table, SHIFT2)).astype(bf16)


def second(residual, mine, came, table, size=256):
    rows, width = residual.shape
    spec = by_rows(size, width)
    return call(
        second_kernel,
        rows // size,
        (residual, mine, came, table),
        [spec, spec, spec, full(table.shape)],
        [like((rows, width), f32), like((rows, width), bf16)],
        [spec, spec],
        flops=10 * rows * width,
        name="second",
    )


def upper_kernel(inner, table, w_up, active, bend):
    lift(inner[...], table, w_up, active, bend)


def upper(inner, table, w_up, size=256):
    rows, width = inner.shape
    hidden = 2 * w_up.shape[2]
    broad = by_rows(size, hidden)
    return call(
        upper_kernel,
        rows // size,
        (inner, table, w_up),
        [by_rows(size, width), full(table.shape), full(w_up.shape)],
        [like((rows, hidden), bf16)] * 2,
        [broad, broad],
        flops=2 * rows * width * hidden,
        special=rows * hidden,
        name="upper",
    )


def ffn_back_kernel(grad_mlp, down_even, down_odd, w_up, bend, grad_upper, *refs):
    parts, sums = refs[:-1], refs[-1]
    step = pl.program_id(0)
    grad = jnp.concatenate([dot(grad_mlp[...], down[...], NT) for down in (down_even, down_odd)], axis=1)
    grad = (grad * bend[...].astype(f32)).astype(bf16)
    grad_upper[...] = grad
    hidden = w_up.shape[2]
    result = (dot(grad[:, :hidden], w_up[0], NT) + dot(grad[:, hidden:], w_up[1], NT)).astype(bf16)
    for index, part in enumerate(parts):

        @pl.when(step == index)
        def _(part=part):
            part[...] = result

    @pl.when(step == 0)
    def _():
        sums[...] = jnp.zeros_like(sums)

    sums[0:1, :] += over_rows(grad.astype(f32))


def ffn_back(grad_mlp, down_even, down_odd, w_up, bend, size=256):
    rows, width = grad_mlp.shape
    hidden = 2 * down_even.shape[0]
    spec, broad = by_rows(size, width), by_rows(size, hidden)
    return call(
        ffn_back_kernel,
        rows // size,
        (grad_mlp, down_even, down_odd, w_up, bend),
        [spec, full(down_even.shape), full(down_odd.shape), full(w_up.shape), broad],
        [like((rows, hidden), bf16)] + [like((size, width), bf16)] * (rows // size) + [like((8, hidden), f32)],
        [broad] + [full((size, width))] * (rows // size) + [full((8, hidden))],
        flops=4 * rows * width * hidden,
        name="ffn_back",
    )


def ffn_weights_kernel(place_of, left_own, left_other, right_own, right_other, *refs):
    pieces, whole = refs[:-1], refs[-1]
    whole[...] = (dot(left_own[...], right_own[...], TN) + dot(left_other[...], right_other[...], TN)).astype(bf16)
    size = whole.shape[0] // 4
    if len(pieces) == 1:
        for index in range(4):
            pieces[0][index, 0] = whole[index * size : (index + 1) * size, :]
        return
    for turn, piece in enumerate(pieces):
        rows = pl.ds(pl.multiple_of((place_of[0] ^ turn) * size, 16), size)
        piece[0] = whole[rows, :]


def ffn_weights(place_of, left, right, split_left, ordered):
    rows, width = right[0].shape if split_left else left[0].shape
    hidden = (left if split_left else right)[0].shape[1] // 2
    whole, halved = full((rows, width)), pl.BlockSpec((rows, hidden), lambda i: (0, i))
    lefts, rights = (halved, whole) if split_left else (whole, halved)
    shape = (hidden, width) if split_left else (width, hidden)
    size = shape[0] // 4
    if ordered:
        outs, specs = [(4, 2, size, shape[1])], [pl.BlockSpec((4, 1, size, shape[1]), lambda i: (0, i, 0, 0))]
    else:
        outs, specs = [(2, size, shape[1])] * 4, [pl.BlockSpec((1, size, shape[1]), lambda i: (i, 0, 0))] * 4
    return call(
        ffn_weights_kernel,
        2,
        (place_of,) + tuple(left) + tuple(right),
        [pl.BlockSpec(memory_space=pltpu.SMEM), lefts, lefts, rights, rights],
        [like(out, bf16) for out in outs],
        specs,
        [pltpu.VMEM(shape, bf16)],
        flops=8 * rows * width * hidden,
        name="ffn_weights",
    )


def sum_kernel(count, *refs):
    pieces, outs = refs[:count], refs[count:]
    for index, out in enumerate(outs):
        values = [p[...] if len(p.shape) == 2 else p[index] for p in pieces]
        out[...] = sum(v.astype(f32) for v in values).astype(out.dtype)


def add(pieces, count=1, dtype=bf16):
    shape = pieces[0].shape[-2:]
    result = pl.pallas_call(
        functools.partial(sum_kernel, len(pieces)),
        in_specs=[pl.BlockSpec(memory_space=pltpu.VMEM)] * len(pieces),
        out_specs=[pl.BlockSpec(memory_space=pltpu.VMEM)] * count,
        out_shape=[like(shape, dtype)] * count,
        name="add",
        compiler_params=pltpu.CompilerParams(vmem_limit_bytes=12 * MIB),
    )(*pieces)
    return result if count > 1 else result[0]


def middle_kernel(parts, *refs):
    mine, came = refs[:parts], refs[parts : 2 * parts]
    upstream, second_res, attn_mine, attn_came, table, grad_res, grad_attn, sums = refs[2 * parts :]
    step = pl.program_id(0)
    grad = mine[0][...].astype(f32) + came[0][...].astype(f32)
    for index in range(1, parts):
        grad = jnp.where(step == index, mine[index][...].astype(f32) + came[index][...].astype(f32), grad)
    hat, inverse = centered(second_res[...])
    factor = row(table, NORM2) * (1.0 + row(table, SCALE2))
    result = upstream[...].astype(f32) + norm_back(grad, hat, inverse, factor)
    grad_res[...] = result
    grad_attn[...] = (row(table, GATE1) * result).astype(bf16)

    @pl.when(step == 0)
    def _():
        sums[...] = jnp.zeros_like(sums)

    attn = attn_mine[...].astype(f32) + attn_came[...].astype(f32)
    sums[0:1, :] += over_rows(grad)
    sums[1:2, :] += over_rows(grad * hat)
    sums[2:3, :] += over_rows(result * attn)


def middle(mine, came, upstream, second_res, attn_mine, attn_came, table, size=256):
    rows, width = upstream.shape
    spec = by_rows(size, width)
    return call(
        functools.partial(middle_kernel, len(mine)),
        rows // size,
        (*mine, *came, upstream, second_res, attn_mine, attn_came, table),
        [full((size, width))] * (2 * len(mine)) + [spec] * 4 + [full(table.shape)],
        [like((rows, width), f32), like((rows, width), bf16), like((8, width), f32)],
        [spec, spec, full((8, width))],
        flops=40 * rows * width,
        name="middle",
    )


def lower_kernel(active, down_even, down_odd, part):
    half = down_even.shape[0]
    part[...] = (dot(active[:, :half], down_even[...]) + dot(active[:, half:], down_odd[...])).astype(bf16)


def lower(active, down_even, down_odd, size=256):
    rows, hidden = active.shape
    width = down_even.shape[1]
    return call(
        lower_kernel,
        rows // size,
        (active, down_even, down_odd),
        [by_rows(size, hidden), full(down_even.shape), full(down_odd.shape)],
        [like((rows, width), bf16)],
        [by_rows(size, width)],
        flops=2 * rows * hidden * width,
        name="lower",
    )[0]


def leave_kernel(second_res, mine, came, upstream, part_even, part_odd, table, even, odd, sums):
    mlp = mine[...].astype(f32) + came[...].astype(f32) + row(table, B_DOWN)
    layer = (second_res[...] + row(table, GATE2) * mlp).astype(bf16)
    rows = layer.shape[0] // 2
    even[:rows, :] = layer[:rows]
    odd[:rows, :] = layer[rows:]
    even[rows:, :] = part_even[...]
    odd[rows:, :] = part_odd[...]
    grads = upstream[...].astype(f32)
    sums[...] = jnp.zeros_like(sums)
    sums[0:1, :] = over_rows(grads * mlp)
    sums[1:2, :] = over_rows((row(table, GATE2) * grads).astype(bf16).astype(f32))


def leave(second_res, mine, came, upstream, parts, table):
    rows, width = upstream.shape
    spec, part = full((rows, width)), full(parts[0].shape)
    out = (rows // 2 + parts[0].shape[0], width)
    return call(
        leave_kernel,
        1,
        (second_res, mine, came, upstream, *parts, table),
        [spec] * 4 + [part] * 2 + [full(table.shape)],
        [like(out, bf16)] * 2 + [like((8, width), f32)],
        [full(out)] * 2 + [full((8, width))],
        flops=6 * rows * width,
        name="leave",
    )


def end_kernel(mine, came, residual, pack_even, pack_odd, grad_res, table, even, odd, sums):
    rows = even.shape[0]
    factor = row(table, NORM1) * (1.0 + row(table, SCALE1))
    sums[...] = jnp.zeros_like(sums)
    for index, (out, pack) in enumerate(((even, pack_even), (odd, pack_odd))):
        here = slice(index * rows, (index + 1) * rows)
        grad = mine[here, :].astype(f32) + came[here, :].astype(f32)
        hat, inverse = centered(residual[here, :])
        result = grad_res[here, :] + norm_back(grad, hat, inverse, factor)
        out[...] = result.astype(bf16)
        sums[0:1, :] += over_rows(grad)
        sums[1:2, :] += over_rows(grad * hat)
        sums[2:3, :] += over_rows(result * mask_column(pack[:, :rows]))


def end(mine, came, residual, pack_even, pack_odd, grad_res, table):
    rows, width = mine.shape
    spec = full((rows, width))
    extra = pl.BlockSpec((EXTRA, width), lambda i: (rows // 2 // EXTRA, 0))
    return call(
        end_kernel,
        1,
        (mine, came, residual, pack_even, pack_odd, grad_res, table),
        [spec, spec, spec, extra, extra, spec, full(table.shape)],
        [like((rows // 2, width), bf16)] * 2 + [like((8, width), f32)],
        [full((rows // 2, width))] * 2 + [full((8, width))],
        flops=30 * rows * width,
        name="end",
    )


def split3(values):
    high = lax.reduce_precision(values, 8, 7)
    rest = values - high
    middle_term = lax.reduce_precision(rest, 8, 7)
    return jnp.stack([high, middle_term, rest - middle_term]).astype(bf16)


class Moves:
    def __init__(self, dp_size, rank_size):
        self.dp_size, self.rank_size = dp_size, rank_size

    def by(self, values, target, back=False):
        pairs = []
        for dp in range(self.dp_size):
            for rank in range(self.rank_size):
                core, to_rank = target(dp & 1, rank)
                pair = (dp * self.rank_size + rank, (dp >> 1 << 1 | core) * self.rank_size + to_rank)
                pairs.append(pair[::-1] if back else pair)
        return lax.ppermute(values, AXES, pairs)

    def flip(self, values, mask):
        pairs = [
            (dp * self.rank_size + rank, (dp ^ mask) * self.rank_size + rank)
            for dp in range(self.dp_size)
            for rank in range(self.rank_size)
        ]
        return lax.ppermute(values, AXES, pairs)

    def swap(self, values):
        return self.flip(values, 1)

    def flip_rank(self, values, bit):
        return self.by(values, lambda core, rank: (core, rank ^ 1 << bit))

    @staticmethod
    def even_target(core, rank):
        return (core, rank) if core == rank >> 1 else (rank >> 1, rank ^ 2)

    @staticmethod
    def odd_target(core, rank):
        return (core, rank ^ 1) if core == rank >> 1 else (rank >> 1, rank ^ 3)

    def even(self, values, back=False):
        return self.by(values, self.even_target, back)

    def odd(self, values, back=False):
        return self.by(values, self.odd_target, back)


def shards(
    tokens_in,
    token_mask,
    grid_index,
    time_table,
    cotangent,
    w_ada,
    b_ada,
    norm1,
    norm2,
    mask_vector,
    w_qkv,
    w_out,
    w_up,
    b_up,
    w_down,
    b_down,
):
    dp_size, ranks = lax.axis_size(DP), lax.axis_size("tensor")
    dp, rank = lax.axis_index(DP), lax.axis_index("tensor")
    core, quarter = dp & 1, dp >> 1 & 3
    parity = rank & 1
    moves = Moves(dp_size, ranks)
    _, row_count, width = tokens_in.shape
    shard_width = w_out.shape[0]
    hidden = w_up.shape[1]
    cond_width = time_table.shape[1]
    place_of = jnp.stack([quarter, core]).astype(jnp.int32)

    came_grid = moves.swap(grid_index)
    pair_grid = jnp.where(core == 0, jnp.concatenate([grid_index, came_grid]), jnp.concatenate([came_grid, grid_index]))
    here = lax.dynamic_index_in_dim(pair_grid, rank, 0, keepdims=False)
    cond_pre = lax.dynamic_slice(time_table, (here, 0), (1, cond_width))
    cond_low = jax.nn.silu(cond_pre).astype(bf16)
    ada_flat = w_ada.reshape(cond_width, 6 * width)
    modulation = jnp.dot(cond_low, ada_flat, preferred_element_type=f32).reshape(6, width) + b_ada

    starts = jnp.stack([(2 * side + (parity ^ odd)) * row_count for side in (core, 1 - core) for odd in range(2)])
    positions = starts[:, None] + jnp.arange(row_count, dtype=jnp.int32)[None, :]
    lane = jnp.arange(LANES, dtype=jnp.int32)
    half_dim = HEAD_DIM // 2
    frequency = 10000.0 ** (-(lane % half_dim).astype(f32) / half_dim)
    angles = positions.reshape(-1, 1).astype(f32) * frequency[None, :]
    cosine = jnp.cos(angles)
    sine = jnp.sin(angles) * jnp.where(lane % HEAD_DIM < half_dim, -1.0, 1.0)[None, :]

    def quarter_of(values, rows):
        return lax.dynamic_slice_in_dim(values, quarter * rows, rows, 0)

    def along(piece):
        return jnp.stack([moves.even(piece), moves.odd(piece)])

    def across(first, second, *before):
        first_x, second_y = together((moves.flip(first, 1 << 1), moves.flip(second, 2 << 1)), *before)
        one, two = jnp.stack([first, first_x]), jnp.stack([second, second_y])
        return one, two, moves.flip(one, 2 << 1), moves.flip(two, 1 << 1)

    def across_at_once(first, second):
        both = jnp.stack([first, second])
        return [both] + [moves.flip(both, turn << 1) for turn in (1, 2, 3)]

    qkv_rows = shard_width // 4
    qkv_slice = lax.dynamic_slice_in_dim(w_qkv, quarter * qkv_rows, qkv_rows, 2)
    qkv_piece = qkv_slice.transpose(1, 2, 0).reshape(3 * qkv_rows, width)
    attn_piece = jnp.concatenate([qkv_piece, quarter_of(w_out, qkv_rows)])
    up_piece, down_piece = quarter_of(w_up, width // 4), quarter_of(w_down, hidden // 4)
    odd_piece = jnp.concatenate([up_piece, down_piece])
    attn_even, attn_odd = moves.even(attn_piece), moves.odd(attn_piece)

    def sent(values, odd):
        return lax.dynamic_index_in_dim(values, parity ^ odd, 0, keepdims=False)

    mask_rows = jnp.pad(token_mask.astype(bf16), ((0, 0), (0, width - row_count)))[:, None]
    bias_rows = jnp.broadcast_to(split3(b_up)[None], (2, 3, width))
    rest = jnp.zeros((2, EXTRA - 4, width), bf16)
    packs = jnp.concatenate([after(tokens_in, came_grid, attn_piece), mask_rows, bias_rows, rest], axis=1)
    sent_even, sent_odd = sent(packs, 0), sent(packs, 1)
    cot_even, cot_odd = sent(cotangent, 0), sent(cotangent, 1)
    pack_even, pack_odd = moves.even(sent_even), moves.odd(sent_odd)
    attn_even, attn_odd = together(
        (attn_even, attn_odd), odd_piece, up_piece, cot_even, cot_odd, cosine, sine, modulation
    )
    attn_pieces = across(attn_even, attn_odd)
    odd_piece, up_piece = together((odd_piece, up_piece), pack_even, pack_odd)
    ffn_even, ffn_odd = moves.even(up_piece), moves.odd(odd_piece)
    cot_even, cot_odd = together((cot_even, cot_odd), ffn_even, ffn_odd)
    qkv_t, out_rows = place(
        attn_pieces,
        place_of,
        [
            ((shard, index * qkv_rows, qkv_rows), int(index == 3), (None if index == 3 else index, shard * shard_width, qkv_rows))
            for shard in range(2)
            for index in range(4)
        ],
        [like((3, 2 * shard_width, width), bf16), like((2 * shard_width, width), bf16)],
    )

    def bias_of(pack):
        return jnp.sum(pack[row_count + 1 : row_count + 4].astype(f32), axis=0, keepdims=True)

    table = jnp.concatenate(
        [
            modulation,
            norm1[None],
            norm2[None],
            mask_vector[None],
            b_down[None],
            bias_of(pack_even),
            bias_of(pack_odd),
            jnp.zeros((4, width), f32),
        ]
    )

    residual, first_own = enter(pack_even, pack_odd, table)
    first_other = moves.swap(after(first_own, attn_pieces[0], attn_pieces[1]))
    first_other = after(first_other, attn_pieces[2], attn_pieces[3], ffn_even, ffn_odd)
    cot_even, cot_odd, up_even, up_odd = together(
        (cot_even, cot_odd, ffn_even, ffn_odd[: width // 4]), first_other
    )
    cot_even, cot_odd = moves.even(cot_even), moves.odd(cot_odd)
    upstream = jnp.concatenate([cot_even, cot_odd])
    up_pieces = across_at_once(up_even, up_odd)
    queries, keys, values, mixed, log_sum, attn_own, attn_given = attend(
        first_own, first_other, qkv_t, out_rows, cosine, sine
    )
    down_quarter, down_shard = together((ffn_odd[width // 4 :], w_down), attn_own)
    attn_came = moves.swap(after(attn_given, cot_even, cot_odd, *up_pieces[1:]))
    down_even = moves.even(down_shard)
    down_pieces = [down_quarter] + [moves.flip(down_quarter, turn << 1) for turn in (1, 2, 3)]
    (up_full,) = place(
        up_pieces,
        place_of,
        [((shard, 0, width // 4), 0, (shard, 0, width // 4)) for shard in range(2)],
        [like((2, width, hidden), bf16)],
        steps=1,
    )
    attn_came = after(attn_came, *down_pieces[1:])
    second_res, second_own = second(residual, attn_own, attn_came, table)
    second_other = moves.swap(second_own)
    active_own, bend_own = upper(second_own, table, up_full)
    active_other, bend_other = upper(after(second_other, down_even, active_own), table, up_full)
    grad_mlp_own = (modulation[5:6] * upstream.astype(f32)).astype(bf16)
    grad_mlp_other = moves.swap(grad_mlp_own)

    def meet(pieces):
        return add([pieces[0]] + [moves.flip(pieces[turn], turn << 1) for turn in (1, 2, 3)], pieces[0].ndim == 3 and 2 or 1)

    def back(first, second):
        return [moves.even(first, back=True), moves.odd(second, back=True)]

    def share(mine):
        mine = mine + moves.swap(mine)
        for bit in range(3, dp_size.bit_length() - 1):
            mine = mine + moves.flip(mine, 1 << bit)
        return mine

    def spread(mine):
        low = mine.astype(bf16)
        axis = low.ndim - 2
        rows = low.shape[axis] // 2
        kept = lax.dynamic_slice_in_dim(low, core * rows, rows, axis)
        given = lax.dynamic_slice_in_dim(low, (1 - core) * rows, rows, axis)
        came = [moves.flip(kept, turn << 1) for turn in (1, 2, 3)]
        back = moves.swap(jnp.stack(came))
        return [kept, given, came[0], back[0], came[1], back[1], came[2], back[2]]

    d_down = ffn_weights(place_of, (active_own, active_other), (grad_mlp_own, grad_mlp_other), True, False)
    (down_odd,) = place(
        together(tuple(down_pieces), d_down[0]),
        place_of,
        [((0, 0, hidden // 4), 0, (None, 0, hidden // 4))],
        [like((hidden, width), bf16)],
        steps=0,
    )
    down_came = [moves.flip(d_down[turn], turn << 1) for turn in (1, 2, 3)]

    grad_mlp_late = after(grad_mlp_other, d_down[0])
    upper_grad_other, *part_given, sum_other = ffn_back(grad_mlp_late, down_even, down_odd, up_full, bend_other)
    part_came = [moves.swap(p) for p in part_given]
    upper_grad_own, *part_own, sum_own = ffn_back(
        after(grad_mlp_own, *part_given, down_came[0], down_came[1]), down_even, down_odd, up_full, bend_own
    )
    grad_res, grad_attn_own, sum_middle = middle(
        part_own, part_came, upstream, second_res, attn_own, attn_came, table
    )
    grad_attn_other = moves.swap(grad_attn_own)
    d_up = ffn_weights(
        place_of, (second_own, second_other), (upper_grad_own, after(upper_grad_other, grad_attn_own)), False, False
    )
    down_came = together(tuple(down_came), d_up[0])
    mlp_given = lower(after(active_other, *down_came), down_even, down_odd)
    mlp_came = moves.swap(mlp_given)
    mlp_own = lower(after(active_own, mlp_given), down_even, down_odd)
    down_parts = add([d_down[0], *down_came], 2)
    layer_even, layer_odd, sum_leave = leave(second_res, mlp_own, mlp_came, upstream, down_parts, table)

    def to_ranks(even, odd):
        return jnp.where(parity == 0, jnp.stack([even, odd]), jnp.stack([odd, even]))

    d_up = together(tuple(d_up), layer_even)
    up_came = [moves.flip(d_up[turn], turn << 1) for turn in (1, 2, 3)]
    layer_back = back(layer_even, layer_odd)
    d_first, found, rest, finish_back = attend_back(
        place_of,
        after(grad_attn_own, layer_even),
        grad_attn_other,
        first_own,
        first_other,
        qkv_t,
        out_rows,
        cosine,
        sine,
        queries,
        keys,
        values,
        mixed,
        log_sum,
    )
    up_came = together(tuple(up_came), found)
    d_first = together(tuple(d_first), found, *up_came)
    up_parts = add([d_up[0], *up_came], 2)
    first_came = [moves.flip(d_first[turn], turn << 1) for turn in (1, 2, 3)]
    found, rest = together((found, rest), *up_parts)
    d_second, last, first_grads = finish_back(found, rest)
    d_second = together(tuple(d_second), *first_came, *layer_back)
    layer_back = together(tuple(layer_back), last)
    up_back = back(*together(tuple(up_parts), *layer_back))
    first_parts = add([d_first[0], *first_came])
    second_came = [moves.flip(d_second[turn], turn << 1) for turn in (1, 2, 3)]
    first_part, first_given = first_grads(after(last, d_second[0]))
    first_came = moves.swap(after(first_given, *second_came, *up_back))
    second_parts = add([d_second[0]] + second_came)
    attn_back = back(first_parts, second_parts)
    in_even, in_odd, sum_end = end(first_part, first_came, residual, pack_even, pack_odd, grad_res, table)
    layer_back = together(tuple(layer_back), sum_end)
    layer_out = to_ranks(*[p[:row_count] for p in layer_back])
    ffn_part = share(
        jnp.concatenate(
            [add([p[row_count:] for p in layer_back], dtype=f32), add(together(tuple(up_back), sum_end), dtype=f32)]
        )
    )
    attn_part = share(add(together(tuple(attn_back), sum_end), dtype=f32))
    ffn_spread = spread(ffn_part.reshape(2, -1, width))
    grad_w_down = finish([p[0] for p in ffn_spread], place_of, (hidden, width))
    grad_w_up = finish([p[1] for p in ffn_spread], place_of, (width, hidden))
    grad_attn_rows = finish(spread(attn_part), place_of, (4 * shard_width, width)).reshape(4, 4, qkv_rows, width)
    grad_w_out = grad_attn_rows[:, 3].reshape(shard_width, width)
    grad_w_qkv = grad_attn_rows[:, :3].transpose(3, 1, 0, 2).reshape(width, 3, shard_width)

    scale_up = 1.0 + modulation
    upper_two = (sum_own[0] + sum_other[0]).reshape(2, hidden)
    upper_two = jnp.where(parity == 1, upper_two[::-1], upper_two)
    blank = jnp.zeros((2, hidden), f32)
    cond_row = jnp.pad(jnp.concatenate([cond_pre[0], here.astype(f32)[None]]), (0, width - cond_width - 1))
    cond_row = jnp.where(core == 0, cond_row, 0.0)
    rows = jnp.concatenate(
        [
            jnp.stack(
                [
                    sum_end[0],
                    sum_end[1] * norm1,
                    sum_middle[2],
                    sum_middle[0],
                    sum_middle[1] * norm2,
                    sum_leave[0],
                    cond_row,
                    sum_end[1] * scale_up[1],
                    sum_end[2],
                    sum_middle[1] * scale_up[4],
                    sum_leave[1],
                ]
            ),
            jnp.where(core == 0, upper_two, blank),
            jnp.where(core == 0, blank, upper_two),
        ]
    )
    rows = rows + moves.swap(rows)
    each, sums = rows[:7], rows[7:]
    steps = [(moves.flip, 1 << bit, dp >> bit & 1) for bit in range(1, dp_size.bit_length() - 1)]
    steps += [(moves.flip_rank, bit, rank >> bit & 1) for bit in range(ranks.bit_length() - 1)]
    for move, which, ahead in steps:
        came = move(jnp.concatenate([each, sums]), which)
        sums = sums + came[each.shape[0] :]
        came = came[: each.shape[0]]
        each = jnp.where(ahead == 1, jnp.concatenate([came, each]), jnp.concatenate([each, came]))
        if move == moves.flip_rank and which == 0:
            grad_in = to_ranks(*back(*together((in_even, in_odd), came)))
    each, sums = together((each, sums), attn_part)
    each = each.reshape(-1, 7, width)
    grad_mods = each[:, :6]
    cond_all = each[:, 6, :cond_width]
    grid_all = each[:, 6, cond_width].astype(jnp.int32)
    grad_b_up = lax.dynamic_index_in_dim(sums[4:], rank, 0, keepdims=False)

    points = time_table.shape[0]
    onehot = (grid_all[:, None] == jnp.arange(points, dtype=jnp.int32)[None, :]).astype(f32)
    cond_act, silu_back = jax.vjp(jax.nn.silu, cond_all)
    cond_act = cond_act.astype(bf16).astype(f32)
    grad_flat = grad_mods.reshape(-1, 6 * width)
    grad_w_ada = jnp.dot(cond_act.T, grad_flat, precision=highest).reshape(cond_width, 6, width)
    grad_b_ada = jnp.sum(grad_mods, axis=0)
    grad_cond = jnp.dot(grad_flat, ada_flat.astype(f32).T, precision=highest)
    grad_pre = silu_back(grad_cond)[0]
    grad_table = jnp.dot(onehot.T, grad_pre, precision=highest)
    return (
        layer_out,
        grad_in,
        grad_table,
        sums[1],
        grad_w_ada,
        grad_b_ada,
        sums[0],
        sums[2],
        grad_w_qkv,
        grad_w_out,
        grad_w_up,
        grad_b_up,
        grad_w_down,
        sums[3],
    )


def solution(mesh):
    parts = (mesh.shape["dp"] // 8, 2, 2, 2, mesh.shape["tensor"])
    finer = jax.sharding.Mesh(mesh.devices.reshape(parts), AXES)
    whole = P()
    split = P(DP, "tensor", None)
    weights = (P(None, None, "tensor"), P("tensor", None), P(None, "tensor"), P("tensor"), P("tensor", None), whole)
    return jax.shard_map(
        shards,
        mesh=finer,
        in_specs=(split, P(DP, "tensor"), P(DP), whole, split) + (whole,) * 5 + weights,
        out_specs=(split, split) + (whole,) * 6 + weights,
        check_vma=False,
    )
```

```python
import functools

import jax
import jax.numpy as jnp
from jax import lax
from jax.experimental import pallas as pl
from jax.experimental.pallas import tpu as pltpu
from jax.sharding import PartitionSpec as P

HEAD_DIM = 64
LANES = 128
EXTRA = 16
f32 = jnp.float32
bf16 = jnp.bfloat16
highest = lax.Precision.HIGHEST
NN = (((1,), (0,)), ((), ()))
NT = (((1,), (1,)), ((), ()))
TN = (((0,), (0,)), ((), ()))
DP = ("r", "y", "x", "c")
AXES = DP + ("tensor",)
MIB = 2**20
SHARE = 64

SHIFT1, SCALE1, GATE1, SHIFT2, SCALE2, GATE2, NORM1, NORM2, MASKED, B_DOWN, B_UP = range(11)


def dot(left, right, dims=NN):
    return lax.dot_general(left, right, dims, preferred_element_type=f32)


def row(table, index):
    return table[index : index + 1, :]


def full(shape):
    return pl.BlockSpec(shape, lambda *i: (0,) * len(shape))


def by_rows(size, width):
    return pl.BlockSpec((size, width), lambda i: (i, 0))


def like(shape, dtype):
    return jax.ShapeDtypeStruct(shape, dtype)


def call(body, grid, ins, specs, outs, out_specs, scratch=(), mib=24, flops=0, special=0, name=None):
    moved = sum(x.size * x.dtype.itemsize for x in ins) + sum(x.size * x.dtype.itemsize for x in outs)
    return pl.pallas_call(
        body,
        grid=(grid,),
        in_specs=specs,
        out_specs=out_specs,
        out_shape=outs,
        scratch_shapes=list(scratch),
        name=name,
        compiler_params=pltpu.CompilerParams(vmem_limit_bytes=mib * MIB),
        cost_estimate=pl.CostEstimate(flops=flops // SHARE, bytes_accessed=moved // SHARE, transcendentals=special // SHARE),
    )(*ins)


def centered(values):
    average = jnp.mean(values, axis=-1, keepdims=True)
    away = values - average
    inverse = lax.rsqrt(jnp.mean(away * away, axis=-1, keepdims=True) + 1e-05)
    return away * inverse, inverse


def norm_back(grads, hat, inverse, factor):
    slope = grads * factor
    lean = jnp.mean(slope, axis=-1, keepdims=True)
    tilt = jnp.mean(slope * hat, axis=-1, keepdims=True)
    return (slope - lean - hat * tilt) * inverse


def after(values, *others):
    return lax.optimization_barrier((values,) + others)[0]


def together(values, *others):
    return lax.optimization_barrier(values + others)[: len(values)]


def over_rows(values):
    return jnp.sum(values, axis=0, keepdims=True)


def mask_column(extra):
    count = extra.shape[1] // LANES * LANES
    line = extra[0:1, :].astype(f32)
    return jnp.broadcast_to(line, (LANES, count)).T[:, 0:1]


def place_kernel(plan, steps, place_of, *refs):
    (one, two, first_y, second_x), outs = refs[:4], refs[4:]
    if steps == 0:
        shards_of = (tuple((piece, None) for piece in refs[:4]),)
    elif steps == 1:
        shards_of = tuple(tuple((piece, shard) for piece in refs[:4]) for shard in range(2))
    else:
        shards_of = (((one, 0), (one, 1), (first_y, 0), (first_y, 1)), ((two, 0), (second_x, 0), (two, 1), (second_x, 1)))
    for turn in range(4):
        here = place_of[0] ^ turn
        for (shard, start, size), out, (lead, base, pitch) in plan:
            piece, index = shards_of[shard][turn]
            rows = pl.ds(pl.multiple_of(base + here * pitch, 16), size)
            where = (rows, slice(None)) if lead is None else (lead, rows, slice(None))
            rows_of = slice(start, start + size)
            outs[out][where] = piece[rows_of, :] if index is None else piece[index, rows_of, :]


def place(pieces, place_of, plan, outs, steps=2):
    moved = sum(2 * x.size * x.dtype.itemsize for x in outs)
    return pl.pallas_call(
        functools.partial(place_kernel, plan, steps),
        in_specs=[pl.BlockSpec(memory_space=pltpu.SMEM)] + [pl.BlockSpec(memory_space=pltpu.VMEM)] * 4,
        out_specs=[pl.BlockSpec(memory_space=pltpu.VMEM)] * len(outs),
        out_shape=outs,
        name="place",
        compiler_params=pltpu.CompilerParams(vmem_limit_bytes=12 * MIB),
        cost_estimate=pl.CostEstimate(flops=0, bytes_accessed=moved // SHARE, transcendentals=0),
    )(place_of, *pieces)


def finish_kernel(plan, place_of, *refs):
    pieces, outs = refs[:8], refs[8:]
    quarter, core = place_of[0], place_of[1]
    for turn in range(4):
        here = quarter ^ turn
        for side in range(2):
            which = core ^ side
            piece = pieces[2 * turn + side]
            for out, size, pitch in plan:
                rows = pl.ds(pl.multiple_of(here * pitch + which * size, 8), size)
                outs[out][rows, :] = piece[...].astype(f32)


def finish(pieces, place_of, shape):
    half = pieces[0].shape[0]
    return pl.pallas_call(
        functools.partial(finish_kernel, ((0, half, 2 * half),)),
        in_specs=[pl.BlockSpec(memory_space=pltpu.SMEM)] + [pl.BlockSpec(memory_space=pltpu.VMEM)] * 8,
        out_specs=[pl.BlockSpec(memory_space=pltpu.VMEM)],
        out_shape=[like(shape, f32)],
        name="finish",
        compiler_params=pltpu.CompilerParams(vmem_limit_bytes=16 * MIB),
        cost_estimate=pl.CostEstimate(flops=0, bytes_accessed=6 * shape[0] * shape[1] // SHARE, transcendentals=0),
    )(place_of, *pieces)[0]


def enter_kernel(even, odd, table, residual, first):
    rows = even.shape[0] - EXTRA
    for index, pack in enumerate((even, odd)):
        here = slice(index * rows, (index + 1) * rows)
        mask = mask_column(pack[rows:, :rows])
        values = pack[:rows, :].astype(f32) + mask * row(table, MASKED)
        residual[here, :] = values
        hat, _ = centered(values)
        factor = row(table, NORM1) * (1.0 + row(table, SCALE1))
        first[here, :] = (hat * factor + row(table, SHIFT1)).astype(bf16)


def enter(even, odd, table):
    rows, width = 2 * (even.shape[0] - EXTRA), even.shape[1]
    return call(
        enter_kernel,
        1,
        (even, odd, table),
        [full(even.shape), full(odd.shape), full(table.shape)],
        [like((rows, width), f32), like((rows, width), bf16)],
        [full((rows, width))] * 2,
        name="enter",
    )


def partner(values):
    lane = lax.broadcasted_iota(jnp.int32, values.shape, 1)
    ahead = pltpu.roll(values, LANES - HEAD_DIM // 2, 1)
    behind = pltpu.roll(values, HEAD_DIM // 2, 1)
    return jnp.where(lane % HEAD_DIM < HEAD_DIM // 2, ahead, behind)


def heads_of(values):
    lane = lax.broadcasted_iota(jnp.int32, values.shape, 1)
    return lane < HEAD_DIM


def attend_kernel(
    own, other, weights, w_out, cosine, sine, queries, keys, values, mixed, log_sum, part_own, part_other, total
):
    step = pl.program_id(0)
    half = own.shape[0]
    length = 2 * half
    chunk = 256
    for index, tokens in enumerate((own, other)):
        here = slice(index * half, (index + 1) * half)
        query = dot(tokens[...], weights[0], NT)
        turned = (query * cosine[here, :] + partner(query) * sine[here, :]).astype(bf16)
        queries[here, :] = (turned * HEAD_DIM**-0.5).astype(bf16)
        key = dot(tokens[...], weights[1], NT)
        keys[here, :] = (key * cosine[here, :] + partner(key) * sine[here, :]).astype(bf16)
        values[here, :] = dot(tokens[...], weights[2], NT).astype(bf16)

    @pl.when(step == 0)
    def _():
        total[...] = jnp.zeros_like(total)

    every_key, every_value = keys[...], values[...]
    items = [(start, head) for start in range(0, length, chunk) for head in range(2)]

    def score(start, head):
        block = queries[pl.ds(start, chunk), :]
        former = heads_of(block)
        return dot(jnp.where(former if head == 0 else ~former, block, 0), every_key, NT)

    following = score(*items[0])
    halves = []
    for index, (start, head) in enumerate(items):
        scores = following
        if index + 1 < len(items):
            following = score(*items[index + 1])
        top = jnp.max(scores, axis=1, keepdims=True)
        powers = jnp.exp(scores - top)
        sums = jnp.sum(powers, axis=1, keepdims=True)
        halves.append((dot(powers.astype(bf16), every_value) * (1.0 / sums), top + jnp.log(sums)))
        if head == 1:
            here = pl.ds(start, chunk)
            former = heads_of(halves[0][0])
            out = jnp.where(former, halves[0][0], halves[1][0])
            mixed[here, :] = out
            log_sum[here, :] = jnp.where(former, halves[0][1], halves[1][1])
            total[here, :] += dot(out.astype(bf16), w_out[...])
            halves = []

    @pl.when(step == pl.num_programs(0) - 1)
    def _():
        part_own[...] = total[:half, :].astype(bf16)
        part_other[...] = total[half:, :].astype(bf16)


def attend(own, other, weights, w_out, cosine, sine):
    half, width = own.shape
    length = 2 * half
    wide = w_out.shape[0]
    tall = pl.BlockSpec((length, LANES), lambda i: (0, i))
    return call(
        attend_kernel,
        wide // LANES,
        (own, other, weights, w_out, cosine, sine),
        [
            full(own.shape),
            full(own.shape),
            pl.BlockSpec((3, LANES, width), lambda i: (0, i, 0)),
            pl.BlockSpec((LANES, width), lambda i: (i, 0)),
            full(cosine.shape),
            full(sine.shape),
        ],
        [like((length, wide), bf16)] * 3 + [like((length, wide), f32)] * 2 + [like((half, width), bf16)] * 2,
        [tall] * 5 + [full((half, width))] * 2,
        [pltpu.VMEM((length, width), f32)],
        mib=36,
        flops=8 * length * width * wide + 16 * length * length * wide,
        special=length * length * wide // HEAD_DIM,
        name="attend",
    )


def pair_back(grads_own, grads_other, own, other, w_out, cosine, sine, queries, keys, values, mixed, log_sum):
    half = own.shape[0]
    length = 2 * half
    chunk = 256
    outs = mixed[...]
    low = outs.astype(bf16)
    grad = jnp.concatenate([dot(grads_own[...], w_out[...], NT), dot(grads_other[...], w_out[...], NT)]).astype(bf16)
    d_out = dot(low[:half], grads_own[...], TN) + dot(low[half:], grads_other[...], TN)
    lean_t = (grad.astype(f32) * outs).T
    log_t = log_sum[...].T
    query, key, value = queries[...], keys[...], values[...]
    former = heads_of(query)
    former_chunk = heads_of(query[:chunk])
    items = [(head, start) for head in range(2) for start in range(0, length, chunk)]

    def products(head, start):
        mine = former_chunk if head == 0 else ~former_chunk
        key_rows = jnp.where(mine, key[start : start + chunk], 0)
        value_rows = jnp.where(mine, value[start : start + chunk], 0)
        return dot(key_rows, query, NT), dot(value_rows, grad, NT)

    found_q, found_k, found_v = [None, None], ([], []), ([], [])

    def collect(head, start, probs, slopes):
        found_v[head].append(dot(probs, grad))
        found_k[head].append(dot(slopes, query))
        more = dot(key[start : start + chunk], slopes, TN)
        found_q[head] = more if found_q[head] is None else found_q[head] + more

    following, pending = products(*items[0]), None
    for index, (head, start) in enumerate(items):
        scores, against = following
        if index + 1 < len(items):
            following = products(*items[index + 1])
        if pending is not None:
            collect(*pending)
        lean = over_rows(lean_t[head * HEAD_DIM : (head + 1) * HEAD_DIM])
        probs = jnp.exp(scores - log_t[head * HEAD_DIM : head * HEAD_DIM + 1])
        pending = (head, start, probs.astype(bf16), (probs * (against - lean)).astype(bf16))
    collect(*pending)
    row_head = lax.broadcasted_iota(jnp.int32, found_q[0].shape, 0)
    d_query = jnp.where(row_head < HEAD_DIM, found_q[0], found_q[1]).T * HEAD_DIM**-0.5
    d_key = jnp.where(former, jnp.concatenate(found_k[0]), jnp.concatenate(found_k[1]))
    d_value = jnp.where(former, jnp.concatenate(found_v[0]), jnp.concatenate(found_v[1])).astype(bf16)
    d_query = (d_query * cosine[...] + partner(d_query * sine[...])).astype(bf16)
    d_key = (d_key * cosine[...] + partner(d_key * sine[...])).astype(bf16)
    found = (d_query, d_key, d_value)
    return found, [dot(g[:half], own[...], TN) + dot(g[half:], other[...], TN) for g in found] + [d_out]


def put_pieces(pieces, rows_of_weight, quarter, size):
    for turn, piece in enumerate(pieces):
        rows = pl.ds(pl.multiple_of((quarter ^ turn) * size, 16), size)
        for index in range(4):
            piece[index * size : (index + 1) * size, :] = rows_of_weight[index, rows, :]


def attend_back_kernel(shard_rows, place_of, *refs):
    ins, (found_all, *pieces), rest, d_weights = refs[:12], refs[12:17], refs[17], refs[18]
    step = pl.program_id(0)
    found, rows = pair_back(*ins)
    here = pl.ds(pl.multiple_of(step * LANES, LANES), LANES)
    for index in range(3):
        found_all[index] = found[index]
    for index in range(4):
        d_weights[index, here, :] = rows[index].astype(bf16)

    @pl.when(step == pl.num_programs(0) - 1)
    def _():
        put_pieces(pieces, d_weights, place_of[0], shard_rows // 4)
        rest[...] = d_weights[:, shard_rows:, :]


def attend_back_end_kernel(shard_rows, place_of, rows_before, *refs):
    ins, (found_all, *pieces), d_weights = refs[:12], refs[12:17], refs[17]
    found, rows = pair_back(*ins)
    start = rows_before.shape[1]
    d_weights[:, :start, :] = rows_before[...]
    for index in range(3):
        found_all[index] = found[index]
    for index in range(4):
        d_weights[index, start:, :] = rows[index].astype(bf16)
    put_pieces(pieces, d_weights, place_of[0], shard_rows // 4)


def first_grads_kernel(before, last, weights, part_own, part_other):
    half, wide = part_own.shape[0], before.shape[2]
    for out, here in ((part_other, slice(half, None)), (part_own, slice(0, half))):
        total = dot(last[0, here, :], weights[0, wide:, :])
        total += dot(last[1, here, :], weights[1, wide:, :]) + dot(last[2, here, :], weights[2, wide:, :])
        for index in range(3):
            total += dot(before[index, here, :], weights[index, :wide, :])
        out[...] = total.astype(bf16)


def attend_back(place_of, grads_own, grads_other, own, other, weights, w_out, cosine, sine, *kept):
    half, width = own.shape
    length = 2 * half
    wide = w_out.shape[0]
    shard_rows = wide // 2
    first = -(-shard_rows // LANES)
    rows = full((half, width))
    quarter = like((shard_rows, width), bf16)
    smem = pl.BlockSpec(memory_space=pltpu.SMEM)

    def specs(base):
        tall = pl.BlockSpec((length, LANES), lambda i: (0, i + base))
        flat = pl.BlockSpec((LANES, width), lambda i: (i + base, 0))
        return [rows] * 4 + [flat, full(cosine.shape), full(sine.shape)] + [tall] * 5

    ins = (grads_own, grads_other, own, other, w_out, cosine, sine) + kept
    work = dict(flops=14 * length * width * LANES + 40 * length * length * LANES, special=2 * length * length)
    found, *pieces, rest = call(
        functools.partial(attend_back_kernel, shard_rows),
        first,
        (place_of,) + ins,
        [smem] + specs(0),
        [like((3, length, first * LANES), bf16)] + [quarter] * 4 + [like((4, first * LANES - shard_rows, width), bf16)],
        [pl.BlockSpec((3, length, LANES), lambda i: (0, 0, i))]
        + [full(quarter.shape)] * 4
        + [full((4, first * LANES - shard_rows, width))],
        [pltpu.VMEM((4, first * LANES, width), bf16)],
        mib=60,
        name="attend_back",
        **work,
    )

    def finish_back(found, rest):
        last, *more = call(
            functools.partial(attend_back_end_kernel, shard_rows),
            1,
            (place_of, rest) + ins,
            [smem, full(rest.shape)] + specs(first),
            [like((3, length, LANES), bf16)] + [quarter] * 4,
            [full((3, length, LANES))] + [full(quarter.shape)] * 4,
            [pltpu.VMEM((4, shard_rows, width), bf16)],
            mib=60,
            name="attend_back_end",
            **work,
        )

        def first_grads(last):
            return call(
                first_grads_kernel,
                1,
                (found, last, weights),
                [full(found.shape), full(last.shape), full(weights.shape)],
                [like((half, width), bf16)] * 2,
                [rows] * 2,
                mib=60,
        name="first_grads",
            )

        return more, last, first_grads

    return pieces, found, rest, finish_back


def lift(inner, table, w_up, active, bend):
    hidden = w_up.shape[2]
    root = 0.7978845608028654
    for block in range(2):
        span = slice(block * hidden, (block + 1) * hidden)
        u = dot(inner, w_up[block]) + table[B_UP + block : B_UP + block + 1, :hidden]
        square = u * u
        curve = jnp.tanh(root * (u + 0.044715 * (square * u)))
        rise = 0.5 + 0.5 * curve
        active[:, span] = (u * rise).astype(bf16)
        slope = rise + (0.5 * root) * u * (1.0 - curve * curve) * (1.0 + 0.134145 * square)
        bend[:, span] = slope.astype(bf16)


def second_kernel(residual, mine, came, table, second_res, second):
    values = residual[...] + row(table, GATE1) * (mine[...].astype(f32) + came[...].astype(f32))
    second_res[...] = values
    hat, _ = centered(values)
    factor = row(table, NORM2) * (1.0 + row(table, SCALE2))
    second[...] = (hat * factor + row(table, SHIFT2)).astype(bf16)


def second(residual, mine, came, table, size=256):
    rows, width = residual.shape
    spec = by_rows(size, width)
    return call(
        second_kernel,
        rows // size,
        (residual, mine, came, table),
        [spec, spec, spec, full(table.shape)],
        [like((rows, width), f32), like((rows, width), bf16)],
        [spec, spec],
        flops=10 * rows * width,
        name="second",
    )


def upper_kernel(inner, table, w_up, active, bend):
    lift(inner[...], table, w_up, active, bend)


def upper(inner, table, w_up, size=256):
    rows, width = inner.shape
    hidden = 2 * w_up.shape[2]
    broad = by_rows(size, hidden)
    return call(
        upper_kernel,
        rows // size,
        (inner, table, w_up),
        [by_rows(size, width), full(table.shape), full(w_up.shape)],
        [like((rows, hidden), bf16)] * 2,
        [broad, broad],
        flops=2 * rows * width * hidden,
        special=rows * hidden,
        name="upper",
    )


def ffn_back_kernel(grad_mlp, down_even, down_odd, w_up, bend, grad_upper, *refs):
    parts, sums = refs[:-1], refs[-1]
    step = pl.program_id(0)
    grad = jnp.concatenate([dot(grad_mlp[...], down[...], NT) for down in (down_even, down_odd)], axis=1)
    grad = (grad * bend[...].astype(f32)).astype(bf16)
    grad_upper[...] = grad
    hidden = w_up.shape[2]
    result = (dot(grad[:, :hidden], w_up[0], NT) + dot(grad[:, hidden:], w_up[1], NT)).astype(bf16)
    for index, part in enumerate(parts):

        @pl.when(step == index)
        def _(part=part):
            part[...] = result

    @pl.when(step == 0)
    def _():
        sums[...] = jnp.zeros_like(sums)

    sums[0:1, :] += over_rows(grad.astype(f32))


def ffn_back(grad_mlp, down_even, down_odd, w_up, bend, size=256):
    rows, width = grad_mlp.shape
    hidden = 2 * down_even.shape[0]
    spec, broad = by_rows(size, width), by_rows(size, hidden)
    return call(
        ffn_back_kernel,
        rows // size,
        (grad_mlp, down_even, down_odd, w_up, bend),
        [spec, full(down_even.shape), full(down_odd.shape), full(w_up.shape), broad],
        [like((rows, hidden), bf16)] + [like((size, width), bf16)] * (rows // size) + [like((8, hidden), f32)],
        [broad] + [full((size, width))] * (rows // size) + [full((8, hidden))],
        flops=4 * rows * width * hidden,
        name="ffn_back",
    )


def ffn_weights_kernel(place_of, left_own, left_other, right_own, right_other, *refs):
    pieces, whole = refs[:-1], refs[-1]
    whole[...] = (dot(left_own[...], right_own[...], TN) + dot(left_other[...], right_other[...], TN)).astype(bf16)
    size = whole.shape[0] // 4
    if len(pieces) == 1:
        for index in range(4):
            pieces[0][index, 0] = whole[index * size : (index + 1) * size, :]
        return
    for turn, piece in enumerate(pieces):
        rows = pl.ds(pl.multiple_of((place_of[0] ^ turn) * size, 16), size)
        piece[0] = whole[rows, :]


def ffn_weights(place_of, left, right, split_left, ordered):
    rows, width = right[0].shape if split_left else left[0].shape
    hidden = (left if split_left else right)[0].shape[1] // 2
    whole, halved = full((rows, width)), pl.BlockSpec((rows, hidden), lambda i: (0, i))
    lefts, rights = (halved, whole) if split_left else (whole, halved)
    shape = (hidden, width) if split_left else (width, hidden)
    size = shape[0] // 4
    if ordered:
        outs, specs = [(4, 2, size, shape[1])], [pl.BlockSpec((4, 1, size, shape[1]), lambda i: (0, i, 0, 0))]
    else:
        outs, specs = [(2, size, shape[1])] * 4, [pl.BlockSpec((1, size, shape[1]), lambda i: (i, 0, 0))] * 4
    return call(
        ffn_weights_kernel,
        2,
        (place_of,) + tuple(left) + tuple(right),
        [pl.BlockSpec(memory_space=pltpu.SMEM), lefts, lefts, rights, rights],
        [like(out, bf16) for out in outs],
        specs,
        [pltpu.VMEM(shape, bf16)],
        flops=8 * rows * width * hidden,
        name="ffn_weights",
    )


def sum_kernel(count, *refs):
    pieces, outs = refs[:count], refs[count:]
    for index, out in enumerate(outs):
        values = [p[...] if len(p.shape) == 2 else p[index] for p in pieces]
        out[...] = sum(v.astype(f32) for v in values).astype(out.dtype)


def add(pieces, count=1, dtype=bf16):
    shape = pieces[0].shape[-2:]
    result = pl.pallas_call(
        functools.partial(sum_kernel, len(pieces)),
        in_specs=[pl.BlockSpec(memory_space=pltpu.VMEM)] * len(pieces),
        out_specs=[pl.BlockSpec(memory_space=pltpu.VMEM)] * count,
        out_shape=[like(shape, dtype)] * count,
        name="add",
        compiler_params=pltpu.CompilerParams(vmem_limit_bytes=12 * MIB),
    )(*pieces)
    return result if count > 1 else result[0]


def middle_kernel(parts, *refs):
    mine, came = refs[:parts], refs[parts : 2 * parts]
    upstream, second_res, attn_mine, attn_came, table, grad_res, grad_attn, sums = refs[2 * parts :]
    step = pl.program_id(0)
    grad = mine[0][...].astype(f32) + came[0][...].astype(f32)
    for index in range(1, parts):
        grad = jnp.where(step == index, mine[index][...].astype(f32) + came[index][...].astype(f32), grad)
    hat, inverse = centered(second_res[...])
    factor = row(table, NORM2) * (1.0 + row(table, SCALE2))
    result = upstream[...].astype(f32) + norm_back(grad, hat, inverse, factor)
    grad_res[...] = result
    grad_attn[...] = (row(table, GATE1) * result).astype(bf16)

    @pl.when(step == 0)
    def _():
        sums[...] = jnp.zeros_like(sums)

    attn = attn_mine[...].astype(f32) + attn_came[...].astype(f32)
    sums[0:1, :] += over_rows(grad)
    sums[1:2, :] += over_rows(grad * hat)
    sums[2:3, :] += over_rows(result * attn)


def middle(mine, came, upstream, second_res, attn_mine, attn_came, table, size=256):
    rows, width = upstream.shape
    spec = by_rows(size, width)
    return call(
        functools.partial(middle_kernel, len(mine)),
        rows // size,
        (*mine, *came, upstream, second_res, attn_mine, attn_came, table),
        [full((size, width))] * (2 * len(mine)) + [spec] * 4 + [full(table.shape)],
        [like((rows, width), f32), like((rows, width), bf16), like((8, width), f32)],
        [spec, spec, full((8, width))],
        flops=40 * rows * width,
        name="middle",
    )


def lower_kernel(active, down_even, down_odd, part):
    half = down_even.shape[0]
    part[...] = (dot(active[:, :half], down_even[...]) + dot(active[:, half:], down_odd[...])).astype(bf16)


def lower(active, down_even, down_odd, size=256):
    rows, hidden = active.shape
    width = down_even.shape[1]
    return call(
        lower_kernel,
        rows // size,
        (active, down_even, down_odd),
        [by_rows(size, hidden), full(down_even.shape), full(down_odd.shape)],
        [like((rows, width), bf16)],
        [by_rows(size, width)],
        flops=2 * rows * hidden * width,
        name="lower",
    )[0]


def leave_kernel(second_res, mine, came, upstream, part_even, part_odd, table, even, odd, sums):
    mlp = mine[...].astype(f32) + came[...].astype(f32) + row(table, B_DOWN)
    layer = (second_res[...] + row(table, GATE2) * mlp).astype(bf16)
    rows = layer.shape[0] // 2
    even[:rows, :] = layer[:rows]
    odd[:rows, :] = layer[rows:]
    even[rows:, :] = part_even[...]
    odd[rows:, :] = part_odd[...]
    grads = upstream[...].astype(f32)
    sums[...] = jnp.zeros_like(sums)
    sums[0:1, :] = over_rows(grads * mlp)
    sums[1:2, :] = over_rows((row(table, GATE2) * grads).astype(bf16).astype(f32))


def leave(second_res, mine, came, upstream, parts, table):
    rows, width = upstream.shape
    spec, part = full((rows, width)), full(parts[0].shape)
    out = (rows // 2 + parts[0].shape[0], width)
    return call(
        leave_kernel,
        1,
        (second_res, mine, came, upstream, *parts, table),
        [spec] * 4 + [part] * 2 + [full(table.shape)],
        [like(out, bf16)] * 2 + [like((8, width), f32)],
        [full(out)] * 2 + [full((8, width))],
        flops=6 * rows * width,
        name="leave",
    )


def end_kernel(mine, came, residual, pack_even, pack_odd, grad_res, table, even, odd, sums):
    rows = even.shape[0]
    factor = row(table, NORM1) * (1.0 + row(table, SCALE1))
    sums[...] = jnp.zeros_like(sums)
    for index, (out, pack) in enumerate(((even, pack_even), (odd, pack_odd))):
        here = slice(index * rows, (index + 1) * rows)
        grad = mine[here, :].astype(f32) + came[here, :].astype(f32)
        hat, inverse = centered(residual[here, :])
        result = grad_res[here, :] + norm_back(grad, hat, inverse, factor)
        out[...] = result.astype(bf16)
        sums[0:1, :] += over_rows(grad)
        sums[1:2, :] += over_rows(grad * hat)
        sums[2:3, :] += over_rows(result * mask_column(pack[:, :rows]))


def end(mine, came, residual, pack_even, pack_odd, grad_res, table):
    rows, width = mine.shape
    spec = full((rows, width))
    extra = pl.BlockSpec((EXTRA, width), lambda i: (rows // 2 // EXTRA, 0))
    return call(
        end_kernel,
        1,
        (mine, came, residual, pack_even, pack_odd, grad_res, table),
        [spec, spec, spec, extra, extra, spec, full(table.shape)],
        [like((rows // 2, width), bf16)] * 2 + [like((8, width), f32)],
        [full((rows // 2, width))] * 2 + [full((8, width))],
        flops=30 * rows * width,
        mib=60,
        name="end",
    )


def split3(values):
    high = lax.reduce_precision(values, 8, 7)
    rest = values - high
    middle_term = lax.reduce_precision(rest, 8, 7)
    return jnp.stack([high, middle_term, rest - middle_term]).astype(bf16)


class Moves:
    def __init__(self, dp_size, rank_size):
        self.dp_size, self.rank_size = dp_size, rank_size

    def by(self, values, target, back=False):
        pairs = []
        for dp in range(self.dp_size):
            for rank in range(self.rank_size):
                core, to_rank = target(dp & 1, rank)
                pair = (dp * self.rank_size + rank, (dp >> 1 << 1 | core) * self.rank_size + to_rank)
                pairs.append(pair[::-1] if back else pair)
        return lax.ppermute(values, AXES, pairs)

    def flip(self, values, mask):
        pairs = [
            (dp * self.rank_size + rank, (dp ^ mask) * self.rank_size + rank)
            for dp in range(self.dp_size)
            for rank in range(self.rank_size)
        ]
        return lax.ppermute(values, AXES, pairs)

    def swap(self, values):
        return self.flip(values, 1)

    def flip_rank(self, values, bit):
        return self.by(values, lambda core, rank: (core, rank ^ 1 << bit))

    @staticmethod
    def even_target(core, rank):
        return (core, rank) if core == rank >> 1 else (rank >> 1, rank ^ 2)

    @staticmethod
    def odd_target(core, rank):
        return (core, rank ^ 1) if core == rank >> 1 else (rank >> 1, rank ^ 3)

    def even(self, values, back=False):
        return self.by(values, self.even_target, back)

    def odd(self, values, back=False):
        return self.by(values, self.odd_target, back)


def shards(
    tokens_in,
    token_mask,
    grid_index,
    time_table,
    cotangent,
    w_ada,
    b_ada,
    norm1,
    norm2,
    mask_vector,
    w_qkv,
    w_out,
    w_up,
    b_up,
    w_down,
    b_down,
):
    dp_size, ranks = lax.axis_size(DP), lax.axis_size("tensor")
    dp, rank = lax.axis_index(DP), lax.axis_index("tensor")
    core, quarter = dp & 1, dp >> 1 & 3
    parity = rank & 1
    moves = Moves(dp_size, ranks)
    _, row_count, width = tokens_in.shape
    shard_width = w_out.shape[0]
    hidden = w_up.shape[1]
    cond_width = time_table.shape[1]
    place_of = jnp.stack([quarter, core]).astype(jnp.int32)

    came_grid = moves.swap(grid_index)
    pair_grid = jnp.where(core == 0, jnp.concatenate([grid_index, came_grid]), jnp.concatenate([came_grid, grid_index]))
    here = lax.dynamic_index_in_dim(pair_grid, rank, 0, keepdims=False)
    cond_pre = lax.dynamic_slice(time_table, (here, 0), (1, cond_width))
    cond_low = jax.nn.silu(cond_pre).astype(bf16)
    ada_flat = w_ada.reshape(cond_width, 6 * width)
    modulation = jnp.dot(cond_low, ada_flat, preferred_element_type=f32).reshape(6, width) + b_ada

    starts = jnp.stack([(2 * side + (parity ^ odd)) * row_count for side in (core, 1 - core) for odd in range(2)])
    positions = starts[:, None] + jnp.arange(row_count, dtype=jnp.int32)[None, :]
    lane = jnp.arange(LANES, dtype=jnp.int32)
    half_dim = HEAD_DIM // 2
    frequency = 10000.0 ** (-(lane % half_dim).astype(f32) / half_dim)
    angles = positions.reshape(-1, 1).astype(f32) * frequency[None, :]
    cosine = jnp.cos(angles)
    sine = jnp.sin(angles) * jnp.where(lane % HEAD_DIM < half_dim, -1.0, 1.0)[None, :]

    def quarter_of(values, rows):
        return lax.dynamic_slice_in_dim(values, quarter * rows, rows, 0)

    def along(piece):
        return jnp.stack([moves.even(piece), moves.odd(piece)])

    def across(first, second, *before):
        first_x, second_y = together((moves.flip(first, 1 << 1), moves.flip(second, 2 << 1)), *before)
        one, two = jnp.stack([first, first_x]), jnp.stack([second, second_y])
        return one, two, moves.flip(one, 2 << 1), moves.flip(two, 1 << 1)

    def across_at_once(first, second):
        both = jnp.stack([first, second])
        return [both] + [moves.flip(both, turn << 1) for turn in (1, 2, 3)]

    qkv_rows = shard_width // 4
    qkv_slice = lax.dynamic_slice_in_dim(w_qkv, quarter * qkv_rows, qkv_rows, 2)
    qkv_piece = qkv_slice.transpose(1, 2, 0).reshape(3 * qkv_rows, width)
    attn_piece = jnp.concatenate([qkv_piece, quarter_of(w_out, qkv_rows)])
    up_piece, down_piece = quarter_of(w_up, width // 4), quarter_of(w_down, hidden // 4)
    odd_piece = jnp.concatenate([up_piece, down_piece])
    attn_even, attn_odd = moves.even(attn_piece), moves.odd(attn_piece)

    def sent(values, odd):
        return lax.dynamic_index_in_dim(values, parity ^ odd, 0, keepdims=False)

    mask_rows = jnp.pad(token_mask.astype(bf16), ((0, 0), (0, width - row_count)))[:, None]
    bias_rows = jnp.broadcast_to(split3(b_up)[None], (2, 3, width))
    rest = jnp.zeros((2, EXTRA - 4, width), bf16)
    packs = jnp.concatenate([after(tokens_in, came_grid, attn_piece), mask_rows, bias_rows, rest], axis=1)
    sent_even, sent_odd = sent(packs, 0), sent(packs, 1)
    cot_even, cot_odd = sent(cotangent, 0), sent(cotangent, 1)
    pack_even, pack_odd = moves.even(sent_even), moves.odd(sent_odd)
    attn_even, attn_odd = together(
        (attn_even, attn_odd), odd_piece, up_piece, cot_even, cot_odd, cosine, sine, modulation
    )
    attn_pieces = across(attn_even, attn_odd)
    odd_piece, up_piece = together((odd_piece, up_piece), pack_even, pack_odd)
    ffn_even, ffn_odd = moves.even(up_piece), moves.odd(odd_piece)
    cot_even, cot_odd = together((cot_even, cot_odd), ffn_even, ffn_odd)
    qkv_t, out_rows = place(
        attn_pieces,
        place_of,
        [
            ((shard, index * qkv_rows, qkv_rows), int(index == 3), (None if index == 3 else index, shard * shard_width, qkv_rows))
            for shard in range(2)
            for index in range(4)
        ],
        [like((3, 2 * shard_width, width), bf16), like((2 * shard_width, width), bf16)],
    )

    def bias_of(pack):
        return jnp.sum(pack[row_count + 1 : row_count + 4].astype(f32), axis=0, keepdims=True)

    table = jnp.concatenate(
        [
            modulation,
            norm1[None],
            norm2[None],
            mask_vector[None],
            b_down[None],
            bias_of(pack_even),
            bias_of(pack_odd),
            jnp.zeros((4, width), f32),
        ]
    )

    residual, first_own = enter(pack_even, pack_odd, table)
    first_other = moves.swap(after(first_own, attn_pieces[0], attn_pieces[1]))
    first_other = after(first_other, attn_pieces[2], attn_pieces[3], ffn_even, ffn_odd)
    cot_even, cot_odd, up_even, up_odd = together(
        (cot_even, cot_odd, ffn_even, ffn_odd[: width // 4]), first_other
    )
    cot_even, cot_odd = moves.even(cot_even), moves.odd(cot_odd)
    upstream = jnp.concatenate([cot_even, cot_odd])
    up_pieces = across_at_once(up_even, up_odd)
    queries, keys, values, mixed, log_sum, attn_own, attn_given = attend(
        first_own, first_other, qkv_t, out_rows, cosine, sine
    )
    down_quarter, down_shard = together((ffn_odd[width // 4 :], w_down), attn_own)
    attn_came = moves.swap(after(attn_given, cot_even, cot_odd, *up_pieces[1:]))
    down_even = moves.even(down_shard)
    down_pieces = [down_quarter] + [moves.flip(down_quarter, turn << 1) for turn in (1, 2, 3)]
    (up_full,) = place(
        up_pieces,
        place_of,
        [((shard, 0, width // 4), 0, (shard, 0, width // 4)) for shard in range(2)],
        [like((2, width, hidden), bf16)],
        steps=1,
    )
    attn_came = after(attn_came, *down_pieces[1:])
    second_res, second_own = second(residual, attn_own, attn_came, table)
    second_other = moves.swap(second_own)
    active_own, bend_own = upper(second_own, table, up_full)
    active_other, bend_other = upper(after(second_other, active_own), table, up_full)
    grad_mlp_own = (modulation[5:6] * upstream.astype(f32)).astype(bf16)
    grad_mlp_other = moves.swap(grad_mlp_own)

    def meet(pieces):
        return add([pieces[0]] + [moves.flip(pieces[turn], turn << 1) for turn in (1, 2, 3)], pieces[0].ndim == 3 and 2 or 1)

    def back(first, second):
        return [moves.even(first, back=True), moves.odd(second, back=True)]

    def share(mine):
        mine = mine + moves.swap(mine)
        for bit in range(3, dp_size.bit_length() - 1):
            mine = mine + moves.flip(mine, 1 << bit)
        return mine

    def spread(mine, *before):
        low = mine.astype(bf16)
        axis = low.ndim - 2
        rows = low.shape[axis] // 2
        kept = lax.dynamic_slice_in_dim(low, core * rows, rows, axis)
        given = lax.dynamic_slice_in_dim(low, (1 - core) * rows, rows, axis)
        came = together(tuple(moves.flip(kept, turn << 1) for turn in (1, 2, 3)), *before)
        back = moves.swap(jnp.stack(came))
        return [kept, given, came[0], back[0], came[1], back[1], came[2], back[2]]

    d_down = ffn_weights(place_of, (active_own, active_other), (grad_mlp_own, grad_mlp_other), True, False)
    (down_odd,) = place(
        together(tuple(down_pieces), d_down[0], down_even),
        place_of,
        [((0, 0, hidden // 4), 0, (None, 0, hidden // 4))],
        [like((hidden, width), bf16)],
        steps=0,
    )
    down_came = [moves.flip(d_down[turn], turn << 1) for turn in (1, 2, 3)]

    grad_mlp_late = after(grad_mlp_other, d_down[0])
    upper_grad_other, *part_given, sum_other = ffn_back(grad_mlp_late, down_even, down_odd, up_full, bend_other)
    part_came = [moves.swap(p) for p in part_given]
    upper_grad_own, *part_own, sum_own = ffn_back(
        after(grad_mlp_own, *part_given), down_even, down_odd, up_full, bend_own
    )
    grad_res, grad_attn_own, sum_middle = middle(
        part_own, part_came, upstream, second_res, attn_own, attn_came, table
    )
    grad_attn_other = moves.swap(grad_attn_own)
    d_up = ffn_weights(
        place_of, (second_own, second_other), (upper_grad_own, after(upper_grad_other, grad_attn_own)), False, False
    )
    down_came = together(tuple(down_came), d_up[0])
    mlp_given = lower(after(active_other, *down_came), down_even, down_odd)
    mlp_came = moves.swap(mlp_given)
    mlp_own = lower(after(active_own, mlp_given), down_even, down_odd)
    down_parts = add([d_down[0], *down_came], 2)
    layer_even, layer_odd, sum_leave = leave(second_res, mlp_own, mlp_came, upstream, down_parts, table)

    def to_ranks(even, odd):
        return jnp.where(parity == 0, jnp.stack([even, odd]), jnp.stack([odd, even]))

    d_up = together(tuple(d_up), layer_even)
    up_came = [moves.flip(d_up[turn], turn << 1) for turn in (1, 2, 3)]
    layer_back = back(layer_even, layer_odd)
    d_first, found, rest, finish_back = attend_back(
        place_of,
        after(grad_attn_own, layer_even),
        grad_attn_other,
        first_own,
        first_other,
        qkv_t,
        out_rows,
        cosine,
        sine,
        queries,
        keys,
        values,
        mixed,
        log_sum,
    )
    up_came = together(tuple(up_came), found)
    d_first = together(tuple(d_first), found, *up_came)
    up_parts = add([d_up[0], *up_came], 2)
    first_came = [moves.flip(d_first[turn], turn << 1) for turn in (1, 2, 3)]
    found, rest = together((found, rest), *up_parts)
    d_second, last, first_grads = finish_back(found, rest)
    d_second = together(tuple(d_second), *first_came, *layer_back)
    layer_back = together(tuple(layer_back), last)
    up_back = back(*together(tuple(up_parts), *layer_back))
    first_parts = add([d_first[0], *first_came])
    second_came = [moves.flip(d_second[turn], turn << 1) for turn in (1, 2, 3)]
    first_part, first_given = first_grads(after(last, d_second[0]))
    first_came = moves.swap(after(first_given, *second_came, *up_back))
    second_parts = add([d_second[0]] + second_came)
    attn_back = back(first_parts, second_parts)
    in_even, in_odd, sum_end = end(first_part, first_came, residual, pack_even, pack_odd, grad_res, table)
    layer_back = together(tuple(layer_back), sum_end)
    layer_out = to_ranks(*[p[:row_count] for p in layer_back])
    ffn_part = share(
        jnp.concatenate(
            [add([p[row_count:] for p in layer_back], dtype=f32), add(together(tuple(up_back), sum_end), dtype=f32)]
        )
    )
    attn_part = share(add(together(tuple(attn_back), sum_end), dtype=f32))
    ffn_spread = spread(ffn_part.reshape(2, -1, width))
    grad_w_down = finish([p[0] for p in ffn_spread], place_of, (hidden, width))
    grad_w_up = finish([p[1] for p in ffn_spread], place_of, (width, hidden))
    attn_spread = spread(attn_part, ffn_spread[2], ffn_spread[4], ffn_spread[6])
    grad_attn_rows = finish(attn_spread, place_of, (4 * shard_width, width)).reshape(4, 4, qkv_rows, width)
    grad_w_out = grad_attn_rows[:, 3].reshape(shard_width, width)
    grad_w_qkv = grad_attn_rows[:, :3].transpose(3, 1, 0, 2).reshape(width, 3, shard_width)

    scale_up = 1.0 + modulation
    upper_two = (sum_own[0] + sum_other[0]).reshape(2, hidden)
    upper_two = jnp.where(parity == 1, upper_two[::-1], upper_two)
    blank = jnp.zeros((2, hidden), f32)
    cond_row = jnp.pad(jnp.concatenate([cond_pre[0], here.astype(f32)[None]]), (0, width - cond_width - 1))
    cond_row = jnp.where(core == 0, cond_row, 0.0)
    rows = jnp.concatenate(
        [
            jnp.stack(
                [
                    sum_end[0],
                    sum_end[1] * norm1,
                    sum_middle[2],
                    sum_middle[0],
                    sum_middle[1] * norm2,
                    sum_leave[0],
                    cond_row,
                    sum_end[1] * scale_up[1],
                    sum_end[2],
                    sum_middle[1] * scale_up[4],
                    sum_leave[1],
                ]
            ),
            jnp.where(core == 0, upper_two, blank),
            jnp.where(core == 0, blank, upper_two),
        ]
    )
    rows = rows + moves.swap(rows)
    each, sums = rows[:7], rows[7:]
    steps = [(moves.flip, 1 << bit, dp >> bit & 1) for bit in range(1, dp_size.bit_length() - 1)]
    steps += [(moves.flip_rank, bit, rank >> bit & 1) for bit in range(ranks.bit_length() - 1)]
    for move, which, ahead in steps:
        came = move(jnp.concatenate([each, sums]), which)
        if which == steps[-1][1] and move == steps[-1][0]:
            came = after(came, ffn_spread[2], ffn_spread[4], ffn_spread[6])
        sums = sums + came[each.shape[0] :]
        came = came[: each.shape[0]]
        each = jnp.where(ahead == 1, jnp.concatenate([came, each]), jnp.concatenate([each, came]))
        if move == moves.flip_rank and which == 0:
            grad_in = to_ranks(*back(*together((in_even, in_odd), came)))
    each, sums = together((each, sums), attn_spread[2], attn_spread[4], attn_spread[6])
    each = each.reshape(-1, 7, width)
    grad_mods = each[:, :6]
    cond_all = each[:, 6, :cond_width]
    grid_all = each[:, 6, cond_width].astype(jnp.int32)
    grad_b_up = lax.dynamic_index_in_dim(sums[4:], rank, 0, keepdims=False)

    points = time_table.shape[0]
    onehot = (grid_all[:, None] == jnp.arange(points, dtype=jnp.int32)[None, :]).astype(f32)
    cond_act, silu_back = jax.vjp(jax.nn.silu, cond_all)
    cond_act = cond_act.astype(bf16).astype(f32)
    grad_flat = grad_mods.reshape(-1, 6 * width)
    grad_w_ada = jnp.dot(cond_act.T, grad_flat, precision=highest).reshape(cond_width, 6, width)
    grad_b_ada = jnp.sum(grad_mods, axis=0)
    grad_cond = jnp.dot(grad_flat, ada_flat.astype(f32).T, precision=highest)
    grad_pre = silu_back(grad_cond)[0]
    grad_table = jnp.dot(onehot.T, grad_pre, precision=highest)
    return (
        layer_out,
        grad_in,
        grad_table,
        sums[1],
        grad_w_ada,
        grad_b_ada,
        sums[0],
        sums[2],
        grad_w_qkv,
        grad_w_out,
        grad_w_up,
        grad_b_up,
        grad_w_down,
        sums[3],
    )


def solution(mesh):
    parts = (mesh.shape["dp"] // 8, 2, 2, 2, mesh.shape["tensor"])
    finer = jax.sharding.Mesh(mesh.devices.reshape(parts), AXES)
    whole = P()
    split = P(DP, "tensor", None)
    weights = (P(None, None, "tensor"), P("tensor", None), P(None, "tensor"), P("tensor"), P("tensor", None), whole)
    return jax.shard_map(
        shards,
        mesh=finer,
        in_specs=(split, P(DP, "tensor"), P(DP), whole, split) + (whole,) * 5 + weights,
        out_specs=(split, split) + (whole,) * 6 + weights,
        check_vma=False,
    )
```

```python
import functools

import jax
import jax.numpy as jnp
from jax import lax
from jax.experimental import pallas as pl
from jax.experimental.pallas import tpu as pltpu
from jax.sharding import PartitionSpec as P

HEAD_DIM = 64
LANES = 128
EXTRA = 16
f32 = jnp.float32
bf16 = jnp.bfloat16
highest = lax.Precision.HIGHEST
NN = (((1,), (0,)), ((), ()))
NT = (((1,), (1,)), ((), ()))
TN = (((0,), (0,)), ((), ()))
DP = ("r", "y", "x", "c")
AXES = DP + ("tensor",)
MIB = 2**20
SHARE = 64

SHIFT1, SCALE1, GATE1, SHIFT2, SCALE2, GATE2, NORM1, NORM2, MASKED, B_DOWN, B_UP = range(11)


def dot(left, right, dims=NN):
    return lax.dot_general(left, right, dims, preferred_element_type=f32)


def row(table, index):
    return table[index : index + 1, :]


def full(shape):
    return pl.BlockSpec(shape, lambda *i: (0,) * len(shape))


def by_rows(size, width):
    return pl.BlockSpec((size, width), lambda i: (i, 0))


def like(shape, dtype):
    return jax.ShapeDtypeStruct(shape, dtype)


def call(body, grid, ins, specs, outs, out_specs, scratch=(), mib=24, flops=0, special=0, name=None):
    moved = sum(x.size * x.dtype.itemsize for x in ins) + sum(x.size * x.dtype.itemsize for x in outs)
    return pl.pallas_call(
        body,
        grid=(grid,),
        in_specs=specs,
        out_specs=out_specs,
        out_shape=outs,
        scratch_shapes=list(scratch),
        name=name,
        compiler_params=pltpu.CompilerParams(vmem_limit_bytes=mib * MIB),
        cost_estimate=pl.CostEstimate(flops=flops // SHARE, bytes_accessed=moved // SHARE, transcendentals=special // SHARE),
    )(*ins)


def centered(values):
    average = jnp.mean(values, axis=-1, keepdims=True)
    away = values - average
    inverse = lax.rsqrt(jnp.mean(away * away, axis=-1, keepdims=True) + 1e-05)
    return away * inverse, inverse


def norm_back(grads, hat, inverse, factor):
    slope = grads * factor
    lean = jnp.mean(slope, axis=-1, keepdims=True)
    tilt = jnp.mean(slope * hat, axis=-1, keepdims=True)
    return (slope - lean - hat * tilt) * inverse


def after(values, *others):
    return lax.optimization_barrier((values,) + others)[0]


def together(values, *others):
    return lax.optimization_barrier(values + others)[: len(values)]


def over_rows(values):
    return jnp.sum(values, axis=0, keepdims=True)


def mask_column(extra):
    count = extra.shape[1] // LANES * LANES
    line = extra[0:1, :].astype(f32)
    return jnp.broadcast_to(line, (LANES, count)).T[:, 0:1]


def place_kernel(plan, steps, place_of, *refs):
    count = 5 if steps == 0 else 4
    (one, two, first_y, second_x), outs = refs[:4], refs[count:]
    if steps == 0:
        shards_of = (tuple((piece, None) for piece in refs[:4]),)
        outs[0][: refs[4].shape[0], :] = refs[4][...]
    elif steps == 1:
        shards_of = tuple(tuple((piece, shard) for piece in refs[:4]) for shard in range(2))
    else:
        shards_of = (((one, 0), (one, 1), (first_y, 0), (first_y, 1)), ((two, 0), (second_x, 0), (two, 1), (second_x, 1)))
    for turn in range(4):
        here = place_of[0] ^ turn
        for (shard, start, size), out, (lead, base, pitch) in plan:
            piece, index = shards_of[shard][turn]
            rows = pl.ds(pl.multiple_of(base + here * pitch, 16), size)
            where = (rows, slice(None)) if lead is None else (lead, rows, slice(None))
            rows_of = slice(start, start + size)
            outs[out][where] = piece[rows_of, :] if index is None else piece[index, rows_of, :]


def place(pieces, place_of, plan, outs, steps=2):
    moved = sum(2 * x.size * x.dtype.itemsize for x in outs)
    return pl.pallas_call(
        functools.partial(place_kernel, plan, steps),
        in_specs=[pl.BlockSpec(memory_space=pltpu.SMEM)] + [pl.BlockSpec(memory_space=pltpu.VMEM)] * len(pieces),
        out_specs=[pl.BlockSpec(memory_space=pltpu.VMEM)] * len(outs),
        out_shape=outs,
        name="place",
        compiler_params=pltpu.CompilerParams(vmem_limit_bytes=12 * MIB),
        cost_estimate=pl.CostEstimate(flops=0, bytes_accessed=moved // SHARE, transcendentals=0),
    )(place_of, *pieces)


def finish_kernel(place_of, *refs):
    pieces, outs = refs[:8], refs[8:]
    quarter, core = place_of[0], place_of[1]
    for turn in range(4):
        for side in range(2):
            piece = pieces[2 * turn + side]
            size = piece.shape[1]
            rows = pl.ds(pl.multiple_of((quarter ^ turn) * 2 * size + (core ^ side) * size, 8), size)
            for index, out in enumerate(outs):
                out[rows, :] = piece[index].astype(f32)


def finish(pieces, place_of, shapes):
    return pl.pallas_call(
        finish_kernel,
        in_specs=[pl.BlockSpec(memory_space=pltpu.SMEM)] + [pl.BlockSpec(memory_space=pltpu.VMEM)] * 8,
        out_specs=[pl.BlockSpec(memory_space=pltpu.VMEM)] * len(shapes),
        out_shape=[like(shape, f32) for shape in shapes],
        name="finish",
        compiler_params=pltpu.CompilerParams(vmem_limit_bytes=24 * MIB),
    )(place_of, *pieces)


def enter_kernel(even, odd, table, residual, first):
    rows = even.shape[0] - EXTRA
    for index, pack in enumerate((even, odd)):
        here = slice(index * rows, (index + 1) * rows)
        mask = mask_column(pack[rows:, :rows])
        values = pack[:rows, :].astype(f32) + mask * row(table, MASKED)
        residual[here, :] = values
        hat, _ = centered(values)
        factor = row(table, NORM1) * (1.0 + row(table, SCALE1))
        first[here, :] = (hat * factor + row(table, SHIFT1)).astype(bf16)


def enter(even, odd, table):
    rows, width = 2 * (even.shape[0] - EXTRA), even.shape[1]
    return call(
        enter_kernel,
        1,
        (even, odd, table),
        [full(even.shape), full(odd.shape), full(table.shape)],
        [like((rows, width), f32), like((rows, width), bf16)],
        [full((rows, width))] * 2,
        name="enter",
    )


def partner(values):
    lane = lax.broadcasted_iota(jnp.int32, values.shape, 1)
    ahead = pltpu.roll(values, LANES - HEAD_DIM // 2, 1)
    behind = pltpu.roll(values, HEAD_DIM // 2, 1)
    return jnp.where(lane % HEAD_DIM < HEAD_DIM // 2, ahead, behind)


def heads_of(values):
    lane = lax.broadcasted_iota(jnp.int32, values.shape, 1)
    return lane < HEAD_DIM


def attend_kernel(
    own, other, weights, w_out, cosine, sine, queries, keys, values, mixed, log_sum, part_own, part_other, total
):
    step = pl.program_id(0)
    half = own.shape[0]
    length = 2 * half
    chunk = 256
    for index, tokens in enumerate((own, other)):
        here = slice(index * half, (index + 1) * half)
        query = dot(tokens[...], weights[0], NT)
        turned = (query * cosine[here, :] + partner(query) * sine[here, :]).astype(bf16)
        queries[here, :] = (turned * HEAD_DIM**-0.5).astype(bf16)
        key = dot(tokens[...], weights[1], NT)
        keys[here, :] = (key * cosine[here, :] + partner(key) * sine[here, :]).astype(bf16)
        values[here, :] = dot(tokens[...], weights[2], NT).astype(bf16)

    @pl.when(step == 0)
    def _():
        total[...] = jnp.zeros_like(total)

    every_key, every_value = keys[...], values[...]
    items = [(start, head) for start in range(0, length, chunk) for head in range(2)]

    def score(start, head):
        block = queries[pl.ds(start, chunk), :]
        former = heads_of(block)
        return dot(jnp.where(former if head == 0 else ~former, block, 0), every_key, NT)

    following = score(*items[0])
    halves = []
    for index, (start, head) in enumerate(items):
        scores = following
        if index + 1 < len(items):
            following = score(*items[index + 1])
        top = jnp.max(scores, axis=1, keepdims=True)
        powers = jnp.exp(scores - top)
        sums = jnp.sum(powers, axis=1, keepdims=True)
        halves.append((dot(powers.astype(bf16), every_value) * (1.0 / sums), top + jnp.log(sums)))
        if head == 1:
            here = pl.ds(start, chunk)
            former = heads_of(halves[0][0])
            out = jnp.where(former, halves[0][0], halves[1][0])
            mixed[here, :] = out
            log_sum[here, :] = jnp.where(former, halves[0][1], halves[1][1])
            total[here, :] += dot(out.astype(bf16), w_out[...])
            halves = []

    @pl.when(step == pl.num_programs(0) - 1)
    def _():
        part_own[...] = total[:half, :].astype(bf16)
        part_other[...] = total[half:, :].astype(bf16)


def attend(own, other, weights, w_out, cosine, sine):
    half, width = own.shape
    length = 2 * half
    wide = w_out.shape[0]
    tall = pl.BlockSpec((length, LANES), lambda i: (0, i))
    return call(
        attend_kernel,
        wide // LANES,
        (own, other, weights, w_out, cosine, sine),
        [
            full(own.shape),
            full(own.shape),
            pl.BlockSpec((3, LANES, width), lambda i: (0, i, 0)),
            pl.BlockSpec((LANES, width), lambda i: (i, 0)),
            full(cosine.shape),
            full(sine.shape),
        ],
        [like((length, wide), bf16)] * 3 + [like((length, wide), f32)] * 2 + [like((half, width), bf16)] * 2,
        [tall] * 5 + [full((half, width))] * 2,
        [pltpu.VMEM((length, width), f32)],
        mib=36,
        flops=8 * length * width * wide + 16 * length * length * wide,
        special=length * length * wide // HEAD_DIM,
        name="attend",
    )


def pair_back(grads_own, grads_other, own, other, w_out, cosine, sine, queries, keys, values, mixed, log_sum):
    half = own.shape[0]
    length = 2 * half
    chunk = 256
    outs = mixed[...]
    low = outs.astype(bf16)
    grad = jnp.concatenate([dot(grads_own[...], w_out[...], NT), dot(grads_other[...], w_out[...], NT)]).astype(bf16)
    d_out = dot(low[:half], grads_own[...], TN) + dot(low[half:], grads_other[...], TN)
    lean_t = (grad.astype(f32) * outs).T
    log_t = log_sum[...].T
    query, key, value = queries[...], keys[...], values[...]
    former = heads_of(query)
    former_chunk = heads_of(query[:chunk])
    items = [(head, start) for head in range(2) for start in range(0, length, chunk)]

    def products(head, start):
        mine = former_chunk if head == 0 else ~former_chunk
        key_rows = jnp.where(mine, key[start : start + chunk], 0)
        value_rows = jnp.where(mine, value[start : start + chunk], 0)
        return dot(key_rows, query, NT), dot(value_rows, grad, NT)

    found_q, found_k, found_v = [None, None], ([], []), ([], [])

    def collect(head, start, probs, slopes):
        found_v[head].append(dot(probs, grad))
        found_k[head].append(dot(slopes, query))
        more = dot(key[start : start + chunk], slopes, TN)
        found_q[head] = more if found_q[head] is None else found_q[head] + more

    following, pending = products(*items[0]), None
    for index, (head, start) in enumerate(items):
        scores, against = following
        if index + 1 < len(items):
            following = products(*items[index + 1])
        if pending is not None:
            collect(*pending)
        lean = over_rows(lean_t[head * HEAD_DIM : (head + 1) * HEAD_DIM])
        probs = jnp.exp(scores - log_t[head * HEAD_DIM : head * HEAD_DIM + 1])
        pending = (head, start, probs.astype(bf16), (probs * (against - lean)).astype(bf16))
    collect(*pending)
    row_head = lax.broadcasted_iota(jnp.int32, found_q[0].shape, 0)
    d_query = jnp.where(row_head < HEAD_DIM, found_q[0], found_q[1]).T * HEAD_DIM**-0.5
    d_key = jnp.where(former, jnp.concatenate(found_k[0]), jnp.concatenate(found_k[1]))
    d_value = jnp.where(former, jnp.concatenate(found_v[0]), jnp.concatenate(found_v[1])).astype(bf16)
    d_query = (d_query * cosine[...] + partner(d_query * sine[...])).astype(bf16)
    d_key = (d_key * cosine[...] + partner(d_key * sine[...])).astype(bf16)
    found = (d_query, d_key, d_value)
    return found, [dot(g[:half], own[...], TN) + dot(g[half:], other[...], TN) for g in found] + [d_out]


def put_pieces(pieces, rows_of_weight, quarter, size):
    for turn, piece in enumerate(pieces):
        rows = pl.ds(pl.multiple_of((quarter ^ turn) * size, 16), size)
        for index in range(4):
            piece[index * size : (index + 1) * size, :] = rows_of_weight[index, rows, :]


def attend_back_kernel(shard_rows, place_of, *refs):
    ins, (found_all, *pieces), rest, d_weights = refs[:12], refs[12:17], refs[17], refs[18]
    step = pl.program_id(0)
    found, rows = pair_back(*ins)
    here = pl.ds(pl.multiple_of(step * LANES, LANES), LANES)
    for index in range(3):
        found_all[index] = found[index]
    for index in range(4):
        d_weights[index, here, :] = rows[index].astype(bf16)

    @pl.when(step == pl.num_programs(0) - 1)
    def _():
        put_pieces(pieces, d_weights, place_of[0], shard_rows // 4)
        rest[...] = d_weights[:, shard_rows:, :]


def attend_back_end_kernel(shard_rows, place_of, rows_before, *refs):
    ins, (found_all, *pieces), d_weights = refs[:12], refs[12:17], refs[17]
    found, rows = pair_back(*ins)
    start = rows_before.shape[1]
    d_weights[:, :start, :] = rows_before[...]
    for index in range(3):
        found_all[index] = found[index]
    for index in range(4):
        d_weights[index, start:, :] = rows[index].astype(bf16)
    put_pieces(pieces, d_weights, place_of[0], shard_rows // 4)


def first_grads_kernel(before, last, weights, part_own, part_other):
    step, wide = pl.program_id(0), before.shape[2]
    total = dot(last[0], weights[0, wide:, :])
    total += dot(last[1], weights[1, wide:, :]) + dot(last[2], weights[2, wide:, :])
    for index in range(3):
        total += dot(before[index], weights[index, :wide, :])
    result = total.astype(bf16)

    @pl.when(step == 0)
    def _():
        part_other[...] = result

    @pl.when(step == 1)
    def _():
        part_own[...] = result


def attend_back(place_of, grads_own, grads_other, own, other, weights, w_out, cosine, sine, *kept):
    half, width = own.shape
    length = 2 * half
    wide = w_out.shape[0]
    shard_rows = wide // 2
    first = -(-shard_rows // LANES)
    rows = full((half, width))
    quarter = like((shard_rows, width), bf16)
    smem = pl.BlockSpec(memory_space=pltpu.SMEM)

    def specs(base):
        tall = pl.BlockSpec((length, LANES), lambda i: (0, i + base))
        flat = pl.BlockSpec((LANES, width), lambda i: (i + base, 0))
        return [rows] * 4 + [flat, full(cosine.shape), full(sine.shape)] + [tall] * 5

    ins = (grads_own, grads_other, own, other, w_out, cosine, sine) + kept
    work = dict(flops=14 * length * width * LANES + 40 * length * length * LANES, special=2 * length * length)
    found, *pieces, rest = call(
        functools.partial(attend_back_kernel, shard_rows),
        first,
        (place_of,) + ins,
        [smem] + specs(0),
        [like((3, length, first * LANES), bf16)] + [quarter] * 4 + [like((4, first * LANES - shard_rows, width), bf16)],
        [pl.BlockSpec((3, length, LANES), lambda i: (0, 0, i))]
        + [full(quarter.shape)] * 4
        + [full((4, first * LANES - shard_rows, width))],
        [pltpu.VMEM((4, first * LANES, width), bf16)],
        mib=60,
        name="attend_back",
        **work,
    )

    def finish_back(found, rest):
        last, *more = call(
            functools.partial(attend_back_end_kernel, shard_rows),
            1,
            (place_of, rest) + ins,
            [smem, full(rest.shape)] + specs(first),
            [like((3, length, LANES), bf16)] + [quarter] * 4,
            [full((3, length, LANES))] + [full(quarter.shape)] * 4,
            [pltpu.VMEM((4, shard_rows, width), bf16)],
            mib=60,
            name="attend_back_end",
            **work,
        )

        def first_grads(last):
            return call(
                first_grads_kernel,
                2,
                (found, last, weights),
                [
                    pl.BlockSpec((3, half, found.shape[2]), lambda i: (0, 1 - i, 0)),
                    pl.BlockSpec((3, half, LANES), lambda i: (0, 1 - i, 0)),
                    full(weights.shape),
                ],
                [like((half, width), bf16)] * 2,
                [rows] * 2,
                mib=60,
        name="first_grads",
            )

        return more, last, first_grads

    return pieces, found, rest, finish_back


def lift(inner, table, w_up, active, bend):
    hidden = w_up.shape[2]
    root = 0.7978845608028654
    for block in range(2):
        span = slice(block * hidden, (block + 1) * hidden)
        u = dot(inner, w_up[block]) + table[B_UP + block : B_UP + block + 1, :hidden]
        square = u * u
        curve = jnp.tanh(root * (u + 0.044715 * (square * u)))
        rise = 0.5 + 0.5 * curve
        active[:, span] = (u * rise).astype(bf16)
        slope = rise + (0.5 * root) * u * (1.0 - curve * curve) * (1.0 + 0.134145 * square)
        bend[:, span] = slope.astype(bf16)


def second_kernel(residual, mine, came, table, second_res, second):
    values = residual[...] + row(table, GATE1) * (mine[...].astype(f32) + came[...].astype(f32))
    second_res[...] = values
    hat, _ = centered(values)
    factor = row(table, NORM2) * (1.0 + row(table, SCALE2))
    second[...] = (hat * factor + row(table, SHIFT2)).astype(bf16)


def second(residual, mine, came, table, size=256):
    rows, width = residual.shape
    spec = by_rows(size, width)
    return call(
        second_kernel,
        rows // size,
        (residual, mine, came, table),
        [spec, spec, spec, full(table.shape)],
        [like((rows, width), f32), like((rows, width), bf16)],
        [spec, spec],
        flops=10 * rows * width,
        name="second",
    )


def upper_kernel(inner, table, w_up, active, bend):
    lift(inner[...], table, w_up, active, bend)


def upper(inner, table, w_up, size=256):
    rows, width = inner.shape
    hidden = 2 * w_up.shape[2]
    broad = by_rows(size, hidden)
    return call(
        upper_kernel,
        rows // size,
        (inner, table, w_up),
        [by_rows(size, width), full(table.shape), full(w_up.shape)],
        [like((rows, hidden), bf16)] * 2,
        [broad, broad],
        flops=2 * rows * width * hidden,
        special=rows * hidden,
        name="upper",
    )


def ffn_back_kernel(grad_mlp, down_even, down_odd, w_up, bend, grad_upper, *refs):
    parts, sums = refs[:-1], refs[-1]
    step = pl.program_id(0)
    grad = jnp.concatenate([dot(grad_mlp[...], down[...], NT) for down in (down_even, down_odd)], axis=1)
    grad = (grad * bend[...].astype(f32)).astype(bf16)
    grad_upper[...] = grad
    hidden = w_up.shape[2]
    result = (dot(grad[:, :hidden], w_up[0], NT) + dot(grad[:, hidden:], w_up[1], NT)).astype(bf16)
    for index, part in enumerate(parts):

        @pl.when(step == index)
        def _(part=part):
            part[...] = result

    @pl.when(step == 0)
    def _():
        sums[...] = jnp.zeros_like(sums)

    sums[0:1, :] += over_rows(grad.astype(f32))


def ffn_back(grad_mlp, down_even, down_odd, w_up, bend, size=256):
    rows, width = grad_mlp.shape
    hidden = 2 * down_even.shape[0]
    spec, broad = by_rows(size, width), by_rows(size, hidden)
    return call(
        ffn_back_kernel,
        rows // size,
        (grad_mlp, down_even, down_odd, w_up, bend),
        [spec, full(down_even.shape), full(down_odd.shape), full(w_up.shape), broad],
        [like((rows, hidden), bf16)] + [like((size, width), bf16)] * (rows // size) + [like((8, hidden), f32)],
        [broad] + [full((size, width))] * (rows // size) + [full((8, hidden))],
        flops=4 * rows * width * hidden,
        name="ffn_back",
    )


def ffn_weights_kernel(place_of, left_own, left_other, right_own, right_other, *refs):
    pieces, whole = refs[:-1], refs[-1]
    whole[...] = (dot(left_own[...], right_own[...], TN) + dot(left_other[...], right_other[...], TN)).astype(bf16)
    size = whole.shape[0] // 4
    if len(pieces) == 1:
        for index in range(4):
            pieces[0][index, 0] = whole[index * size : (index + 1) * size, :]
        return
    for turn, piece in enumerate(pieces):
        rows = pl.ds(pl.multiple_of((place_of[0] ^ turn) * size, 16), size)
        piece[0] = whole[rows, :]


def ffn_weights(place_of, left, right, split_left, ordered):
    rows, width = right[0].shape if split_left else left[0].shape
    hidden = (left if split_left else right)[0].shape[1] // 2
    whole, halved = full((rows, width)), pl.BlockSpec((rows, hidden), lambda i: (0, i))
    lefts, rights = (halved, whole) if split_left else (whole, halved)
    shape = (hidden, width) if split_left else (width, hidden)
    size = shape[0] // 4
    if ordered:
        outs, specs = [(4, 2, size, shape[1])], [pl.BlockSpec((4, 1, size, shape[1]), lambda i: (0, i, 0, 0))]
    else:
        outs, specs = [(2, size, shape[1])] * 4, [pl.BlockSpec((1, size, shape[1]), lambda i: (i, 0, 0))] * 4
    return call(
        ffn_weights_kernel,
        2,
        (place_of,) + tuple(left) + tuple(right),
        [pl.BlockSpec(memory_space=pltpu.SMEM), lefts, lefts, rights, rights],
        [like(out, bf16) for out in outs],
        specs,
        [pltpu.VMEM(shape, bf16)],
        flops=8 * rows * width * hidden,
        name="ffn_weights",
    )


def sum_kernel(count, *refs):
    pieces, outs = refs[:count], refs[count:]
    for index, out in enumerate(outs):
        values = [p[...] if len(p.shape) == 2 else p[index] for p in pieces]
        out[...] = sum(v.astype(f32) for v in values).astype(out.dtype)


def add(pieces, count=1, dtype=bf16):
    shape = pieces[0].shape[-2:]
    result = pl.pallas_call(
        functools.partial(sum_kernel, len(pieces)),
        in_specs=[pl.BlockSpec(memory_space=pltpu.VMEM)] * len(pieces),
        out_specs=[pl.BlockSpec(memory_space=pltpu.VMEM)] * count,
        out_shape=[like(shape, dtype)] * count,
        name="add",
        compiler_params=pltpu.CompilerParams(vmem_limit_bytes=12 * MIB),
    )(*pieces)
    return result if count > 1 else result[0]


def middle_kernel(parts, *refs):
    mine, came = refs[:parts], refs[parts : 2 * parts]
    upstream, second_res, attn_mine, attn_came, table, grad_res, grad_attn, sums = refs[2 * parts :]
    step = pl.program_id(0)
    grad = mine[0][...].astype(f32) + came[0][...].astype(f32)
    for index in range(1, parts):
        grad = jnp.where(step == index, mine[index][...].astype(f32) + came[index][...].astype(f32), grad)
    hat, inverse = centered(second_res[...])
    factor = row(table, NORM2) * (1.0 + row(table, SCALE2))
    result = upstream[...].astype(f32) + norm_back(grad, hat, inverse, factor)
    grad_res[...] = result
    grad_attn[...] = (row(table, GATE1) * result).astype(bf16)

    @pl.when(step == 0)
    def _():
        sums[...] = jnp.zeros_like(sums)

    attn = attn_mine[...].astype(f32) + attn_came[...].astype(f32)
    sums[0:1, :] += over_rows(grad)
    sums[1:2, :] += over_rows(grad * hat)
    sums[2:3, :] += over_rows(result * attn)


def middle(mine, came, upstream, second_res, attn_mine, attn_came, table, size=256):
    rows, width = upstream.shape
    spec = by_rows(size, width)
    return call(
        functools.partial(middle_kernel, len(mine)),
        rows // size,
        (*mine, *came, upstream, second_res, attn_mine, attn_came, table),
        [full((size, width))] * (2 * len(mine)) + [spec] * 4 + [full(table.shape)],
        [like((rows, width), f32), like((rows, width), bf16), like((8, width), f32)],
        [spec, spec, full((8, width))],
        flops=40 * rows * width,
        name="middle",
    )


def lower_kernel(active, down_even, down_odd, part):
    half = down_even.shape[0]
    part[...] = (dot(active[:, :half], down_even[...]) + dot(active[:, half:], down_odd[...])).astype(bf16)


def lower(active, down_even, down_odd, size=256):
    rows, hidden = active.shape
    width = down_even.shape[1]
    return call(
        lower_kernel,
        rows // size,
        (active, down_even, down_odd),
        [by_rows(size, hidden), full(down_even.shape), full(down_odd.shape)],
        [like((rows, width), bf16)],
        [by_rows(size, width)],
        flops=2 * rows * hidden * width,
        name="lower",
    )[0]


def leave_kernel(second_res, mine, came, upstream, part_even, part_odd, table, even, odd, sums):
    mlp = mine[...].astype(f32) + came[...].astype(f32) + row(table, B_DOWN)
    layer = (second_res[...] + row(table, GATE2) * mlp).astype(bf16)
    rows = layer.shape[0] // 2
    even[:rows, :] = layer[:rows]
    odd[:rows, :] = layer[rows:]
    even[rows:, :] = part_even[...]
    odd[rows:, :] = part_odd[...]
    grads = upstream[...].astype(f32)
    sums[...] = jnp.zeros_like(sums)
    sums[0:1, :] = over_rows(grads * mlp)
    sums[1:2, :] = over_rows((row(table, GATE2) * grads).astype(bf16).astype(f32))


def leave(second_res, mine, came, upstream, parts, table):
    rows, width = upstream.shape
    spec, part = full((rows, width)), full(parts[0].shape)
    out = (rows // 2 + parts[0].shape[0], width)
    return call(
        leave_kernel,
        1,
        (second_res, mine, came, upstream, *parts, table),
        [spec] * 4 + [part] * 2 + [full(table.shape)],
        [like(out, bf16)] * 2 + [like((8, width), f32)],
        [full(out)] * 2 + [full((8, width))],
        flops=6 * rows * width,
        name="leave",
    )


def end_kernel(mine, came, residual, pack_even, pack_odd, grad_res, table, even, odd, sums):
    step, rows = pl.program_id(0), even.shape[0]
    factor = row(table, NORM1) * (1.0 + row(table, SCALE1))
    mask = jnp.where(step == 0, mask_column(pack_even[:, :rows]), mask_column(pack_odd[:, :rows]))
    grad = mine[...].astype(f32) + came[...].astype(f32)
    hat, inverse = centered(residual[...])
    result = grad_res[...] + norm_back(grad, hat, inverse, factor)
    low = result.astype(bf16)

    @pl.when(step == 0)
    def _():
        even[...] = low
        sums[...] = jnp.zeros_like(sums)

    @pl.when(step == 1)
    def _():
        odd[...] = low

    sums[0:1, :] += over_rows(grad)
    sums[1:2, :] += over_rows(grad * hat)
    sums[2:3, :] += over_rows(result * mask)


def end(mine, came, residual, pack_even, pack_odd, grad_res, table):
    rows, width = mine.shape[0] // 2, mine.shape[1]
    spec = by_rows(rows, width)
    extra = pl.BlockSpec((EXTRA, width), lambda i: (rows // EXTRA, 0))
    return call(
        end_kernel,
        2,
        (mine, came, residual, pack_even, pack_odd, grad_res, table),
        [spec, spec, spec, extra, extra, spec, full(table.shape)],
        [like((rows, width), bf16)] * 2 + [like((8, width), f32)],
        [full((rows, width))] * 2 + [full((8, width))],
        flops=60 * rows * width,
        mib=60,
        name="end",
    )


def split3(values):
    high = lax.reduce_precision(values, 8, 7)
    rest = values - high
    middle_term = lax.reduce_precision(rest, 8, 7)
    return jnp.stack([high, middle_term, rest - middle_term]).astype(bf16)


class Moves:
    def __init__(self, dp_size, rank_size):
        self.dp_size, self.rank_size = dp_size, rank_size

    def by(self, values, target, back=False, away=False):
        pairs = []
        for dp in range(self.dp_size):
            for rank in range(self.rank_size):
                core, to_rank = target(dp & 1, rank)
                pair = (dp * self.rank_size + rank, (dp >> 1 << 1 | core) * self.rank_size + to_rank)
                if not away or pair[0] != pair[1]:
                    pairs.append(pair[::-1] if back else pair)
        return lax.ppermute(values, AXES, pairs)

    def flip(self, values, mask):
        pairs = [
            (dp * self.rank_size + rank, (dp ^ mask) * self.rank_size + rank)
            for dp in range(self.dp_size)
            for rank in range(self.rank_size)
        ]
        return lax.ppermute(values, AXES, pairs)

    def swap(self, values):
        return self.flip(values, 1)

    def flip_rank(self, values, bit):
        return self.by(values, lambda core, rank: (core, rank ^ 1 << bit))

    @staticmethod
    def even_target(core, rank):
        return (core, rank) if core == rank >> 1 else (rank >> 1, rank ^ 2)

    @staticmethod
    def odd_target(core, rank):
        return (core, rank ^ 1) if core == rank >> 1 else (rank >> 1, rank ^ 3)

    def even(self, values, back=False):
        return self.by(values, self.even_target, back)

    def odd(self, values, back=False):
        return self.by(values, self.odd_target, back)


def shards(
    tokens_in,
    token_mask,
    grid_index,
    time_table,
    cotangent,
    w_ada,
    b_ada,
    norm1,
    norm2,
    mask_vector,
    w_qkv,
    w_out,
    w_up,
    b_up,
    w_down,
    b_down,
):
    dp_size, ranks = lax.axis_size(DP), lax.axis_size("tensor")
    dp, rank = lax.axis_index(DP), lax.axis_index("tensor")
    core, quarter = dp & 1, dp >> 1 & 3
    parity = rank & 1
    moves = Moves(dp_size, ranks)
    _, row_count, width = tokens_in.shape
    shard_width = w_out.shape[0]
    hidden = w_up.shape[1]
    cond_width = time_table.shape[1]
    place_of = jnp.stack([quarter, core]).astype(jnp.int32)

    came_grid = moves.swap(grid_index)
    pair_grid = jnp.where(core == 0, jnp.concatenate([grid_index, came_grid]), jnp.concatenate([came_grid, grid_index]))
    here = lax.dynamic_index_in_dim(pair_grid, rank, 0, keepdims=False)
    cond_pre = lax.dynamic_slice(time_table, (here, 0), (1, cond_width))
    cond_low = jax.nn.silu(cond_pre).astype(bf16)
    ada_flat = w_ada.reshape(cond_width, 6 * width)
    modulation = jnp.dot(cond_low, ada_flat, preferred_element_type=f32).reshape(6, width) + b_ada

    starts = jnp.stack([(2 * side + (parity ^ odd)) * row_count for side in (core, 1 - core) for odd in range(2)])
    positions = starts[:, None] + jnp.arange(row_count, dtype=jnp.int32)[None, :]
    lane = jnp.arange(LANES, dtype=jnp.int32)
    half_dim = HEAD_DIM // 2
    frequency = 10000.0 ** (-(lane % half_dim).astype(f32) / half_dim)
    angles = positions.reshape(-1, 1).astype(f32) * frequency[None, :]
    cosine = jnp.cos(angles)
    sine = jnp.sin(angles) * jnp.where(lane % HEAD_DIM < half_dim, -1.0, 1.0)[None, :]

    def quarter_of(values, rows):
        return lax.dynamic_slice_in_dim(values, quarter * rows, rows, 0)

    def along(piece):
        return jnp.stack([moves.even(piece), moves.odd(piece)])

    def across(first, second, *before):
        first_x, second_y = together((moves.flip(first, 1 << 1), moves.flip(second, 2 << 1)), *before)
        one, two = jnp.stack([first, first_x]), jnp.stack([second, second_y])
        return one, two, moves.flip(one, 2 << 1), moves.flip(two, 1 << 1)

    def across_at_once(first, second):
        both = jnp.stack([first, second])
        return [both] + [moves.flip(both, turn << 1) for turn in (1, 2, 3)]

    qkv_rows = shard_width // 4
    qkv_slice = lax.dynamic_slice_in_dim(w_qkv, quarter * qkv_rows, qkv_rows, 2)
    qkv_piece = qkv_slice.transpose(1, 2, 0).reshape(3 * qkv_rows, width)
    attn_piece = jnp.concatenate([qkv_piece, quarter_of(w_out, qkv_rows)])
    up_piece, down_piece = quarter_of(w_up, width // 4), quarter_of(w_down, hidden // 4)
    low_rows = hidden // 4
    low_piece = lax.dynamic_slice_in_dim(w_down, hidden - low_rows + quarter * (low_rows // 4), low_rows // 4, 0)
    odd_piece = jnp.concatenate([up_piece, down_piece])
    even_piece = jnp.concatenate([up_piece, low_piece])
    attn_even, attn_odd = moves.even(attn_piece), moves.odd(attn_piece)

    def sent(values, odd):
        return lax.dynamic_index_in_dim(values, parity ^ odd, 0, keepdims=False)

    mask_rows = jnp.pad(token_mask.astype(bf16), ((0, 0), (0, width - row_count)))[:, None]
    bias_rows = jnp.broadcast_to(split3(b_up)[None], (2, 3, width))
    rest = jnp.zeros((2, EXTRA - 4, width), bf16)
    packs = jnp.concatenate([after(tokens_in, came_grid, attn_piece), mask_rows, bias_rows, rest], axis=1)
    sent_even, sent_odd = sent(packs, 0), sent(packs, 1)
    cot_even, cot_odd = sent(cotangent, 0), sent(cotangent, 1)
    pack_even, pack_odd = moves.even(sent_even), moves.odd(sent_odd)
    attn_even, attn_odd = together(
        (attn_even, attn_odd), odd_piece, even_piece, cot_even, cot_odd, cosine, sine, modulation
    )
    attn_pieces = across(attn_even, attn_odd)
    odd_piece, even_piece = together((odd_piece, even_piece), pack_even, pack_odd)
    ffn_even, ffn_odd = moves.even(even_piece), moves.odd(odd_piece)
    cot_even, cot_odd = together((cot_even, cot_odd), ffn_even, ffn_odd)
    qkv_t, out_rows = place(
        attn_pieces,
        place_of,
        [
            ((shard, index * qkv_rows, qkv_rows), int(index == 3), (None if index == 3 else index, shard * shard_width, qkv_rows))
            for shard in range(2)
            for index in range(4)
        ],
        [like((3, 2 * shard_width, width), bf16), like((2 * shard_width, width), bf16)],
    )

    def bias_of(pack):
        return jnp.sum(pack[row_count + 1 : row_count + 4].astype(f32), axis=0, keepdims=True)

    table = jnp.concatenate(
        [
            modulation,
            norm1[None],
            norm2[None],
            mask_vector[None],
            b_down[None],
            bias_of(pack_even),
            bias_of(pack_odd),
            jnp.zeros((4, width), f32),
        ]
    )

    residual, first_own = enter(pack_even, pack_odd, table)
    first_other = moves.swap(after(first_own, attn_pieces[0], attn_pieces[1]))
    first_other = after(first_other, attn_pieces[2], attn_pieces[3], ffn_even, ffn_odd)
    cot_even, cot_odd, up_even, up_odd = together(
        (cot_even, cot_odd, ffn_even[: width // 4], ffn_odd[: width // 4]), first_other
    )
    cot_even, cot_odd = moves.even(cot_even), moves.odd(cot_odd)
    upstream = jnp.concatenate([cot_even, cot_odd])
    up_pieces = across_at_once(up_even, up_odd)
    queries, keys, values, mixed, log_sum, attn_own, attn_given = attend(
        first_own, first_other, qkv_t, out_rows, cosine, sine
    )
    down_quarter = jnp.concatenate([ffn_odd[width // 4 :], ffn_even[width // 4 :]])
    down_quarter, down_most = together((down_quarter, w_down[: hidden - low_rows]), attn_own)
    attn_came = moves.swap(after(attn_given, cot_even, cot_odd, *up_pieces[1:]))
    down_most = moves.even(down_most)
    down_pieces = [down_quarter] + [moves.flip(down_quarter, turn << 1) for turn in (1, 2, 3)]
    (up_full,) = place(
        up_pieces,
        place_of,
        [((shard, 0, width // 4), 0, (shard, 0, width // 4)) for shard in range(2)],
        [like((2, width, hidden), bf16)],
        steps=1,
    )
    second_res, second_own = second(residual, attn_own, attn_came, table)
    second_other = moves.swap(second_own)
    active_own, bend_own = upper(second_own, table, up_full)
    active_other, bend_other = upper(after(second_other, active_own), table, up_full)
    grad_mlp_own = (modulation[5:6] * upstream.astype(f32)).astype(bf16)
    grad_mlp_other = moves.swap(grad_mlp_own)

    def meet(pieces):
        return add([pieces[0]] + [moves.flip(pieces[turn], turn << 1) for turn in (1, 2, 3)], pieces[0].ndim == 3 and 2 or 1)

    def back(first, second):
        return [moves.even(first, back=True), moves.odd(second, back=True)]

    def share(mine):
        mine = mine + moves.swap(mine)
        for bit in range(3, dp_size.bit_length() - 1):
            mine = mine + moves.flip(mine, 1 << bit)
        return mine

    def spread(mine, *before):
        low = mine.astype(bf16)
        axis = low.ndim - 2
        rows = low.shape[axis] // 2
        kept = lax.dynamic_slice_in_dim(low, core * rows, rows, axis)
        given = lax.dynamic_slice_in_dim(low, (1 - core) * rows, rows, axis)
        came = together(tuple(moves.flip(kept, turn << 1) for turn in (1, 2, 3)), *before)
        back = moves.swap(jnp.stack(came))
        return [kept, given, came[0], back[0], came[1], back[1], came[2], back[2]]

    d_down = ffn_weights(place_of, (active_own, active_other), (grad_mlp_own, grad_mlp_other), True, False)
    down_even, down_odd = place(
        (*together(tuple(down_pieces), d_down[0], down_most), down_most),
        place_of,
        [
            ((0, 0, hidden // 4), 1, (None, 0, hidden // 4)),
            ((0, hidden // 4, low_rows // 4), 0, (None, hidden - low_rows, low_rows // 4)),
        ],
        [like((hidden, width), bf16)] * 2,
        steps=0,
    )
    down_came = [moves.flip(d_down[turn], turn << 1) for turn in (1, 2, 3)]

    grad_mlp_late = after(grad_mlp_other, d_down[0])
    upper_grad_other, *part_given, sum_other = ffn_back(grad_mlp_late, down_even, down_odd, up_full, bend_other)
    part_came = [moves.swap(p) for p in part_given]
    upper_grad_own, *part_own, sum_own = ffn_back(
        after(grad_mlp_own, *part_given), down_even, down_odd, up_full, bend_own
    )
    grad_res, grad_attn_own, sum_middle = middle(
        part_own, part_came, upstream, second_res, attn_own, attn_came, table
    )
    grad_attn_other = moves.swap(grad_attn_own)
    d_up = ffn_weights(
        place_of, (second_own, second_other), (upper_grad_own, after(upper_grad_other, grad_attn_own)), False, False
    )
    down_came = together(tuple(down_came), d_up[0])
    mlp_given = lower(after(active_other, *down_came), down_even, down_odd)
    mlp_came = moves.swap(mlp_given)
    mlp_own = lower(after(active_own, mlp_given), down_even, down_odd)
    down_parts = add([d_down[0], *down_came], 2)
    layer_even, layer_odd, sum_leave = leave(second_res, mlp_own, mlp_came, upstream, down_parts, table)

    def to_ranks(even, odd):
        return jnp.where(parity == 0, jnp.stack([even, odd]), jnp.stack([odd, even]))

    d_up = together(tuple(d_up), layer_even)
    up_came = [moves.flip(d_up[turn], turn << 1) for turn in (1, 2, 3)]
    layer_back = [moves.by(layer_even, moves.even_target, True, True), moves.odd(layer_odd, back=True)]
    d_first, found, rest, finish_back = attend_back(
        place_of,
        after(grad_attn_own, layer_even),
        grad_attn_other,
        first_own,
        first_other,
        qkv_t,
        out_rows,
        cosine,
        sine,
        queries,
        keys,
        values,
        mixed,
        log_sum,
    )
    up_came = together(tuple(up_came), found)
    d_first = together(tuple(d_first), found, *up_came)
    up_parts = add([d_up[0], *up_came], 2)
    first_came = [moves.flip(d_first[turn], turn << 1) for turn in (1, 2, 3)]
    found, rest = together((found, rest), *up_parts)
    d_second, last, first_grads = finish_back(found, rest)
    d_second = together(tuple(d_second), *first_came, *layer_back)
    layer_back = together(tuple(layer_back), last)
    first_parts = add([d_first[0], *first_came])
    second_came = [moves.flip(d_second[turn], turn << 1) for turn in (1, 2, 3)]
    first_part, first_given = first_grads(after(last, d_second[0]))
    first_came = moves.swap(after(first_given, *second_came))
    second_parts = add([d_second[0]] + second_came)
    attn_back = back(first_parts, second_parts)
    first_came = after(first_came, first_parts, second_parts)
    in_even, in_odd, sum_end = end(first_part, first_came, residual, pack_even, pack_odd, grad_res, table)
    up_back = back(*together(tuple(up_parts), *layer_back, sum_end))
    layer_back = together(tuple(layer_back), sum_end)
    layer_back = [jnp.where(core == rank >> 1, layer_even, layer_back[0]), layer_back[1]]
    layer_out = to_ranks(*[p[:row_count] for p in layer_back])
    attn_mine = add(together(tuple(attn_back), sum_end), dtype=f32)
    attn_part = share(attn_mine)
    up_back = together(tuple(up_back), attn_part)
    ffn_part = share(
        jnp.concatenate([add([p[row_count:] for p in layer_back], dtype=f32), add(up_back, dtype=f32)])
    )
    attn_spread = spread(attn_part)
    ffn_spread = spread(ffn_part.reshape(2, -1, width), attn_spread[2], attn_spread[4], attn_spread[6])
    grad_w_down, grad_w_up = finish(ffn_spread, place_of, [(hidden, width), (width, hidden)])
    (grad_attn_rows,) = finish([p[None] for p in attn_spread], place_of, [(4 * shard_width, width)])
    grad_attn_rows = grad_attn_rows.reshape(4, 4, qkv_rows, width)
    grad_w_out = grad_attn_rows[:, 3].reshape(shard_width, width)
    grad_w_qkv = grad_attn_rows[:, :3].transpose(3, 1, 0, 2).reshape(width, 3, shard_width)

    scale_up = 1.0 + modulation
    upper_two = (sum_own[0] + sum_other[0]).reshape(2, hidden)
    upper_two = jnp.where(parity == 1, upper_two[::-1], upper_two)
    blank = jnp.zeros((2, hidden), f32)
    cond_row = jnp.pad(jnp.concatenate([cond_pre[0], here.astype(f32)[None]]), (0, width - cond_width - 1))
    cond_row = jnp.where(core == 0, cond_row, 0.0)
    rows = jnp.concatenate(
        [
            jnp.stack(
                [
                    sum_end[0],
                    sum_end[1] * norm1,
                    sum_middle[2],
                    sum_middle[0],
                    sum_middle[1] * norm2,
                    sum_leave[0],
                    cond_row,
                    sum_end[1] * scale_up[1],
                    sum_end[2],
                    sum_middle[1] * scale_up[4],
                    sum_leave[1],
                ]
            ),
            jnp.where(core == 0, upper_two, blank),
            jnp.where(core == 0, blank, upper_two),
        ]
    )
    rows = rows + moves.swap(rows)
    each, sums = rows[:7], rows[7:]
    steps = [(moves.flip, 1 << bit, dp >> bit & 1) for bit in range(1, dp_size.bit_length() - 1)]
    steps += [(moves.flip_rank, bit, rank >> bit & 1) for bit in range(ranks.bit_length() - 1)]
    for move, which, ahead in steps:
        came = move(jnp.concatenate([each, sums]), which)
        sums = sums + came[each.shape[0] :]
        came = came[: each.shape[0]]
        each = jnp.where(ahead == 1, jnp.concatenate([came, each]), jnp.concatenate([each, came]))
        if move == moves.flip_rank and which == 0:
            in_back = back(*together((in_even, in_odd), came))
    each, sums = together((each, sums), ffn_spread[2], ffn_spread[4], ffn_spread[6])
    grad_in = to_ranks(*together(tuple(in_back), ffn_spread[2], ffn_spread[4], ffn_spread[6]))
    each = each.reshape(-1, 7, width)
    grad_mods = each[:, :6]
    cond_all = each[:, 6, :cond_width]
    grid_all = each[:, 6, cond_width].astype(jnp.int32)
    grad_b_up = lax.dynamic_index_in_dim(sums[4:], rank, 0, keepdims=False)

    points = time_table.shape[0]
    onehot = (grid_all[:, None] == jnp.arange(points, dtype=jnp.int32)[None, :]).astype(f32)
    cond_act, silu_back = jax.vjp(jax.nn.silu, cond_all)
    cond_act = cond_act.astype(bf16).astype(f32)
    grad_flat = grad_mods.reshape(-1, 6 * width)
    grad_w_ada = jnp.dot(cond_act.T, grad_flat, precision=highest).reshape(cond_width, 6, width)
    grad_b_ada = jnp.sum(grad_mods, axis=0)
    grad_cond = jnp.dot(grad_flat, ada_flat.astype(f32).T, precision=highest)
    grad_pre = silu_back(grad_cond)[0]
    grad_table = jnp.dot(onehot.T, grad_pre, precision=highest)
    return (
        layer_out,
        grad_in,
        grad_table,
        sums[1],
        grad_w_ada,
        grad_b_ada,
        sums[0],
        sums[2],
        grad_w_qkv,
        grad_w_out,
        grad_w_up,
        grad_b_up,
        grad_w_down,
        sums[3],
    )


def solution(mesh):
    parts = (mesh.shape["dp"] // 8, 2, 2, 2, mesh.shape["tensor"])
    finer = jax.sharding.Mesh(mesh.devices.reshape(parts), AXES)
    whole = P()
    split = P(DP, "tensor", None)
    weights = (P(None, None, "tensor"), P("tensor", None), P(None, "tensor"), P("tensor"), P("tensor", None), whole)
    return jax.shard_map(
        shards,
        mesh=finer,
        in_specs=(split, P(DP, "tensor"), P(DP), whole, split) + (whole,) * 5 + weights,
        out_specs=(split, split) + (whole,) * 6 + weights,
        check_vma=False,
    )
```

```python
import functools

import jax
import jax.numpy as jnp
from jax import lax
from jax.experimental import pallas as pl
from jax.experimental.pallas import tpu as pltpu
from jax.sharding import PartitionSpec as P

HEAD_DIM = 64
LANES = 128
EXTRA = 16
f32 = jnp.float32
bf16 = jnp.bfloat16
highest = lax.Precision.HIGHEST
NN = (((1,), (0,)), ((), ()))
NT = (((1,), (1,)), ((), ()))
TN = (((0,), (0,)), ((), ()))
DP = ("r", "y", "x", "c")
AXES = DP + ("tensor",)
MIB = 2**20
SHARE = 64

SHIFT1, SCALE1, GATE1, SHIFT2, SCALE2, GATE2, NORM1, NORM2, MASKED, B_DOWN, B_UP = range(11)


def dot(left, right, dims=NN):
    return lax.dot_general(left, right, dims, preferred_element_type=f32)


def row(table, index):
    return table[index : index + 1, :]


def full(shape):
    return pl.BlockSpec(shape, lambda *i: (0,) * len(shape))


def by_rows(size, width):
    return pl.BlockSpec((size, width), lambda i: (i, 0))


def like(shape, dtype):
    return jax.ShapeDtypeStruct(shape, dtype)


def call(body, grid, ins, specs, outs, out_specs, scratch=(), mib=24, flops=0, special=0, name=None):
    moved = sum(x.size * x.dtype.itemsize for x in ins) + sum(x.size * x.dtype.itemsize for x in outs)
    return pl.pallas_call(
        body,
        grid=(grid,),
        in_specs=specs,
        out_specs=out_specs,
        out_shape=outs,
        scratch_shapes=list(scratch),
        name=name,
        compiler_params=pltpu.CompilerParams(vmem_limit_bytes=mib * MIB),
        cost_estimate=pl.CostEstimate(flops=flops // SHARE, bytes_accessed=moved // SHARE, transcendentals=special // SHARE),
    )(*ins)


def centered(values):
    average = jnp.mean(values, axis=-1, keepdims=True)
    away = values - average
    inverse = lax.rsqrt(jnp.mean(away * away, axis=-1, keepdims=True) + 1e-05)
    return away * inverse, inverse


def norm_back(grads, hat, inverse, factor):
    slope = grads * factor
    lean = jnp.mean(slope, axis=-1, keepdims=True)
    tilt = jnp.mean(slope * hat, axis=-1, keepdims=True)
    return (slope - lean - hat * tilt) * inverse


def after(values, *others):
    return lax.optimization_barrier((values,) + others)[0]


def together(values, *others):
    return lax.optimization_barrier(values + others)[: len(values)]


def over_rows(values):
    return jnp.sum(values, axis=0, keepdims=True)


def mask_column(extra):
    count = extra.shape[1] // LANES * LANES
    line = extra[0:1, :].astype(f32)
    return jnp.broadcast_to(line, (LANES, count)).T[:, 0:1]


def place_kernel(plan, steps, place_of, *refs):
    count = 5 if steps == 0 else 4
    (one, two, first_y, second_x), outs = refs[:4], refs[count:]
    if steps == 0:
        shards_of = (tuple((piece, None) for piece in refs[:4]),)
        outs[0][: refs[4].shape[0], :] = refs[4][...]
    elif steps == 1:
        shards_of = tuple(tuple((piece, shard) for piece in refs[:4]) for shard in range(2))
    else:
        shards_of = (((one, 0), (one, 1), (first_y, 0), (first_y, 1)), ((two, 0), (second_x, 0), (two, 1), (second_x, 1)))
    for turn in range(4):
        here = place_of[0] ^ turn
        for (shard, start, size), out, (lead, base, pitch) in plan:
            piece, index = shards_of[shard][turn]
            rows = pl.ds(pl.multiple_of(base + here * pitch, 16), size)
            where = (rows, slice(None)) if lead is None else (lead, rows, slice(None))
            rows_of = slice(start, start + size)
            outs[out][where] = piece[rows_of, :] if index is None else piece[index, rows_of, :]


def place(pieces, place_of, plan, outs, steps=2):
    moved = sum(2 * x.size * x.dtype.itemsize for x in outs)
    return pl.pallas_call(
        functools.partial(place_kernel, plan, steps),
        in_specs=[pl.BlockSpec(memory_space=pltpu.SMEM)] + [pl.BlockSpec(memory_space=pltpu.VMEM)] * len(pieces),
        out_specs=[pl.BlockSpec(memory_space=pltpu.VMEM)] * len(outs),
        out_shape=outs,
        name="place",
        compiler_params=pltpu.CompilerParams(vmem_limit_bytes=12 * MIB),
        cost_estimate=pl.CostEstimate(flops=0, bytes_accessed=moved // SHARE, transcendentals=0),
    )(place_of, *pieces)


def finish_kernel(place_of, *refs):
    pieces, outs = refs[:8], refs[8:]
    step, core = pl.program_id(0), place_of[1]
    size = pieces[0].shape[1]
    for turn in range(4):

        @pl.when(step == turn)
        def _(turn=turn):
            for side in range(2):
                rows = pl.ds(pl.multiple_of((core ^ side) * size, 8), size)
                for index, out in enumerate(outs):
                    out[rows, :] = pieces[2 * turn + side][index].astype(f32)


def finish(pieces, place_of, shapes):
    return pl.pallas_call(
        finish_kernel,
        grid_spec=pltpu.PrefetchScalarGridSpec(
            num_scalar_prefetch=1,
            grid=(4,),
            in_specs=[pl.BlockSpec(p.shape, lambda i, at: (0, 0, 0)) for p in pieces],
            out_specs=[pl.BlockSpec((rows // 4, width), lambda i, at: (at[0] ^ i, 0)) for rows, width in shapes],
        ),
        out_shape=[like(shape, f32) for shape in shapes],
        name="finish",
        compiler_params=pltpu.CompilerParams(vmem_limit_bytes=24 * MIB),
    )(place_of, *pieces)


def enter_kernel(even, odd, table, residual, first):
    rows = even.shape[0] - EXTRA
    for index, pack in enumerate((even, odd)):
        here = slice(index * rows, (index + 1) * rows)
        mask = mask_column(pack[rows:, :rows])
        values = pack[:rows, :].astype(f32) + mask * row(table, MASKED)
        residual[here, :] = values
        hat, _ = centered(values)
        factor = row(table, NORM1) * (1.0 + row(table, SCALE1))
        first[here, :] = (hat * factor + row(table, SHIFT1)).astype(bf16)


def enter(even, odd, table):
    rows, width = 2 * (even.shape[0] - EXTRA), even.shape[1]
    return call(
        enter_kernel,
        1,
        (even, odd, table),
        [full(even.shape), full(odd.shape), full(table.shape)],
        [like((rows, width), f32), like((rows, width), bf16)],
        [full((rows, width))] * 2,
        name="enter",
    )


def partner(values):
    lane = lax.broadcasted_iota(jnp.int32, values.shape, 1)
    ahead = pltpu.roll(values, LANES - HEAD_DIM // 2, 1)
    behind = pltpu.roll(values, HEAD_DIM // 2, 1)
    return jnp.where(lane % HEAD_DIM < HEAD_DIM // 2, ahead, behind)


def heads_of(values):
    lane = lax.broadcasted_iota(jnp.int32, values.shape, 1)
    return lane < HEAD_DIM


def attend_kernel(
    own, other, weights, w_out, cosine, sine, queries, keys, values, mixed, log_sum, part_own, part_other, total
):
    step = pl.program_id(0)
    half = own.shape[0]
    length = 2 * half
    chunk = 256
    for index, tokens in enumerate((own, other)):
        here = slice(index * half, (index + 1) * half)
        query = dot(tokens[...], weights[0], NT)
        turned = (query * cosine[here, :] + partner(query) * sine[here, :]).astype(bf16)
        queries[here, :] = (turned * HEAD_DIM**-0.5).astype(bf16)
        key = dot(tokens[...], weights[1], NT)
        keys[here, :] = (key * cosine[here, :] + partner(key) * sine[here, :]).astype(bf16)
        values[here, :] = dot(tokens[...], weights[2], NT).astype(bf16)

    @pl.when(step == 0)
    def _():
        total[...] = jnp.zeros_like(total)

    every_key, every_value = keys[...], values[...]
    items = [(start, head) for start in range(0, length, chunk) for head in range(2)]

    def score(start, head):
        block = queries[pl.ds(start, chunk), :]
        former = heads_of(block)
        return dot(jnp.where(former if head == 0 else ~former, block, 0), every_key, NT)

    following = score(*items[0])
    halves = []
    for index, (start, head) in enumerate(items):
        scores = following
        if index + 1 < len(items):
            following = score(*items[index + 1])
        top = jnp.max(scores, axis=1, keepdims=True)
        powers = jnp.exp(scores - top)
        sums = jnp.sum(powers, axis=1, keepdims=True)
        halves.append((dot(powers.astype(bf16), every_value) * (1.0 / sums), top + jnp.log(sums)))
        if head == 1:
            here = pl.ds(start, chunk)
            former = heads_of(halves[0][0])
            out = jnp.where(former, halves[0][0], halves[1][0])
            mixed[here, :] = out
            log_sum[here, :] = jnp.where(former, halves[0][1], halves[1][1])
            total[here, :] += dot(out.astype(bf16), w_out[...])
            halves = []

    @pl.when(step == pl.num_programs(0) - 1)
    def _():
        part_own[...] = total[:half, :].astype(bf16)
        part_other[...] = total[half:, :].astype(bf16)


def attend(own, other, weights, w_out, cosine, sine):
    half, width = own.shape
    length = 2 * half
    wide = w_out.shape[0]
    tall = pl.BlockSpec((length, LANES), lambda i: (0, i))
    return call(
        attend_kernel,
        wide // LANES,
        (own, other, weights, w_out, cosine, sine),
        [
            full(own.shape),
            full(own.shape),
            pl.BlockSpec((3, LANES, width), lambda i: (0, i, 0)),
            pl.BlockSpec((LANES, width), lambda i: (i, 0)),
            full(cosine.shape),
            full(sine.shape),
        ],
        [like((length, wide), bf16)] * 3 + [like((length, wide), f32)] * 2 + [like((half, width), bf16)] * 2,
        [tall] * 5 + [full((half, width))] * 2,
        [pltpu.VMEM((length, width), f32)],
        mib=36,
        flops=8 * length * width * wide + 16 * length * length * wide,
        special=length * length * wide // HEAD_DIM,
        name="attend",
    )


def pair_back(grads_own, grads_other, own, other, w_out, cosine, sine, queries, keys, values, mixed, log_sum):
    half = own.shape[0]
    length = 2 * half
    chunk = 256
    outs = mixed[...]
    low = outs.astype(bf16)
    grad = jnp.concatenate([dot(grads_own[...], w_out[...], NT), dot(grads_other[...], w_out[...], NT)]).astype(bf16)
    d_out = dot(low[:half], grads_own[...], TN) + dot(low[half:], grads_other[...], TN)
    lean_t = (grad.astype(f32) * outs).T
    log_t = log_sum[...].T
    query, key, value = queries[...], keys[...], values[...]
    former = heads_of(query)
    former_chunk = heads_of(query[:chunk])
    items = [(head, start) for head in range(2) for start in range(0, length, chunk)]

    def products(head, start):
        mine = former_chunk if head == 0 else ~former_chunk
        key_rows = jnp.where(mine, key[start : start + chunk], 0)
        value_rows = jnp.where(mine, value[start : start + chunk], 0)
        return dot(key_rows, query, NT), dot(value_rows, grad, NT)

    found_q, found_k, found_v = [None, None], ([], []), ([], [])

    def collect(head, start, probs, slopes):
        found_v[head].append(dot(probs, grad))
        found_k[head].append(dot(slopes, query))
        more = dot(key[start : start + chunk], slopes, TN)
        found_q[head] = more if found_q[head] is None else found_q[head] + more

    following, pending = products(*items[0]), None
    for index, (head, start) in enumerate(items):
        scores, against = following
        if index + 1 < len(items):
            following = products(*items[index + 1])
        if pending is not None:
            collect(*pending)
        lean = over_rows(lean_t[head * HEAD_DIM : (head + 1) * HEAD_DIM])
        probs = jnp.exp(scores - log_t[head * HEAD_DIM : head * HEAD_DIM + 1])
        pending = (head, start, probs.astype(bf16), (probs * (against - lean)).astype(bf16))
    collect(*pending)
    row_head = lax.broadcasted_iota(jnp.int32, found_q[0].shape, 0)
    d_query = jnp.where(row_head < HEAD_DIM, found_q[0], found_q[1]).T * HEAD_DIM**-0.5
    d_key = jnp.where(former, jnp.concatenate(found_k[0]), jnp.concatenate(found_k[1]))
    d_value = jnp.where(former, jnp.concatenate(found_v[0]), jnp.concatenate(found_v[1])).astype(bf16)
    d_query = (d_query * cosine[...] + partner(d_query * sine[...])).astype(bf16)
    d_key = (d_key * cosine[...] + partner(d_key * sine[...])).astype(bf16)
    found = (d_query, d_key, d_value)
    return found, [dot(g[:half], own[...], TN) + dot(g[half:], other[...], TN) for g in found] + [d_out]


def put_pieces(pieces, rows_of_weight, quarter, size):
    for turn, piece in enumerate(pieces):
        rows = pl.ds(pl.multiple_of((quarter ^ turn) * size, 16), size)
        for index in range(4):
            piece[index * size : (index + 1) * size, :] = rows_of_weight[index, rows, :]


def attend_back_kernel(shard_rows, place_of, *refs):
    ins, (found_all, *pieces), rest, d_weights = refs[:12], refs[12:17], refs[17], refs[18]
    step = pl.program_id(0)
    found, rows = pair_back(*ins)
    here = pl.ds(pl.multiple_of(step * LANES, LANES), LANES)
    for index in range(3):
        found_all[index] = found[index]
    for index in range(4):
        d_weights[index, here, :] = rows[index].astype(bf16)

    @pl.when(step == pl.num_programs(0) - 1)
    def _():
        put_pieces(pieces, d_weights, place_of[0], shard_rows // 4)
        rest[...] = d_weights[:, shard_rows:, :]


def attend_back_end_kernel(shard_rows, place_of, rows_before, *refs):
    ins, (found_all, *pieces), d_weights = refs[:12], refs[12:17], refs[17]
    found, rows = pair_back(*ins)
    start = rows_before.shape[1]
    d_weights[:, :start, :] = rows_before[...]
    for index in range(3):
        found_all[index] = found[index]
    for index in range(4):
        d_weights[index, start:, :] = rows[index].astype(bf16)
    put_pieces(pieces, d_weights, place_of[0], shard_rows // 4)


def first_grads_kernel(before, last, weights, part_own, part_other):
    step, wide = pl.program_id(0), before.shape[2]
    total = dot(last[0], weights[0, wide:, :])
    total += dot(last[1], weights[1, wide:, :]) + dot(last[2], weights[2, wide:, :])
    for index in range(3):
        total += dot(before[index], weights[index, :wide, :])
    result = total.astype(bf16)

    @pl.when(step == 0)
    def _():
        part_other[...] = result

    @pl.when(step == 1)
    def _():
        part_own[...] = result


def attend_back(place_of, grads_own, grads_other, own, other, weights, w_out, cosine, sine, *kept):
    half, width = own.shape
    length = 2 * half
    wide = w_out.shape[0]
    shard_rows = wide // 2
    first = -(-shard_rows // LANES)
    rows = full((half, width))
    quarter = like((shard_rows, width), bf16)
    smem = pl.BlockSpec(memory_space=pltpu.SMEM)

    def specs(base):
        tall = pl.BlockSpec((length, LANES), lambda i: (0, i + base))
        flat = pl.BlockSpec((LANES, width), lambda i: (i + base, 0))
        return [rows] * 4 + [flat, full(cosine.shape), full(sine.shape)] + [tall] * 5

    ins = (grads_own, grads_other, own, other, w_out, cosine, sine) + kept
    work = dict(flops=14 * length * width * LANES + 40 * length * length * LANES, special=2 * length * length)
    found, *pieces, rest = call(
        functools.partial(attend_back_kernel, shard_rows),
        first,
        (place_of,) + ins,
        [smem] + specs(0),
        [like((3, length, first * LANES), bf16)] + [quarter] * 4 + [like((4, first * LANES - shard_rows, width), bf16)],
        [pl.BlockSpec((3, length, LANES), lambda i: (0, 0, i))]
        + [full(quarter.shape)] * 4
        + [full((4, first * LANES - shard_rows, width))],
        [pltpu.VMEM((4, first * LANES, width), bf16)],
        mib=60,
        name="attend_back",
        **work,
    )

    def finish_back(found, rest):
        last, *more = call(
            functools.partial(attend_back_end_kernel, shard_rows),
            1,
            (place_of, rest) + ins,
            [smem, full(rest.shape)] + specs(first),
            [like((3, length, LANES), bf16)] + [quarter] * 4,
            [full((3, length, LANES))] + [full(quarter.shape)] * 4,
            [pltpu.VMEM((4, shard_rows, width), bf16)],
            mib=60,
            name="attend_back_end",
            **work,
        )

        def first_grads(last):
            return call(
                first_grads_kernel,
                2,
                (found, last, weights),
                [
                    pl.BlockSpec((3, half, found.shape[2]), lambda i: (0, 1 - i, 0)),
                    pl.BlockSpec((3, half, LANES), lambda i: (0, 1 - i, 0)),
                    full(weights.shape),
                ],
                [like((half, width), bf16)] * 2,
                [rows] * 2,
                mib=60,
        name="first_grads",
            )

        return more, last, first_grads

    return pieces, found, rest, finish_back


def lift(inner, table, w_up, active, bend):
    hidden = w_up.shape[2]
    root = 0.7978845608028654
    for block in range(2):
        span = slice(block * hidden, (block + 1) * hidden)
        u = dot(inner, w_up[block]) + table[B_UP + block : B_UP + block + 1, :hidden]
        square = u * u
        curve = jnp.tanh(root * (u + 0.044715 * (square * u)))
        rise = 0.5 + 0.5 * curve
        active[:, span] = (u * rise).astype(bf16)
        slope = rise + (0.5 * root) * u * (1.0 - curve * curve) * (1.0 + 0.134145 * square)
        bend[:, span] = slope.astype(bf16)


def second_kernel(residual, mine, came, table, second_res, second):
    values = residual[...] + row(table, GATE1) * (mine[...].astype(f32) + came[...].astype(f32))
    second_res[...] = values
    hat, _ = centered(values)
    factor = row(table, NORM2) * (1.0 + row(table, SCALE2))
    second[...] = (hat * factor + row(table, SHIFT2)).astype(bf16)


def second(residual, mine, came, table, size=256):
    rows, width = residual.shape
    spec = by_rows(size, width)
    return call(
        second_kernel,
        rows // size,
        (residual, mine, came, table),
        [spec, spec, spec, full(table.shape)],
        [like((rows, width), f32), like((rows, width), bf16)],
        [spec, spec],
        flops=10 * rows * width,
        name="second",
    )


def upper_kernel(inner, table, w_up, active, bend):
    lift(inner[...], table, w_up, active, bend)


def upper(inner, table, w_up, size=256):
    rows, width = inner.shape
    hidden = 2 * w_up.shape[2]
    broad = by_rows(size, hidden)
    return call(
        upper_kernel,
        rows // size,
        (inner, table, w_up),
        [by_rows(size, width), full(table.shape), full(w_up.shape)],
        [like((rows, hidden), bf16)] * 2,
        [broad, broad],
        flops=2 * rows * width * hidden,
        special=rows * hidden,
        name="upper",
    )


def ffn_back_kernel(grad_mlp, down_even, down_odd, w_up, bend, grad_upper, *refs):
    parts, sums = refs[:-1], refs[-1]
    step = pl.program_id(0)
    grad = jnp.concatenate([dot(grad_mlp[...], down[...], NT) for down in (down_even, down_odd)], axis=1)
    grad = (grad * bend[...].astype(f32)).astype(bf16)
    grad_upper[...] = grad
    hidden = w_up.shape[2]
    result = (dot(grad[:, :hidden], w_up[0], NT) + dot(grad[:, hidden:], w_up[1], NT)).astype(bf16)
    for index, part in enumerate(parts):

        @pl.when(step == index)
        def _(part=part):
            part[...] = result

    @pl.when(step == 0)
    def _():
        sums[...] = jnp.zeros_like(sums)

    sums[0:1, :] += over_rows(grad.astype(f32))


def ffn_back(grad_mlp, down_even, down_odd, w_up, bend, size=256):
    rows, width = grad_mlp.shape
    hidden = 2 * down_even.shape[0]
    spec, broad = by_rows(size, width), by_rows(size, hidden)
    return call(
        ffn_back_kernel,
        rows // size,
        (grad_mlp, down_even, down_odd, w_up, bend),
        [spec, full(down_even.shape), full(down_odd.shape), full(w_up.shape), broad],
        [like((rows, hidden), bf16)] + [like((size, width), bf16)] * (rows // size) + [like((8, hidden), f32)],
        [broad] + [full((size, width))] * (rows // size) + [full((8, hidden))],
        flops=4 * rows * width * hidden,
        name="ffn_back",
    )


def ffn_weights_kernel(place_of, left_own, left_other, right_own, right_other, *refs):
    pieces, whole = refs[:-1], refs[-1]
    whole[...] = (dot(left_own[...], right_own[...], TN) + dot(left_other[...], right_other[...], TN)).astype(bf16)
    size = whole.shape[0] // 4
    if len(pieces) == 1:
        for index in range(4):
            pieces[0][index, 0] = whole[index * size : (index + 1) * size, :]
        return
    for turn, piece in enumerate(pieces):
        rows = pl.ds(pl.multiple_of((place_of[0] ^ turn) * size, 16), size)
        piece[0] = whole[rows, :]


def ffn_weights(place_of, left, right, split_left, ordered):
    rows, width = right[0].shape if split_left else left[0].shape
    hidden = (left if split_left else right)[0].shape[1] // 2
    whole, halved = full((rows, width)), pl.BlockSpec((rows, hidden), lambda i: (0, i))
    lefts, rights = (halved, whole) if split_left else (whole, halved)
    shape = (hidden, width) if split_left else (width, hidden)
    size = shape[0] // 4
    if ordered:
        outs, specs = [(4, 2, size, shape[1])], [pl.BlockSpec((4, 1, size, shape[1]), lambda i: (0, i, 0, 0))]
    else:
        outs, specs = [(2, size, shape[1])] * 4, [pl.BlockSpec((1, size, shape[1]), lambda i: (i, 0, 0))] * 4
    return call(
        ffn_weights_kernel,
        2,
        (place_of,) + tuple(left) + tuple(right),
        [pl.BlockSpec(memory_space=pltpu.SMEM), lefts, lefts, rights, rights],
        [like(out, bf16) for out in outs],
        specs,
        [pltpu.VMEM(shape, bf16)],
        flops=8 * rows * width * hidden,
        name="ffn_weights",
    )


def sum_kernel(count, *refs):
    pieces, outs = refs[:count], refs[count:]
    for index, out in enumerate(outs):
        values = [p[...] if len(p.shape) == 2 else p[index] for p in pieces]
        out[...] = sum(v.astype(f32) for v in values).astype(out.dtype)


def add(pieces, count=1, dtype=bf16):
    shape = pieces[0].shape[-2:]
    result = pl.pallas_call(
        functools.partial(sum_kernel, len(pieces)),
        in_specs=[pl.BlockSpec(memory_space=pltpu.VMEM)] * len(pieces),
        out_specs=[pl.BlockSpec(memory_space=pltpu.VMEM)] * count,
        out_shape=[like(shape, dtype)] * count,
        name="add",
        compiler_params=pltpu.CompilerParams(vmem_limit_bytes=12 * MIB),
    )(*pieces)
    return result if count > 1 else result[0]


def middle_kernel(parts, *refs):
    mine, came = refs[:parts], refs[parts : 2 * parts]
    upstream, second_res, attn_mine, attn_came, table, grad_res, grad_attn, sums = refs[2 * parts :]
    step = pl.program_id(0)
    grad = mine[0][...].astype(f32) + came[0][...].astype(f32)
    for index in range(1, parts):
        grad = jnp.where(step == index, mine[index][...].astype(f32) + came[index][...].astype(f32), grad)
    hat, inverse = centered(second_res[...])
    factor = row(table, NORM2) * (1.0 + row(table, SCALE2))
    result = upstream[...].astype(f32) + norm_back(grad, hat, inverse, factor)
    grad_res[...] = result
    grad_attn[...] = (row(table, GATE1) * result).astype(bf16)

    @pl.when(step == 0)
    def _():
        sums[...] = jnp.zeros_like(sums)

    attn = attn_mine[...].astype(f32) + attn_came[...].astype(f32)
    sums[0:1, :] += over_rows(grad)
    sums[1:2, :] += over_rows(grad * hat)
    sums[2:3, :] += over_rows(result * attn)


def middle(mine, came, upstream, second_res, attn_mine, attn_came, table, size=256):
    rows, width = upstream.shape
    spec = by_rows(size, width)
    return call(
        functools.partial(middle_kernel, len(mine)),
        rows // size,
        (*mine, *came, upstream, second_res, attn_mine, attn_came, table),
        [full((size, width))] * (2 * len(mine)) + [spec] * 4 + [full(table.shape)],
        [like((rows, width), f32), like((rows, width), bf16), like((8, width), f32)],
        [spec, spec, full((8, width))],
        flops=40 * rows * width,
        name="middle",
    )


def lower_kernel(active, down_even, down_odd, part):
    half = down_even.shape[0]
    part[...] = (dot(active[:, :half], down_even[...]) + dot(active[:, half:], down_odd[...])).astype(bf16)


def lower(active, down_even, down_odd, size=256):
    rows, hidden = active.shape
    width = down_even.shape[1]
    return call(
        lower_kernel,
        rows // size,
        (active, down_even, down_odd),
        [by_rows(size, hidden), full(down_even.shape), full(down_odd.shape)],
        [like((rows, width), bf16)],
        [by_rows(size, width)],
        flops=2 * rows * hidden * width,
        name="lower",
    )[0]


def leave_kernel(second_res, mine, came, upstream, part_even, part_odd, table, even, odd, sums):
    mlp = mine[...].astype(f32) + came[...].astype(f32) + row(table, B_DOWN)
    layer = (second_res[...] + row(table, GATE2) * mlp).astype(bf16)
    rows = layer.shape[0] // 2
    even[:rows, :] = layer[:rows]
    odd[:rows, :] = layer[rows:]
    even[rows:, :] = part_even[...]
    odd[rows:, :] = part_odd[...]
    grads = upstream[...].astype(f32)
    sums[...] = jnp.zeros_like(sums)
    sums[0:1, :] = over_rows(grads * mlp)
    sums[1:2, :] = over_rows((row(table, GATE2) * grads).astype(bf16).astype(f32))


def leave(second_res, mine, came, upstream, parts, table):
    rows, width = upstream.shape
    spec, part = full((rows, width)), full(parts[0].shape)
    out = (rows // 2 + parts[0].shape[0], width)
    return call(
        leave_kernel,
        1,
        (second_res, mine, came, upstream, *parts, table),
        [spec] * 4 + [part] * 2 + [full(table.shape)],
        [like(out, bf16)] * 2 + [like((8, width), f32)],
        [full(out)] * 2 + [full((8, width))],
        flops=6 * rows * width,
        name="leave",
    )


def end_kernel(mine, came, residual, pack_even, pack_odd, grad_res, table, even, odd, sums):
    step, rows = pl.program_id(0), even.shape[0]
    factor = row(table, NORM1) * (1.0 + row(table, SCALE1))
    mask = jnp.where(step == 0, mask_column(pack_even[:, :rows]), mask_column(pack_odd[:, :rows]))
    grad = mine[...].astype(f32) + came[...].astype(f32)
    hat, inverse = centered(residual[...])
    result = grad_res[...] + norm_back(grad, hat, inverse, factor)
    low = result.astype(bf16)

    @pl.when(step == 0)
    def _():
        even[...] = low
        sums[...] = jnp.zeros_like(sums)

    @pl.when(step == 1)
    def _():
        odd[...] = low

    sums[0:1, :] += over_rows(grad)
    sums[1:2, :] += over_rows(grad * hat)
    sums[2:3, :] += over_rows(result * mask)


def end(mine, came, residual, pack_even, pack_odd, grad_res, table):
    rows, width = mine.shape[0] // 2, mine.shape[1]
    spec = by_rows(rows, width)
    extra = pl.BlockSpec((EXTRA, width), lambda i: (rows // EXTRA, 0))
    return call(
        end_kernel,
        2,
        (mine, came, residual, pack_even, pack_odd, grad_res, table),
        [spec, spec, spec, extra, extra, spec, full(table.shape)],
        [like((rows, width), bf16)] * 2 + [like((8, width), f32)],
        [full((rows, width))] * 2 + [full((8, width))],
        flops=60 * rows * width,
        mib=60,
        name="end",
    )


def split3(values):
    high = lax.reduce_precision(values, 8, 7)
    rest = values - high
    middle_term = lax.reduce_precision(rest, 8, 7)
    return jnp.stack([high, middle_term, rest - middle_term]).astype(bf16)


class Moves:
    def __init__(self, dp_size, rank_size):
        self.dp_size, self.rank_size = dp_size, rank_size

    def by(self, values, target, back=False, away=False):
        pairs = []
        for dp in range(self.dp_size):
            for rank in range(self.rank_size):
                core, to_rank = target(dp & 1, rank)
                pair = (dp * self.rank_size + rank, (dp >> 1 << 1 | core) * self.rank_size + to_rank)
                if not away or pair[0] != pair[1]:
                    pairs.append(pair[::-1] if back else pair)
        return lax.ppermute(values, AXES, pairs)

    def flip(self, values, mask):
        pairs = [
            (dp * self.rank_size + rank, (dp ^ mask) * self.rank_size + rank)
            for dp in range(self.dp_size)
            for rank in range(self.rank_size)
        ]
        return lax.ppermute(values, AXES, pairs)

    def swap(self, values):
        return self.flip(values, 1)

    def flip_rank(self, values, bit):
        return self.by(values, lambda core, rank: (core, rank ^ 1 << bit))

    @staticmethod
    def even_target(core, rank):
        return (core, rank) if core == rank >> 1 else (rank >> 1, rank ^ 2)

    @staticmethod
    def odd_target(core, rank):
        return (core, rank ^ 1) if core == rank >> 1 else (rank >> 1, rank ^ 3)

    def even(self, values, back=False):
        return self.by(values, self.even_target, back)

    def odd(self, values, back=False):
        return self.by(values, self.odd_target, back)


def shards(
    tokens_in,
    token_mask,
    grid_index,
    time_table,
    cotangent,
    w_ada,
    b_ada,
    norm1,
    norm2,
    mask_vector,
    w_qkv,
    w_out,
    w_up,
    b_up,
    w_down,
    b_down,
):
    dp_size, ranks = lax.axis_size(DP), lax.axis_size("tensor")
    dp, rank = lax.axis_index(DP), lax.axis_index("tensor")
    core, quarter = dp & 1, dp >> 1 & 3
    parity = rank & 1
    moves = Moves(dp_size, ranks)
    _, row_count, width = tokens_in.shape
    shard_width = w_out.shape[0]
    hidden = w_up.shape[1]
    cond_width = time_table.shape[1]
    place_of = jnp.stack([quarter, core]).astype(jnp.int32)

    came_grid = moves.swap(grid_index)
    pair_grid = jnp.where(core == 0, jnp.concatenate([grid_index, came_grid]), jnp.concatenate([came_grid, grid_index]))
    here = lax.dynamic_index_in_dim(pair_grid, rank, 0, keepdims=False)
    cond_pre = lax.dynamic_slice(time_table, (here, 0), (1, cond_width))
    cond_low = jax.nn.silu(cond_pre).astype(bf16)
    ada_flat = w_ada.reshape(cond_width, 6 * width)
    modulation = jnp.dot(cond_low, ada_flat, preferred_element_type=f32).reshape(6, width) + b_ada

    starts = jnp.stack([(2 * side + (parity ^ odd)) * row_count for side in (core, 1 - core) for odd in range(2)])
    positions = starts[:, None] + jnp.arange(row_count, dtype=jnp.int32)[None, :]
    lane = jnp.arange(LANES, dtype=jnp.int32)
    half_dim = HEAD_DIM // 2
    frequency = 10000.0 ** (-(lane % half_dim).astype(f32) / half_dim)
    angles = positions.reshape(-1, 1).astype(f32) * frequency[None, :]
    cosine = jnp.cos(angles)
    sine = jnp.sin(angles) * jnp.where(lane % HEAD_DIM < half_dim, -1.0, 1.0)[None, :]

    def quarter_of(values, rows):
        return lax.dynamic_slice_in_dim(values, quarter * rows, rows, 0)

    def along(piece):
        return jnp.stack([moves.even(piece), moves.odd(piece)])

    def across(first, second, *before):
        first_x, second_y = together((moves.flip(first, 1 << 1), moves.flip(second, 2 << 1)), *before)
        one, two = jnp.stack([first, first_x]), jnp.stack([second, second_y])
        return one, two, moves.flip(one, 2 << 1), moves.flip(two, 1 << 1)

    def across_at_once(first, second):
        both = jnp.stack([first, second])
        return [both] + [moves.flip(both, turn << 1) for turn in (1, 2, 3)]

    qkv_rows = shard_width // 4
    qkv_slice = lax.dynamic_slice_in_dim(w_qkv, quarter * qkv_rows, qkv_rows, 2)
    qkv_piece = qkv_slice.transpose(1, 2, 0).reshape(3 * qkv_rows, width)
    attn_piece = jnp.concatenate([qkv_piece, quarter_of(w_out, qkv_rows)])
    up_piece, down_piece = quarter_of(w_up, width // 4), quarter_of(w_down, hidden // 4)
    low_rows = hidden // 4
    low_piece = lax.dynamic_slice_in_dim(w_down, hidden - low_rows + quarter * (low_rows // 4), low_rows // 4, 0)
    odd_piece = jnp.concatenate([up_piece, down_piece])
    even_piece = jnp.concatenate([up_piece, low_piece])
    attn_even, attn_odd = moves.even(attn_piece), moves.odd(attn_piece)

    def sent(values, odd):
        return lax.dynamic_index_in_dim(values, parity ^ odd, 0, keepdims=False)

    mask_rows = jnp.pad(token_mask.astype(bf16), ((0, 0), (0, width - row_count)))[:, None]
    bias_rows = jnp.broadcast_to(split3(b_up)[None], (2, 3, width))
    rest = jnp.zeros((2, EXTRA - 4, width), bf16)
    packs = jnp.concatenate([after(tokens_in, came_grid, attn_piece), mask_rows, bias_rows, rest], axis=1)
    sent_even, sent_odd = sent(packs, 0), sent(packs, 1)
    cot_even, cot_odd = sent(cotangent, 0), sent(cotangent, 1)
    pack_even, pack_odd = moves.even(sent_even), moves.odd(sent_odd)
    attn_even, attn_odd = together(
        (attn_even, attn_odd), odd_piece, even_piece, cot_even, cot_odd, cosine, sine, modulation
    )
    attn_pieces = across(attn_even, attn_odd)
    odd_piece, even_piece = together((odd_piece, even_piece), pack_even, pack_odd)
    ffn_even, ffn_odd = moves.even(even_piece), moves.odd(odd_piece)
    cot_even, cot_odd = together((cot_even, cot_odd), ffn_even, ffn_odd)
    qkv_t, out_rows = place(
        attn_pieces,
        place_of,
        [
            ((shard, index * qkv_rows, qkv_rows), int(index == 3), (None if index == 3 else index, shard * shard_width, qkv_rows))
            for shard in range(2)
            for index in range(4)
        ],
        [like((3, 2 * shard_width, width), bf16), like((2 * shard_width, width), bf16)],
    )

    def bias_of(pack):
        return jnp.sum(pack[row_count + 1 : row_count + 4].astype(f32), axis=0, keepdims=True)

    table = jnp.concatenate(
        [
            modulation,
            norm1[None],
            norm2[None],
            mask_vector[None],
            b_down[None],
            bias_of(pack_even),
            bias_of(pack_odd),
            jnp.zeros((4, width), f32),
        ]
    )

    residual, first_own = enter(pack_even, pack_odd, table)
    first_other = moves.swap(after(first_own, attn_pieces[0], attn_pieces[1]))
    first_other = after(first_other, attn_pieces[2], attn_pieces[3], ffn_even, ffn_odd)
    cot_even, cot_odd, up_even, up_odd = together(
        (cot_even, cot_odd, ffn_even[: width // 4], ffn_odd[: width // 4]), first_other
    )
    cot_even, cot_odd = moves.even(cot_even), moves.odd(cot_odd)
    upstream = jnp.concatenate([cot_even, cot_odd])
    up_pieces = across_at_once(up_even, up_odd)
    queries, keys, values, mixed, log_sum, attn_own, attn_given = attend(
        first_own, first_other, qkv_t, out_rows, cosine, sine
    )
    down_quarter = jnp.concatenate([ffn_odd[width // 4 :], ffn_even[width // 4 :]])
    down_quarter, down_most = together((down_quarter, w_down[: hidden - low_rows]), attn_own)
    attn_came = moves.swap(after(attn_given, cot_even, cot_odd, *up_pieces[1:]))
    down_most = moves.even(down_most)
    down_pieces = [down_quarter] + [moves.flip(down_quarter, turn << 1) for turn in (1, 2, 3)]
    (up_full,) = place(
        up_pieces,
        place_of,
        [((shard, 0, width // 4), 0, (shard, 0, width // 4)) for shard in range(2)],
        [like((2, width, hidden), bf16)],
        steps=1,
    )
    second_res, second_own = second(residual, attn_own, attn_came, table)
    second_other = moves.swap(second_own)
    active_own, bend_own = upper(second_own, table, up_full)
    active_other, bend_other = upper(after(second_other, active_own), table, up_full)
    grad_mlp_own = (modulation[5:6] * upstream.astype(f32)).astype(bf16)
    grad_mlp_other = moves.swap(grad_mlp_own)

    def meet(pieces):
        return add([pieces[0]] + [moves.flip(pieces[turn], turn << 1) for turn in (1, 2, 3)], pieces[0].ndim == 3 and 2 or 1)

    def back(first, second):
        return [moves.even(first, back=True), moves.odd(second, back=True)]

    def share(mine):
        mine = mine + moves.swap(mine)
        for bit in range(3, dp_size.bit_length() - 1):
            mine = mine + moves.flip(mine, 1 << bit)
        return mine

    def spread(mine, *before):
        low = mine.astype(bf16)
        axis = low.ndim - 2
        rows = low.shape[axis] // 2
        kept = lax.dynamic_slice_in_dim(low, core * rows, rows, axis)
        given = lax.dynamic_slice_in_dim(low, (1 - core) * rows, rows, axis)
        came = together(tuple(moves.flip(kept, turn << 1) for turn in (1, 2, 3)), *before)
        back = moves.swap(jnp.stack(came))
        return [kept, given, came[0], back[0], came[1], back[1], came[2], back[2]]

    d_down = ffn_weights(place_of, (active_own, active_other), (grad_mlp_own, grad_mlp_other), True, False)
    down_even, down_odd = place(
        (*together(tuple(down_pieces), d_down[0], down_most), down_most),
        place_of,
        [
            ((0, 0, hidden // 4), 1, (None, 0, hidden // 4)),
            ((0, hidden // 4, low_rows // 4), 0, (None, hidden - low_rows, low_rows // 4)),
        ],
        [like((hidden, width), bf16)] * 2,
        steps=0,
    )
    down_came = [moves.flip(d_down[turn], turn << 1) for turn in (1, 2, 3)]

    grad_mlp_late = after(grad_mlp_other, d_down[0])
    upper_grad_other, *part_given, sum_other = ffn_back(grad_mlp_late, down_even, down_odd, up_full, bend_other)
    part_came = [moves.swap(p) for p in part_given]
    upper_grad_own, *part_own, sum_own = ffn_back(
        after(grad_mlp_own, *part_given), down_even, down_odd, up_full, bend_own
    )
    grad_res, grad_attn_own, sum_middle = middle(
        part_own, part_came, upstream, second_res, attn_own, attn_came, table
    )
    grad_attn_other = moves.swap(grad_attn_own)
    d_up = ffn_weights(
        place_of, (second_own, second_other), (upper_grad_own, after(upper_grad_other, grad_attn_own)), False, False
    )
    down_came = together(tuple(down_came), d_up[0])
    mlp_given = lower(after(active_other, *down_came), down_even, down_odd)
    mlp_came = moves.swap(mlp_given)
    mlp_own = lower(after(active_own, mlp_given), down_even, down_odd)
    down_parts = add([d_down[0], *down_came], 2)
    layer_even, layer_odd, sum_leave = leave(second_res, mlp_own, mlp_came, upstream, down_parts, table)

    def to_ranks(even, odd):
        return jnp.where(parity == 0, jnp.stack([even, odd]), jnp.stack([odd, even]))

    d_up = together(tuple(d_up), layer_even)
    up_came = [moves.flip(d_up[turn], turn << 1) for turn in (1, 2, 3)]
    layer_back = [moves.by(layer_even, moves.even_target, True, True), moves.odd(layer_odd, back=True)]
    d_first, found, rest, finish_back = attend_back(
        place_of,
        after(grad_attn_own, layer_even),
        grad_attn_other,
        first_own,
        first_other,
        qkv_t,
        out_rows,
        cosine,
        sine,
        queries,
        keys,
        values,
        mixed,
        log_sum,
    )
    up_came = together(tuple(up_came), found)
    d_first = together(tuple(d_first), found, *up_came)
    up_parts = add([d_up[0], *up_came], 2)
    first_came = [moves.flip(d_first[turn], turn << 1) for turn in (1, 2, 3)]
    found, rest = together((found, rest), *up_parts)
    d_second, last, first_grads = finish_back(found, rest)
    d_second = together(tuple(d_second), *first_came, *layer_back)
    layer_back = together(tuple(layer_back), last)
    first_parts = add([d_first[0], *first_came])
    second_came = [moves.flip(d_second[turn], turn << 1) for turn in (1, 2, 3)]
    first_part, first_given = first_grads(after(last, d_second[0]))
    first_came = moves.swap(after(first_given, *second_came))
    second_parts = add([d_second[0]] + second_came)
    attn_back = back(first_parts, second_parts)
    first_came = after(first_came, first_parts, second_parts)
    in_even, in_odd, sum_end = end(first_part, first_came, residual, pack_even, pack_odd, grad_res, table)
    up_back = back(*together(tuple(up_parts), *layer_back, sum_end))
    layer_back = together(tuple(layer_back), sum_end)
    layer_back = [jnp.where(core == rank >> 1, layer_even, layer_back[0]), layer_back[1]]
    layer_out = to_ranks(*[p[:row_count] for p in layer_back])
    attn_mine = add(together(tuple(attn_back), sum_end), dtype=f32)
    attn_part = share(attn_mine)
    up_back = together(tuple(up_back), attn_part)
    ffn_part = share(
        jnp.concatenate([add([p[row_count:] for p in layer_back], dtype=f32), add(up_back, dtype=f32)])
    )
    attn_spread = spread(attn_part)
    ffn_spread = spread(ffn_part.reshape(2, -1, width), attn_spread[2], attn_spread[4], attn_spread[6])
    grad_w_down, grad_w_up = finish(ffn_spread, place_of, [(hidden, width), (width, hidden)])
    (grad_attn_rows,) = finish([p[None] for p in attn_spread], place_of, [(4 * shard_width, width)])
    grad_attn_rows = grad_attn_rows.reshape(4, 4, qkv_rows, width)
    grad_w_out = grad_attn_rows[:, 3].reshape(shard_width, width)
    grad_w_qkv = grad_attn_rows[:, :3].transpose(3, 1, 0, 2).reshape(width, 3, shard_width)

    scale_up = 1.0 + modulation
    upper_two = (sum_own[0] + sum_other[0]).reshape(2, hidden)
    upper_two = jnp.where(parity == 1, upper_two[::-1], upper_two)
    blank = jnp.zeros((2, hidden), f32)
    cond_row = jnp.pad(jnp.concatenate([cond_pre[0], here.astype(f32)[None]]), (0, width - cond_width - 1))
    cond_row = jnp.where(core == 0, cond_row, 0.0)
    rows = jnp.concatenate(
        [
            jnp.stack(
                [
                    sum_end[0],
                    sum_end[1] * norm1,
                    sum_middle[2],
                    sum_middle[0],
                    sum_middle[1] * norm2,
                    sum_leave[0],
                    cond_row,
                    sum_end[1] * scale_up[1],
                    sum_end[2],
                    sum_middle[1] * scale_up[4],
                    sum_leave[1],
                ]
            ),
            jnp.where(core == 0, upper_two, blank),
            jnp.where(core == 0, blank, upper_two),
        ]
    )
    rows = rows + moves.swap(rows)
    each, sums = rows[:7], rows[7:]
    steps = [(moves.flip, 1 << bit, dp >> bit & 1) for bit in range(1, dp_size.bit_length() - 1)]
    steps += [(moves.flip_rank, bit, rank >> bit & 1) for bit in range(ranks.bit_length() - 1)]
    for move, which, ahead in steps:
        came = move(jnp.concatenate([each, sums]), which)
        sums = sums + came[each.shape[0] :]
        came = came[: each.shape[0]]
        each = jnp.where(ahead == 1, jnp.concatenate([came, each]), jnp.concatenate([each, came]))
        if move == moves.flip_rank and which == 0:
            in_back = back(*together((in_even, in_odd), came))
    each, sums = together((each, sums), ffn_spread[2], ffn_spread[4], ffn_spread[6])
    grad_in = to_ranks(*together(tuple(in_back), ffn_spread[2], ffn_spread[4], ffn_spread[6]))
    each = each.reshape(-1, 7, width)
    grad_mods = each[:, :6]
    cond_all = each[:, 6, :cond_width]
    grid_all = each[:, 6, cond_width].astype(jnp.int32)
    grad_b_up = lax.dynamic_index_in_dim(sums[4:], rank, 0, keepdims=False)

    points = time_table.shape[0]
    onehot = (grid_all[:, None] == jnp.arange(points, dtype=jnp.int32)[None, :]).astype(f32)
    cond_act, silu_back = jax.vjp(jax.nn.silu, cond_all)
    cond_act = cond_act.astype(bf16).astype(f32)
    grad_flat = grad_mods.reshape(-1, 6 * width)
    grad_w_ada = jnp.dot(cond_act.T, grad_flat, precision=highest).reshape(cond_width, 6, width)
    grad_b_ada = jnp.sum(grad_mods, axis=0)
    grad_cond = jnp.dot(grad_flat, ada_flat.astype(f32).T, precision=highest)
    grad_pre = silu_back(grad_cond)[0]
    grad_table = jnp.dot(onehot.T, grad_pre, precision=highest)
    return (
        layer_out,
        grad_in,
        grad_table,
        sums[1],
        grad_w_ada,
        grad_b_ada,
        sums[0],
        sums[2],
        grad_w_qkv,
        grad_w_out,
        grad_w_up,
        grad_b_up,
        grad_w_down,
        sums[3],
    )


def solution(mesh):
    parts = (mesh.shape["dp"] // 8, 2, 2, 2, mesh.shape["tensor"])
    finer = jax.sharding.Mesh(mesh.devices.reshape(parts), AXES)
    whole = P()
    split = P(DP, "tensor", None)
    weights = (P(None, None, "tensor"), P("tensor", None), P(None, "tensor"), P("tensor"), P("tensor", None), whole)
    return jax.shard_map(
        shards,
        mesh=finer,
        in_specs=(split, P(DP, "tensor"), P(DP), whole, split) + (whole,) * 5 + weights,
        out_specs=(split, split) + (whole,) * 6 + weights,
        check_vma=False,
    )
```
